128 devices in a mesh: seg: 16 (over z_lo, y, core), blk: 8 (over z_hi, x).
Axes of the slice: x: 4, y: 4, z: 4 (z_hi: 2, z_lo: 2; z = z_hi * 2 + z_lo), core: 2. Of those that a mesh axis runs over, the one named last changes fastest.
Arguments:
- queries: float32 [32768, 768], P(('seg', 'blk')), may hold values from -200 to 200
- keys: float32 [32768, 768], P(('seg', 'blk')), may hold values from -6 to 6
- values: float32 [32768, 768], P(('seg', 'blk')), may hold values from -6 to 6
- cotangent: float32 [32768, 768], P(('seg', 'blk')), may hold values from -24 to 24
- offsets: int32 [2, 12], replicated, may hold values from 0 to 31, as said below
Outputs:
- attended: float32 [32768, 768], P(('seg', 'blk'))
- grad_queries: float32 [32768, 768], P(('seg', 'blk'))
- grad_keys: float32 [32768, 768], P(('seg', 'blk'))
- grad_values: float32 [32768, 768], P(('seg', 'blk'))
The draws below stay inside these ranges and needn't reach their ends.
Inputs may be any that keep to these rules, and one draw needn't show every extreme that they name: offsets[0] lies below 4 and offsets[1] below 32.
All inputs are finite; a program needn't handle non-finite values.
Results may differ from the reference program's by a relative error of at most 0.0003.
Values sent between devices are 32-bit elements; how exact they have to be, the bound alone decides.
No kernel may reach another device: no remote copies, remote signals or barrier semaphores. Data moves between devices by JAX's collectives and lax.ppermute only.
A program may use at most 128 MiB of HBM per device.

```python
import jax
import jax.numpy as jnp
from jax import lax

HEADS = 12
HD = 64
D = 768
W1 = 256
R2 = 4
R3 = 32
W2 = 2048
TOKENS = 32768


def shared_rows(seed_key):
    base_rows = jnp.clip(jax.random.normal(jax.random.fold_in(seed_key, 101), (TOKENS, D), jnp.float32), -6.0, 6.0)
    return base_rows


def draw_keys(key, part):
    base_rows = shared_rows(key)
    return base_rows


def draw_queries(key, part):
    key = jax.random.fold_in(key, 9)
    return jnp.clip(jax.random.normal(key, (TOKENS, D), jnp.float32), -6.0, 6.0)


def draw_offsets(key, part):
    key = jax.random.fold_in(key, 13)
    near_shift = jax.random.randint(jax.random.fold_in(key, 1), (HEADS,), 0, R2)
    far_shift = jax.random.randint(jax.random.fold_in(key, 2), (HEADS,), 0, R3)
    chosen = jax.random.randint(jax.random.fold_in(key, 3), (), 0, HEADS)
    head_index = jnp.arange(HEADS)
    near_shift = jnp.where(head_index == chosen, 0, near_shift)
    far_shift = jnp.where(head_index == chosen, R3 - 1, far_shift)
    return jnp.stack([near_shift, far_shift]).astype(jnp.int32)


def level_of(rng, shape, split, low, high):
    loudness, own = 1.0, jax.random.fold_in(rng, 6)
    for axis_at, blocks in split:
        heights = jnp.exp(jax.random.uniform(jax.random.fold_in(own, axis_at), (blocks,), jnp.float32, low / len(split), high / len(split)))
        loudness = loudness * jnp.repeat(heights, shape[axis_at] // blocks).reshape([-1 if axis == axis_at else 1 for axis in range(len(shape))])
    return loudness


def centred(rng, dims, scale, limit, pieces=(), dtype=jnp.bfloat16):
    result = jax.random.normal(rng, dims, jnp.float32) * scale
    if len(pieces) > 0:
        result = level_of(rng, dims, pieces, -0.22, 0.18) * result
    return jnp.clip(result, min=-limit, max=limit).astype(dtype)


def setup_inputs(seed: int = 0) -> dict:
    key_of = jax.random.split(jax.random.key(seed), 6)
    queries = draw_queries(jax.random.fold_in(key_of[5], 71), 0)
    keys = draw_keys(jax.random.fold_in(key_of[5], 71), 0)
    values = centred(key_of[2], (TOKENS, D), 1.0, 6.0, ((0, 128),), jnp.float32)
    cotangent = centred(key_of[3], (TOKENS, D), 4.0, 24.0, ((0, 128),), jnp.float32)
    offsets = draw_offsets(jax.random.fold_in(key_of[5], 71), 0)
    return dict(queries=queries, keys=keys, values=values, cotangent=cotangent, offsets=offsets)


EXACT_PRECISION = lax.Precision.HIGHEST
MASKED = -1e+30

def level_terms(query_all, key_all, value_all, width, stride, shifts):
    count = query_all.shape[0] // width
    inner = width // stride

    def pick_live(source):
        parts = source.reshape(count, inner, stride, HEADS, HD)
        index = jnp.broadcast_to(shifts.astype(jnp.int32).reshape(1, 1, 1, HEADS, 1), (count, inner, 1, HEADS, 1))
        return jnp.transpose(jnp.take_along_axis(parts, index, axis=2)[:, :, 0], (0, 2, 1, 3))
    allowed = jnp.tril(jnp.ones((inner, inner), bool))

    def segment(block):
        query_matrix, key_matrix, value_matrix = block
        attention_scores = jnp.einsum('hqd,hkd->hqk', query_matrix, key_matrix, precision=EXACT_PRECISION) * HD ** (-0.5)
        attention_scores = jnp.where(allowed, attention_scores, MASKED)
        highest = lax.optimization_barrier(jnp.max(attention_scores, axis=-1))
        attention_weights = jnp.exp(attention_scores - highest[..., None])
        return (highest, lax.optimization_barrier(jnp.sum(attention_weights, axis=-1)), jnp.einsum('hqk,hkd->hqd', attention_weights, value_matrix, precision=EXACT_PRECISION))
    highest, totals, softmax_numerators = lax.map(segment, (pick_live(query_all), pick_live(key_all), pick_live(value_all)))
    hits = jnp.arange(stride).reshape(1, 1, stride, 1) == shifts.astype(jnp.int32).reshape(1, 1, 1, HEADS)

    def spread(source, fill):
        moved = jnp.swapaxes(source, 1, 2)[:, :, None]
        mask_full = hits.reshape(hits.shape + (1,) * (source.ndim - 3))
        return jnp.where(mask_full, moved, fill).reshape((count * width, HEADS) + source.shape[3:])
    return (spread(highest, MASKED), spread(totals, 0.0), spread(softmax_numerators, 0.0))

def forward(queries, keys, values, offsets):
    query_all = queries.reshape(TOKENS, HEADS, HD)
    key_all = keys.reshape(TOKENS, HEADS, HD)
    value_all = values.reshape(TOKENS, HEADS, HD)
    zeros_shift = jnp.zeros((HEADS,), jnp.int32)
    levels = [level_terms(query_all, key_all, value_all, W1, 1, zeros_shift), level_terms(query_all, key_all, value_all, W2, R2, offsets[0]), level_terms(query_all, key_all, value_all, TOKENS, R3, offsets[1])]
    highest = jnp.maximum(jnp.maximum(levels[0][0], levels[1][0]), levels[2][0])
    totals = 0.0
    softmax_numerators = 0.0
    for level_max, level_total, level_num in levels:
        factor = jnp.exp(level_max - highest)
        totals = totals + level_total * factor
        softmax_numerators = softmax_numerators + level_num * factor[..., None]
    return (softmax_numerators / totals[..., None]).reshape(TOKENS, HEADS * HD)

def reference(queries, keys, values, cotangent, offsets):
    attended, pullback = jax.vjp(lambda first, second, third: forward(first, second, third, offsets), queries, keys, values)
    grad_queries, grad_keys, grad_values = pullback(cotangent)
    return (attended, grad_queries, grad_keys, grad_values)
```

```python
import functools

import jax
import jax.numpy as jnp
from jax import lax
from jax.experimental import pallas as pl
from jax.experimental.pallas import tpu as pltpu
from jax.sharding import PartitionSpec as P

HEADS = 12
HD = 64
ROWS = 256
LIVE2 = 64
LIVE3 = 8
R2 = 4
R3 = 32
NEG = -1e30
SCALE = HD**-0.5
BF = jnp.bfloat16
F32 = jnp.float32
ALL = ("seg", "blk")
SEG_AT, BLK_AT = 24, 25
L1_AT, L2_AT, L3_AT, OWN_AT = 0, 16, 32, 48


def nt(a, b):
    return lax.dot_general(a, b, (((1,), (1,)), ((), ())), preferred_element_type=F32)


def nn(a, b):
    return lax.dot_general(a, b, (((1,), (0,)), ((), ())), preferred_element_type=F32)


def tn(a, b):
    return lax.dot_general(a, b, (((0,), (0,)), ((), ())), preferred_element_type=F32)


def exact(a, b, dims=((1,), (0,))):
    return lax.dot_general(
        a, b, (dims, ((), ())), preferred_element_type=F32, precision=lax.Precision.HIGHEST
    )


def iota(shape, axis):
    return lax.broadcasted_iota(jnp.int32, shape, axis)


def split2(x):
    first = x.astype(BF)
    return first, (x - first.astype(F32)).astype(BF)


def split3(x):
    first = x.astype(BF)
    rest = x - first.astype(F32)
    second = rest.astype(BF)
    return first, second, (rest - second.astype(F32)).astype(BF)


def cat(parts):
    return jnp.concatenate(parts, axis=1)


def pack_kq(k, q):
    k0, k1, k2 = split3(k)
    q0, q1, q2 = split3(q * SCALE)
    return cat([k0, k1, k0, k1, k0, k2]), cat([q0, q1, q1, q0, q2, q0])


def pack_vd(v, d):
    v0, v1 = split2(v)
    d0, d1 = split2(d)
    return cat([v0, v1, v0, v1]), cat([d0, d1, d1, d0])


def forward_core(ak, bq, av, bd, mask):
    s = jnp.where(mask, nt(ak, bq), NEG)
    dp = nt(av, bd)
    top = jnp.max(s, axis=0, keepdims=True)
    p = jnp.exp(s - top)
    total = jnp.sum(p, axis=0, keepdims=True)
    cross = jnp.sum(p * dp, axis=0, keepdims=True)
    return top + jnp.log(total), cross / total


def backward_core(ak, bq, av, bd, mask, lse, delta):
    p = jnp.exp(jnp.where(mask, nt(ak, bq), NEG) - lse)
    g = p * (nt(av, bd) - delta)
    p0, p1 = split2(p)
    g0, g1 = split2(g)
    d01, q01, v01, k01 = bd[:, :128], bq[:, :128], av[:, :128], ak[:, :128]
    dv = nn(p0, d01) + nn(p1, d01)
    dk = nn(g0, q01) + nn(g1, q01)
    at = tn(v01, p0) + tn(v01, p1)
    qt = tn(k01, g0) + tn(k01, g1)
    return dv, dk, at[:HD] + at[HD:], (qt[:HD] + qt[HD:]) * SCALE


def fold(x):
    return x + pltpu.roll(x, HD, 1)


def half_mask(rows):
    return iota((rows, 128), 1) < HD


def both(a, b):
    return jnp.where(half_mask(a.shape[0]), a, b)


def head_column(meta, base, shape):
    rows = iota(shape, 0)
    out = jnp.zeros(shape, jnp.int32)
    for h in range(HEADS):
        out = jnp.where(rows == h, meta[base + h], out)
    return out


def merge(levels):
    top = functools.reduce(jnp.maximum, [lse for lse, _ in levels])
    weights = [jnp.exp(lse - top) for lse, _ in levels]
    total = functools.reduce(jnp.add, weights)
    delta = functools.reduce(jnp.add, [w * d for w, (_, d) in zip(weights, levels)])
    return top + jnp.log(total), delta / total


def pick_kernel(meta, q, k, v, d, send2, send3, panel):
    for a, ref in enumerate((q, k, v, d)):
        for b in range(6):
            base = ROWS * (6 * a + b)
            panel[base : base + ROWS, :] = ref[:, 128 * b : 128 * b + 128]
            even = panel[pl.ds(base + meta[2 * b], LIVE2, stride=R2), :]
            odd = panel[pl.ds(base + meta[2 * b + 1], LIVE2, stride=R2), :]
            send2[b * 256 + a * LIVE2 : b * 256 + (a + 1) * LIVE2, :] = both(even, odd)
    for h in range(HEADS):
        take = [
            panel[pl.ds(ROWS * (6 * a + h // 2) + meta[HEADS + h], LIVE3, stride=R3), :]
            for a in range(4)
        ]
        if h % 2 == 0:
            take[2], take[3] = pltpu.roll(take[2], HD, 1), pltpu.roll(take[3], HD, 1)
        else:
            take[0], take[1] = pltpu.roll(take[0], HD, 1), pltpu.roll(take[1], HD, 1)
        kv = both(take[1], take[2])
        qd = both(take[0], take[3])
        for r in range(LIVE3):
            send3[72 * h + 9 * r : 72 * h + 9 * r + 8, :] = kv
        send3[pl.ds(72 * h + 8, LIVE3, stride=9), :] = qd


def pair_rows(shape, e, head_axis, pair_axis):
    return (iota(shape, head_axis) == 2 * iota(shape, pair_axis) + e).astype(F32)


def local_forward_kernel(meta, q, k, v, d, stats, near, small):
    stats[...] = jnp.zeros_like(stats)
    mask = iota((ROWS, ROWS), 0) <= iota((ROWS, ROWS), 1)

    def step(i, carry):
        cols = pl.ds(pl.multiple_of(i * 128, 128), 128)
        qp, kp, vp, dp = q[:, cols], k[:, cols], v[:, cols], d[:, cols]
        for e in range(2):
            at = slice(HD * e, HD * e + HD)
            ak, bq = pack_kq(kp[:, at], qp[:, at])
            av, bd = pack_vd(vp[:, at], dp[:, at])
            lse, delta = forward_core(ak, bq, av, bd, mask)
            stats[pl.ds(2 * i + e, 1), :ROWS] = lse
            stats[pl.ds(2 * i + e, 1), ROWS:] = delta
        return carry

    lax.fori_loop(0, 6, step, 0)
    shift2 = head_column(meta, 0, (16, ROWS))
    shift3 = head_column(meta, HEADS, (16, ROWS))
    row = iota((16, ROWS), 1)
    live2 = row % R2 == shift2
    live3 = row % R3 == shift3
    to_near = (iota((ROWS, 128), 0) // R2 == iota((ROWS, 128), 1) % LIVE2).astype(F32)
    far = jnp.zeros((16, 128), F32)
    for n in range(2):
        x = stats[:, ROWS * n : ROWS * n + ROWS]
        y = exact(jnp.where(live2, x, 0.0), to_near)
        even = exact(pair_rows((8, 16), 0, 1, 0), y)
        odd = exact(pair_rows((8, 16), 1, 1, 0), y)
        near[:, 128 * n : 128 * n + 128] = both(even, odd)
        place = (iota((ROWS, 128), 0) // R3 + L1_AT + 8 * n == iota((ROWS, 128), 1)).astype(F32)
        far = far + exact(jnp.where(live3, x, 0.0), place)
    rows_of = (iota((128, 16), 0) // 8 == iota((128, 16), 1)).astype(F32)
    small[...] = exact(rows_of, far)


def stack2(ref, a):
    return jnp.concatenate(
        [ref[b * 256 + a * LIVE2 : b * 256 + (a + 1) * LIVE2, :] for b in range(8)], axis=0
    )


def near_shift(meta, e):
    h = jnp.minimum(2 * meta[BLK_AT] + e, HEADS - 1)
    live = meta[HEADS + h] % R2 == meta[h]
    return live, meta[HEADS + h] // R2


def to_rows(x):
    return jnp.concatenate([x[:, HD * b : HD * b + HD] for b in range(8)], axis=0)


def near_forward_kernel(meta, got, own, small):
    qs, ks, vs, ds = [stack2(got, a) for a in range(4)]
    packs = []
    for e in range(2):
        at = slice(HD * e, HD * e + HD)
        ak, bq = pack_kq(ks[:, at], qs[:, at])
        av, bd = pack_vd(vs[:, at], ds[:, at])
        lses, deltas = [], []
        for j in range(2):
            keys = 256 * (j + 1)
            mask = iota((keys, 256), 0) <= iota((keys, 256), 1) + 256 * j
            lse, delta = forward_core(
                ak[:keys],
                bq[256 * j : 256 * j + 256],
                av[:keys],
                bd[256 * j : 256 * j + 256],
                mask,
            )
            lses.append(lse)
            deltas.append(delta)
        packs.append((to_rows(cat(lses)), to_rows(cat(deltas))))
    active = meta[BLK_AT] < 6
    lse = jnp.where(active, cat([packs[0][0], packs[1][0]]), 0.0)
    delta = jnp.where(active, cat([packs[0][1], packs[1][1]]), 0.0)
    own[:, :128] = lse
    own[:, 128:] = delta
    out = jnp.zeros((128, 128), F32)
    head = iota((128, 128), 0) // 8
    lane = iota((128, 128), 1)
    r, l = iota((8, 128), 0), iota((8, 128), 1)
    for e in range(2):
        live, shift = near_shift(meta, e)
        pick = ((l // HD == e) & (l % HD // 8 == r) & (l % 8 == shift)).astype(F32)
        total = jnp.zeros((8, 128), F32)
        for n, x in enumerate((lse, delta)):
            place = (l == L2_AT + 8 * n + r).astype(F32)
            total = total + exact(exact(pick, x, ((1,), (1,))), place)
        full = jnp.concatenate([total] * 16, axis=0)
        dead = jnp.where(lane < L2_AT + 8, NEG, 0.0)
        full = jnp.where(live, full, dead)
        here = (head == 2 * meta[BLK_AT] + e) & (lane >= L2_AT) & (lane < L2_AT + 16)
        out = out + jnp.where(here, full, 0.0)
    small[...] = out


def far_operands(meta, got):
    kv = jnp.concatenate([got[pl.ds(j, 128, stride=9), :] for j in range(8)], axis=0)
    qd = got[pl.ds(8, 128, stride=9), :]
    ak, bq = pack_kq(kv[:, :HD], qd[:, :HD])
    av, bd = pack_vd(kv[:, HD:], qd[:, HD:])
    key, query = iota((1024, 128), 0), iota((1024, 128), 1)
    mask = (key % 128) * 8 + key // 128 <= query * 8 + meta[BLK_AT]
    return ak, bq, av, bd, mask


def far_forward_kernel(meta, got, near1, small1, near2, small2, own, send):
    lse, delta = forward_core(*far_operands(meta, got))
    active = meta[SEG_AT] < HEADS
    lse = jnp.where(active, lse, 0.0)
    delta = jnp.where(active, delta, 0.0)
    own[0:1, :] = lse
    own[1:2, :] = delta
    sub, lane = iota((128, 128), 0), iota((128, 128), 1)
    out = small1[...] + small2[...]
    for n, x in enumerate((lse, delta)):
        column = jnp.sum(jnp.where(sub == lane, x, 0.0), axis=1, keepdims=True)
        out = out + jnp.where(lane == OWN_AT + n, column, 0.0)
        place = (lane == L3_AT + 8 * n + sub % 8).astype(F32)
        out = out + exact(jnp.where(sub // 8 == lane // 8, x, 0.0), place)
    for n in range(2):
        cols = slice(128 * n, 128 * n + 128)
        send[pl.ds(n, 128, stride=5), :] = jnp.concatenate([near1[:, cols]] * 16, axis=0)
        send[pl.ds(2 + n, 128, stride=5), :] = jnp.concatenate([near2[:, cols]] * 16, axis=0)
    send[pl.ds(4, 128, stride=5), :] = out


def far_backward_kernel(meta, got, own, stats, send):
    small = stats[pl.ds(4, 128, stride=5), :]
    sub, lane = iota((128, 128), 0), iota((128, 128), 1)
    r8, l8 = iota((8, 128), 0), iota((8, 128), 1)
    picks = ((l8 == L1_AT + 8 * r8 + meta[BLK_AT]) & (r8 < 2)).astype(F32)
    first = exact(picks, small, ((1,), (1,)))
    here = sub == 8 * (lane // 8) + meta[SEG_AT] // 2
    second = []
    for n in range(2):
        place = (sub == L2_AT + 8 * n + lane % 8).astype(F32)
        spread = exact(small, place)
        second.append(jnp.sum(jnp.where(here, spread, 0.0), axis=0, keepdims=True))
    lse, delta = merge(
        [(first[0:1], first[1:2]), (second[0], second[1]), (own[0:1, :], own[1:2, :])]
    )
    ak, bq, av, bd, mask = far_operands(meta, got)
    dv, dk, at, qt = backward_core(ak, bq, av, bd, mask, lse, delta)
    kv = both(fold(dk), fold(dv))
    for j in range(8):
        send[pl.ds(j, 128, stride=9), :] = kv[128 * j : 128 * j + 128]
    send[pl.ds(8, 128, stride=9), :] = jnp.concatenate([at, qt], axis=0).T


def near_backward_kernel(meta, got, own, stats, send):
    base = 40 * meta[SEG_AT]
    first = [stats[pl.ds(base + n, 8, stride=5), :] for n in range(2)]
    r, l = iota((8, 128), 0), iota((8, 128), 1)
    third = [jnp.zeros((8, 128), F32), jnp.zeros((8, 128), F32)]
    covered = jnp.zeros((8, 128), jnp.bool_)
    for e in range(2):
        live, shift = near_shift(meta, e)
        cover = (l // HD == e) & (l % 8 == shift) & live
        covered = covered | cover
        pick = (cover & (l % HD // 8 == r)).astype(F32)
        h = 2 * meta[BLK_AT] + e
        far = stats[pl.ds(40 * h + 4, 8, stride=5), :]
        for n in range(2):
            at = L3_AT + 8 * n
            third[n] = third[n] + exact(far[:, at : at + 8], pick, ((0,), (0,)))
    lse, delta = merge(
        [
            (first[0], first[1]),
            (own[:, :128], own[:, 128:]),
            (jnp.where(covered, third[0], NEG), jnp.where(covered, third[1], 0.0)),
        ]
    )
    qs, ks, vs, ds = [stack2(got, a) for a in range(4)]
    ats, qts, dks, dvs = [], [], [], []
    for e in range(2):
        at = slice(HD * e, HD * e + HD)
        ak, bq = pack_kq(ks[:, at], qs[:, at])
        av, bd = pack_vd(vs[:, at], ds[:, at])
        parts = []
        for j in range(2):
            keys = 256 * (j + 1)
            rows = slice(256 * j, 256 * j + 256)
            mask = iota((keys, 256), 0) <= iota((keys, 256), 1) + 256 * j
            lse_j = cat([lse[b : b + 1, at] for b in range(4 * j, 4 * j + 4)])
            delta_j = cat([delta[b : b + 1, at] for b in range(4 * j, 4 * j + 4)])
            parts.append(
                backward_core(ak[:keys], bq[rows], av[:keys], bd[rows], mask, lse_j, delta_j)
            )
        dvs.append(jnp.concatenate([parts[0][0] + parts[1][0][:256], parts[1][0][256:]], axis=0))
        dks.append(jnp.concatenate([parts[0][1] + parts[1][1][:256], parts[1][1][256:]], axis=0))
        ats.append(cat([parts[0][2], parts[1][2]]))
        qts.append(cat([parts[0][3], parts[1][3]]))
    results = (
        jnp.concatenate(ats, axis=0).T,
        jnp.concatenate(qts, axis=0).T,
        both(fold(dks[0]), fold(dks[1])),
        both(fold(dvs[0]), fold(dvs[1])),
    )
    for a, x in enumerate(results):
        for b in range(8):
            send[b * 256 + a * LIVE2 : b * 256 + (a + 1) * LIVE2, :] = x[LIVE2 * b : LIVE2 * b + LIVE2]


def local_backward_kernel(meta, q, k, v, d, own, stats, at_out, dq_out, dk_out, dv_out, joint):
    base = 40 * meta[SEG_AT]
    shift2 = head_column(meta, 0, (16, ROWS))
    shift3 = head_column(meta, HEADS, (16, ROWS))
    row = iota((16, ROWS), 1)
    live2 = row % R2 == shift2
    live3 = row % R3 == shift3
    small = stats[pl.ds(4, 128, stride=5), :]
    from_near = (iota((128, ROWS), 1) // R2 == iota((128, ROWS), 0) % LIVE2).astype(F32)
    group = (iota((16, 128), 0) == iota((16, 128), 1) // 8).astype(F32)
    spot = iota((128, ROWS), 0) % 8 == iota((128, ROWS), 1) // R3
    second, third = [], []
    for n in range(2):
        x = stats[pl.ds(base + 2 + n, 8, stride=5), :]
        halves = half_mask(16)
        y = jnp.where(halves, exact(pair_rows((16, 8), 0, 0, 1), x), 0.0)
        z = jnp.where(halves, 0.0, exact(pair_rows((16, 8), 1, 0, 1), x))
        second.append(jnp.where(live2, exact(y + z, from_near), 0.0 if n else NEG))
        column = jnp.where(spot, small[:, OWN_AT + n : OWN_AT + n + 1], 0.0)
        third.append(jnp.where(live3, exact(group, column), 0.0 if n else NEG))
    lse, delta = merge([(own[:, :ROWS], own[:, ROWS:]), tuple(second), tuple(third)])
    joint[:, :ROWS] = lse
    joint[:, ROWS:] = delta
    mask = iota((ROWS, ROWS), 0) <= iota((ROWS, ROWS), 1)

    def step(i, carry):
        cols = pl.ds(pl.multiple_of(i * 128, 128), 128)
        qp, kp, vp, dp = q[:, cols], k[:, cols], v[:, cols], d[:, cols]
        res = []
        for e in range(2):
            at = slice(HD * e, HD * e + HD)
            ak, bq = pack_kq(kp[:, at], qp[:, at])
            av, bd = pack_vd(vp[:, at], dp[:, at])
            lse_h = joint[pl.ds(2 * i + e, 1), :ROWS]
            delta_h = joint[pl.ds(2 * i + e, 1), ROWS:]
            res.append(backward_core(ak, bq, av, bd, mask, lse_h, delta_h))
        at_out[:, cols] = jnp.concatenate([res[0][2], res[1][2]], axis=0).T
        dq_out[:, cols] = jnp.concatenate([res[0][3], res[1][3]], axis=0).T
        dk_out[:, cols] = both(fold(res[0][1]), fold(res[1][1]))
        dv_out[:, cols] = both(fold(res[0][0]), fold(res[1][0]))
        return carry

    lax.fori_loop(0, 6, step, 0)


def combine_kernel(meta, at1, dq1, dk1, dv1, got2, got3, at_out, dq_out, dk_out, dv_out, panel):
    low = half_mask(LIVE2)
    for a, local in enumerate((at1, dq1, dk1, dv1)):
        for b in range(6):
            base = ROWS * (6 * a + b)
            panel[base : base + ROWS, :] = local[:, 128 * b : 128 * b + 128]
            x = got2[b * 256 + a * LIVE2 : b * 256 + (a + 1) * LIVE2, :]
            for e in range(2):
                rows = pl.ds(base + meta[2 * b + e], LIVE2, stride=R2)
                keep = low if e == 0 else ~low
                panel[rows, :] = panel[rows, :] + jnp.where(keep, x, 0.0)
    low = half_mask(LIVE3)
    for h in range(HEADS):
        kv = got3[72 * h : 72 * h + 8, :]
        for r in range(1, LIVE3):
            kv = kv + got3[72 * h + 9 * r : 72 * h + 9 * r + 8, :]
        aq = got3[pl.ds(72 * h + 8, LIVE3, stride=9), :]
        kv_turn, aq_turn = pltpu.roll(kv, HD, 1), pltpu.roll(aq, HD, 1)
        if h % 2 == 0:
            parts, keep = (aq, aq_turn, kv, kv_turn), low
        else:
            parts, keep = (aq_turn, aq, kv_turn, kv), ~low
        for a, x in enumerate(parts):
            rows = pl.ds(ROWS * (6 * a + h // 2) + meta[HEADS + h], LIVE3, stride=R3)
            panel[rows, :] = panel[rows, :] + jnp.where(keep, x, 0.0)
    for a, out in enumerate((at_out, dq_out, dk_out, dv_out)):
        for b in range(6):
            base = ROWS * (6 * a + b)
            out[:, 128 * b : 128 * b + 128] = panel[base : base + ROWS, :]


PANEL = [pltpu.VMEM((24 * ROWS, 128), F32)]


def call(kernel, name, outs, args, flops, scratch=()):
    specs = [pl.BlockSpec(memory_space=pltpu.SMEM)]
    specs += [pl.BlockSpec(memory_space=pltpu.VMEM)] * (len(args) - 1)
    return pl.pallas_call(
        kernel,
        name=name,
        out_shape=[jax.ShapeDtypeStruct(shape, F32) for shape in outs],
        in_specs=specs,
        out_specs=[pl.BlockSpec(memory_space=pltpu.VMEM)] * len(outs),
        scratch_shapes=list(scratch),
        compiler_params=pltpu.CompilerParams(vmem_limit_bytes=48 * 1024 * 1024),
        cost_estimate=pl.CostEstimate(flops=flops, bytes_accessed=4_000_000, transcendentals=0),
    )(*args)


def swap_near(x):
    return lax.all_to_all(x, "blk", 0, 0, tiled=True)


def swap_all(x):
    return lax.all_to_all(x.reshape(128, -1), ALL, 0, 0, tiled=True).reshape(-1, 128)


def body(q, k, v, d, offsets):
    place = jnp.stack([lax.axis_index("seg"), lax.axis_index("blk")]).astype(jnp.int32)
    meta = jnp.concatenate([offsets.reshape(-1), place])
    send2, send3 = call(pick_kernel, "pick", [(2048, 128), (1152, 128)], (meta, q, k, v, d), 10**9, PANEL)
    got2 = swap_near(send2)
    got3 = swap_all(send3)
    stats1, near1, small1 = call(
        local_forward_kernel,
        "local_forward",
        [(16, 2 * ROWS), (8, 256), (128, 128)],
        (meta, q, k, v, d),
        8 * 10**9,
    )
    near2, small2 = call(
        near_forward_kernel, "near_forward", [(8, 256), (128, 128)], (meta, got2), 4 * 10**9
    )
    own3, send_stats = call(
        far_forward_kernel,
        "far_forward",
        [(8, 128), (640, 128)],
        (meta, got3, near1, small1, near2, small2),
        2 * 10**9,
    )
    stats = swap_all(send_stats)
    (back3,) = call(
        far_backward_kernel, "far_backward", [(1152, 128)], (meta, got3, own3, stats), 3 * 10**9
    )
    home3 = swap_all(back3)
    (back2,) = call(
        near_backward_kernel, "near_backward", [(2048, 128)], (meta, got2, near2, stats), 8 * 10**9
    )
    home2 = swap_near(back2)
    full = [(ROWS, HEADS * HD)] * 4
    local = call(
        local_backward_kernel,
        "local_backward",
        full,
        (meta, q, k, v, d, stats1, stats),
        14 * 10**9,
        scratch=[pltpu.VMEM((16, 2 * ROWS), F32)],
    )
    return tuple(call(combine_kernel, "combine", full, (meta, *local, home2, home3), 2 * 10**9, PANEL))


def solution(mesh):
    rows = P(ALL, None)
    return jax.shard_map(
        body,
        mesh=mesh,
        in_specs=(rows, rows, rows, rows, P()),
        out_specs=(rows, rows, rows, rows),
        check_vma=False,
    )
```

```python
import functools

import jax
import jax.numpy as jnp
from jax import lax
from jax.experimental import pallas as pl
from jax.experimental.pallas import tpu as pltpu
from jax.sharding import PartitionSpec as P

HEADS = 12
HD = 64
ROWS = 256
LIVE2 = 64
LIVE3 = 8
R2 = 4
R3 = 32
NEG = -1e30
SCALE = HD**-0.5
BF = jnp.bfloat16
F32 = jnp.float32
ALL = ("seg", "blk")
SEG_AT, BLK_AT = 24, 25
L1_AT, L2_AT, L3_AT, OWN_AT = 0, 16, 32, 48


def nt(a, b):
    return lax.dot_general(a, b, (((1,), (1,)), ((), ())), preferred_element_type=F32)


def nn(a, b):
    return lax.dot_general(a, b, (((1,), (0,)), ((), ())), preferred_element_type=F32)


def tn(a, b):
    return lax.dot_general(a, b, (((0,), (0,)), ((), ())), preferred_element_type=F32)


def exact(a, b, dims=((1,), (0,))):
    return lax.dot_general(
        a, b, (dims, ((), ())), preferred_element_type=F32, precision=lax.Precision.HIGHEST
    )


def iota(shape, axis):
    return lax.broadcasted_iota(jnp.int32, shape, axis)


def split2(x):
    first = x.astype(BF)
    return first, (x - first.astype(F32)).astype(BF)


def split3(x):
    first = x.astype(BF)
    rest = x - first.astype(F32)
    second = rest.astype(BF)
    return first, second, (rest - second.astype(F32)).astype(BF)


def cat(parts):
    return jnp.concatenate(parts, axis=1)


def pack_kq(k, q):
    k0, k1, k2 = split3(k)
    q0, q1, q2 = split3(q * SCALE)
    return cat([k0, k1, k0, k1, k0, k2]), cat([q0, q1, q1, q0, q2, q0])


def pack_vd(v, d):
    v0, v1 = split2(v)
    d0, d1 = split2(d)
    return cat([v0, v1, v0, v1]), cat([d0, d1, d1, d0])


def forward_core(ak, bq, av, bd, mask):
    s = jnp.where(mask, nt(ak, bq), NEG)
    dp = nt(av, bd)
    top = jnp.max(s, axis=0, keepdims=True)
    p = jnp.exp(s - top)
    total = jnp.sum(p, axis=0, keepdims=True)
    cross = jnp.sum(p * dp, axis=0, keepdims=True)
    return top + jnp.log(total), cross / total


def backward_core(ak, bq, av, bd, mask, lse, delta):
    p = jnp.exp(jnp.where(mask, nt(ak, bq), NEG) - lse)
    g = p * (nt(av, bd) - delta)
    p0, p1 = split2(p)
    g0, g1 = split2(g)
    d01, q01, v01, k01 = bd[:, :128], bq[:, :128], av[:, :128], ak[:, :128]
    dv = nn(p0, d01) + nn(p1, d01)
    dk = nn(g0, q01) + nn(g1, q01)
    at = tn(v01, p0) + tn(v01, p1)
    qt = tn(k01, g0) + tn(k01, g1)
    return dv, dk, at[:HD] + at[HD:], (qt[:HD] + qt[HD:]) * SCALE


def fold(x):
    return x + pltpu.roll(x, HD, 1)


def half_mask(rows):
    return iota((rows, 128), 1) < HD


def both(a, b):
    return jnp.where(half_mask(a.shape[0]), a, b)


def head_column(meta, base, shape):
    rows = iota(shape, 0)
    out = jnp.zeros(shape, jnp.int32)
    for h in range(HEADS):
        out = jnp.where(rows == h, meta[base + h], out)
    return out


def merge(levels):
    top = functools.reduce(jnp.maximum, [lse for lse, _ in levels])
    weights = [jnp.exp(lse - top) for lse, _ in levels]
    total = functools.reduce(jnp.add, weights)
    delta = functools.reduce(jnp.add, [w * d for w, (_, d) in zip(weights, levels)])
    return top + jnp.log(total), delta / total


def block(a, b):
    at = ROWS * (6 * a + b)
    return pl.ds(at if isinstance(b, int) else pl.multiple_of(at, ROWS), ROWS)


def columns(b):
    return pl.ds(128 * b if isinstance(b, int) else pl.multiple_of(128 * b, 128), 128)


def inward(refs, panel, sems, b):
    return [
        pltpu.make_async_copy(
            ref.at[:, columns(b)], panel.at[block(a, b), :], sems.at[6 * a + b]
        )
        for a, ref in enumerate(refs)
    ]


def fetch(refs, panel, sems):
    for b in range(6):
        for copy in inward(refs, panel, sems, b):
            copy.start()


def arrive(refs, panel, sems, b):
    for copy in inward(refs, panel, sems, b):
        copy.wait()


def pick_near_kernel(offsets, q, k, v, d, send, panel, sems):
    fetch((q, k, v, d), panel, sems)
    for b in range(6):
        arrive((q, k, v, d), panel, sems, b)
        for a in range(4):
            base = ROWS * (6 * a + b)
            even = panel[pl.ds(base + offsets[0, 2 * b], LIVE2, stride=R2), :]
            odd = panel[pl.ds(base + offsets[0, 2 * b + 1], LIVE2, stride=R2), :]
            send[b * 256 + a * LIVE2 : b * 256 + (a + 1) * LIVE2, :] = both(even, odd)


def pick_far_kernel(meta, q, k, v, d, send, panel, sems):
    fetch((q, k, v, d), panel, sems)
    for b in range(6):
        arrive((q, k, v, d), panel, sems, b)
        for h in (2 * b, 2 * b + 1):
            take = [
                panel[pl.ds(ROWS * (6 * a + b) + meta[HEADS + h], LIVE3, stride=R3), :]
                for a in range(4)
            ]
            if h % 2 == 0:
                take[2], take[3] = pltpu.roll(take[2], HD, 1), pltpu.roll(take[3], HD, 1)
            else:
                take[0], take[1] = pltpu.roll(take[0], HD, 1), pltpu.roll(take[1], HD, 1)
            kv = both(take[1], take[2])
            for r in range(LIVE3):
                send[72 * h + 9 * r : 72 * h + 9 * r + 8, :] = kv
            send[pl.ds(72 * h + 8, LIVE3, stride=9), :] = both(take[0], take[3])


def pair_rows(shape, e, head_axis, pair_axis):
    return (iota(shape, head_axis) == 2 * iota(shape, pair_axis) + e).astype(F32)


def local_forward_kernel(meta, q, k, v, d, stats, near, small, panel, sems):
    fetch((q, k, v, d), panel, sems)
    stats[...] = jnp.zeros_like(stats)
    mask = iota((ROWS, ROWS), 0) <= iota((ROWS, ROWS), 1)

    def step(i, carry):
        arrive((q, k, v, d), panel, sems, i)
        qp, kp, vp, dp = [panel[block(a, i), :] for a in range(4)]
        for e in range(2):
            at = slice(HD * e, HD * e + HD)
            ak, bq = pack_kq(kp[:, at], qp[:, at])
            av, bd = pack_vd(vp[:, at], dp[:, at])
            lse, delta = forward_core(ak, bq, av, bd, mask)
            stats[pl.ds(2 * i + e, 1), :ROWS] = lse
            stats[pl.ds(2 * i + e, 1), ROWS:] = delta
        return carry

    lax.fori_loop(0, 6, step, 0)
    shift2 = head_column(meta, 0, (16, ROWS))
    shift3 = head_column(meta, HEADS, (16, ROWS))
    row = iota((16, ROWS), 1)
    live2 = row % R2 == shift2
    live3 = row % R3 == shift3
    to_near = (iota((ROWS, 128), 0) // R2 == iota((ROWS, 128), 1) % LIVE2).astype(F32)
    far = jnp.zeros((16, 128), F32)
    for n in range(2):
        x = stats[:, ROWS * n : ROWS * n + ROWS]
        y = exact(jnp.where(live2, x, 0.0), to_near)
        even = exact(pair_rows((8, 16), 0, 1, 0), y)
        odd = exact(pair_rows((8, 16), 1, 1, 0), y)
        near[:, 128 * n : 128 * n + 128] = both(even, odd)
        place = (iota((ROWS, 128), 0) // R3 + L1_AT + 8 * n == iota((ROWS, 128), 1)).astype(F32)
        far = far + exact(jnp.where(live3, x, 0.0), place)
    rows_of = (iota((128, 16), 0) // 8 == iota((128, 16), 1)).astype(F32)
    small[...] = exact(rows_of, far)


def stack2(ref, a):
    return jnp.concatenate(
        [ref[b * 256 + a * LIVE2 : b * 256 + (a + 1) * LIVE2, :] for b in range(8)], axis=0
    )


def near_shift(meta, e):
    h = jnp.minimum(2 * meta[BLK_AT] + e, HEADS - 1)
    live = meta[HEADS + h] % R2 == meta[h]
    return live, meta[HEADS + h] // R2


def to_rows(x):
    return jnp.concatenate([x[:, HD * b : HD * b + HD] for b in range(8)], axis=0)


def near_forward_kernel(meta, got, own, small):
    qs, ks, vs, ds = [stack2(got, a) for a in range(4)]
    packs = []
    for e in range(2):
        at = slice(HD * e, HD * e + HD)
        ak, bq = pack_kq(ks[:, at], qs[:, at])
        av, bd = pack_vd(vs[:, at], ds[:, at])
        lses, deltas = [], []
        for j in range(2):
            keys = 256 * (j + 1)
            mask = iota((keys, 256), 0) <= iota((keys, 256), 1) + 256 * j
            lse, delta = forward_core(
                ak[:keys],
                bq[256 * j : 256 * j + 256],
                av[:keys],
                bd[256 * j : 256 * j + 256],
                mask,
            )
            lses.append(lse)
            deltas.append(delta)
        packs.append((to_rows(cat(lses)), to_rows(cat(deltas))))
    active = meta[BLK_AT] < 6
    lse = jnp.where(active, cat([packs[0][0], packs[1][0]]), 0.0)
    delta = jnp.where(active, cat([packs[0][1], packs[1][1]]), 0.0)
    own[:, :128] = lse
    own[:, 128:] = delta
    out = jnp.zeros((128, 128), F32)
    head = iota((128, 128), 0) // 8
    lane = iota((128, 128), 1)
    r, l = iota((8, 128), 0), iota((8, 128), 1)
    for e in range(2):
        live, shift = near_shift(meta, e)
        pick = ((l // HD == e) & (l % HD // 8 == r) & (l % 8 == shift)).astype(F32)
        total = jnp.zeros((8, 128), F32)
        for n, x in enumerate((lse, delta)):
            place = (l == L2_AT + 8 * n + r).astype(F32)
            total = total + exact(exact(pick, x, ((1,), (1,))), place)
        full = jnp.concatenate([total] * 16, axis=0)
        dead = jnp.where(lane < L2_AT + 8, NEG, 0.0)
        full = jnp.where(live, full, dead)
        here = (head == 2 * meta[BLK_AT] + e) & (lane >= L2_AT) & (lane < L2_AT + 16)
        out = out + jnp.where(here, full, 0.0)
    small[...] = out


def far_operands(meta, got):
    kv = jnp.concatenate([got[pl.ds(j, 128, stride=9), :] for j in range(8)], axis=0)
    qd = got[pl.ds(8, 128, stride=9), :]
    ak, bq = pack_kq(kv[:, :HD], qd[:, :HD])
    av, bd = pack_vd(kv[:, HD:], qd[:, HD:])
    key, query = iota((1024, 128), 0), iota((1024, 128), 1)
    mask = (key % 128) * 8 + key // 128 <= query * 8 + meta[BLK_AT]
    return ak, bq, av, bd, mask


def far_forward_kernel(meta, got, near1, small1, near2, small2, own, send):
    lse, delta = forward_core(*far_operands(meta, got))
    active = meta[SEG_AT] < HEADS
    lse = jnp.where(active, lse, 0.0)
    delta = jnp.where(active, delta, 0.0)
    own[0:1, :] = lse
    own[1:2, :] = delta
    sub, lane = iota((128, 128), 0), iota((128, 128), 1)
    out = small1[...] + small2[...]
    for n, x in enumerate((lse, delta)):
        column = jnp.sum(jnp.where(sub == lane, x, 0.0), axis=1, keepdims=True)
        out = out + jnp.where(lane == OWN_AT + n, column, 0.0)
        place = (lane == L3_AT + 8 * n + sub % 8).astype(F32)
        out = out + exact(jnp.where(sub // 8 == lane // 8, x, 0.0), place)
    for n in range(2):
        cols = slice(128 * n, 128 * n + 128)
        send[pl.ds(n, 128, stride=5), :] = jnp.concatenate([near1[:, cols]] * 16, axis=0)
        send[pl.ds(2 + n, 128, stride=5), :] = jnp.concatenate([near2[:, cols]] * 16, axis=0)
    send[pl.ds(4, 128, stride=5), :] = out


def far_backward_kernel(meta, got, own, stats, send):
    small = stats[pl.ds(4, 128, stride=5), :]
    sub, lane = iota((128, 128), 0), iota((128, 128), 1)
    r8, l8 = iota((8, 128), 0), iota((8, 128), 1)
    picks = ((l8 == L1_AT + 8 * r8 + meta[BLK_AT]) & (r8 < 2)).astype(F32)
    first = exact(picks, small, ((1,), (1,)))
    here = sub == 8 * (lane // 8) + meta[SEG_AT] // 2
    second = []
    for n in range(2):
        place = (sub == L2_AT + 8 * n + lane % 8).astype(F32)
        spread = exact(small, place)
        second.append(jnp.sum(jnp.where(here, spread, 0.0), axis=0, keepdims=True))
    lse, delta = merge(
        [(first[0:1], first[1:2]), (second[0], second[1]), (own[0:1, :], own[1:2, :])]
    )
    ak, bq, av, bd, mask = far_operands(meta, got)
    dv, dk, at, qt = backward_core(ak, bq, av, bd, mask, lse, delta)
    kv = both(fold(dk), fold(dv))
    for j in range(8):
        send[pl.ds(j, 128, stride=9), :] = kv[128 * j : 128 * j + 128]
    send[pl.ds(8, 128, stride=9), :] = jnp.concatenate([at, qt], axis=0).T


def near_backward_kernel(meta, got, own, stats, send):
    base = 40 * meta[SEG_AT]
    first = [stats[pl.ds(base + n, 8, stride=5), :] for n in range(2)]
    r, l = iota((8, 128), 0), iota((8, 128), 1)
    third = [jnp.zeros((8, 128), F32), jnp.zeros((8, 128), F32)]
    covered = jnp.zeros((8, 128), jnp.bool_)
    for e in range(2):
        live, shift = near_shift(meta, e)
        cover = (l // HD == e) & (l % 8 == shift) & live
        covered = covered | cover
        pick = (cover & (l % HD // 8 == r)).astype(F32)
        h = 2 * meta[BLK_AT] + e
        far = stats[pl.ds(40 * h + 4, 8, stride=5), :]
        for n in range(2):
            at = L3_AT + 8 * n
            third[n] = third[n] + exact(far[:, at : at + 8], pick, ((0,), (0,)))
    lse, delta = merge(
        [
            (first[0], first[1]),
            (own[:, :128], own[:, 128:]),
            (jnp.where(covered, third[0], NEG), jnp.where(covered, third[1], 0.0)),
        ]
    )
    qs, ks, vs, ds = [stack2(got, a) for a in range(4)]
    ats, qts, dks, dvs = [], [], [], []
    for e in range(2):
        at = slice(HD * e, HD * e + HD)
        ak, bq = pack_kq(ks[:, at], qs[:, at])
        av, bd = pack_vd(vs[:, at], ds[:, at])
        parts = []
        for j in range(2):
            keys = 256 * (j + 1)
            rows = slice(256 * j, 256 * j + 256)
            mask = iota((keys, 256), 0) <= iota((keys, 256), 1) + 256 * j
            lse_j = cat([lse[b : b + 1, at] for b in range(4 * j, 4 * j + 4)])
            delta_j = cat([delta[b : b + 1, at] for b in range(4 * j, 4 * j + 4)])
            parts.append(
                backward_core(ak[:keys], bq[rows], av[:keys], bd[rows], mask, lse_j, delta_j)
            )
        dvs.append(jnp.concatenate([parts[0][0] + parts[1][0][:256], parts[1][0][256:]], axis=0))
        dks.append(jnp.concatenate([parts[0][1] + parts[1][1][:256], parts[1][1][256:]], axis=0))
        ats.append(cat([parts[0][2], parts[1][2]]))
        qts.append(cat([parts[0][3], parts[1][3]]))
    results = (
        jnp.concatenate(ats, axis=0).T,
        jnp.concatenate(qts, axis=0).T,
        both(fold(dks[0]), fold(dks[1])),
        both(fold(dvs[0]), fold(dvs[1])),
    )
    for a, x in enumerate(results):
        for b in range(8):
            send[b * 256 + a * LIVE2 : b * 256 + (a + 1) * LIVE2, :] = x[LIVE2 * b : LIVE2 * b + LIVE2]


def local_backward_kernel(meta, q, k, v, d, own, stats, home3, out, joint, panel, sems):
    fetch((q, k, v, d), panel, sems)
    base = 40 * meta[SEG_AT]
    shift2 = head_column(meta, 0, (16, ROWS))
    shift3 = head_column(meta, HEADS, (16, ROWS))
    row = iota((16, ROWS), 1)
    live2 = row % R2 == shift2
    live3 = row % R3 == shift3
    small = stats[pl.ds(4, 128, stride=5), :]
    from_near = (iota((128, ROWS), 1) // R2 == iota((128, ROWS), 0) % LIVE2).astype(F32)
    group = (iota((16, 128), 0) == iota((16, 128), 1) // 8).astype(F32)
    spot = iota((128, ROWS), 0) % 8 == iota((128, ROWS), 1) // R3
    second, third = [], []
    for n in range(2):
        x = stats[pl.ds(base + 2 + n, 8, stride=5), :]
        halves = half_mask(16)
        y = jnp.where(halves, exact(pair_rows((16, 8), 0, 0, 1), x), 0.0)
        z = jnp.where(halves, 0.0, exact(pair_rows((16, 8), 1, 0, 1), x))
        second.append(jnp.where(live2, exact(y + z, from_near), 0.0 if n else NEG))
        column = jnp.where(spot, small[:, OWN_AT + n : OWN_AT + n + 1], 0.0)
        third.append(jnp.where(live3, exact(group, column), 0.0 if n else NEG))
    lse, delta = merge([(own[:, :ROWS], own[:, ROWS:]), tuple(second), tuple(third)])
    joint[:, :ROWS] = lse
    joint[:, ROWS:] = delta
    mask = iota((ROWS, ROWS), 0) <= iota((ROWS, ROWS), 1)
    low = half_mask(LIVE3)

    def step(i, carry):
        arrive((q, k, v, d), panel, sems, i)
        qp, kp, vp, dp = [panel[block(a, i), :] for a in range(4)]
        res = []
        for e in range(2):
            at = slice(HD * e, HD * e + HD)
            ak, bq = pack_kq(kp[:, at], qp[:, at])
            av, bd = pack_vd(vp[:, at], dp[:, at])
            lse_h = joint[pl.ds(2 * i + e, 1), :ROWS]
            delta_h = joint[pl.ds(2 * i + e, 1), ROWS:]
            res.append(backward_core(ak, bq, av, bd, mask, lse_h, delta_h))
        out[block(0, i), :] = jnp.concatenate([res[0][2], res[1][2]], axis=0).T
        out[block(1, i), :] = jnp.concatenate([res[0][3], res[1][3]], axis=0).T
        out[block(2, i), :] = both(fold(res[0][1]), fold(res[1][1]))
        out[block(3, i), :] = both(fold(res[0][0]), fold(res[1][0]))
        for e in range(2):
            h = 2 * i + e
            kv = home3[pl.ds(72 * h, LIVE3), :]
            for r in range(1, LIVE3):
                kv = kv + home3[pl.ds(72 * h + 9 * r, LIVE3), :]
            aq = home3[pl.ds(72 * h + 8, LIVE3, stride=9), :]
            kv_turn, aq_turn = pltpu.roll(kv, HD, 1), pltpu.roll(aq, HD, 1)
            parts = (aq, aq_turn, kv, kv_turn) if e == 0 else (aq_turn, aq, kv_turn, kv)
            keep = low if e == 0 else ~low
            for a, x in enumerate(parts):
                rows = pl.ds(ROWS * (6 * a + i) + meta[HEADS + h], LIVE3, stride=R3)
                out[rows, :] = out[rows, :] + jnp.where(keep, x, 0.0)
        return carry

    lax.fori_loop(0, 6, step, 0)


def combine_kernel(meta, local, got, at_out, dq_out, dk_out, dv_out, panel, sems):
    low = half_mask(LIVE2)
    copies = []
    for b in range(6):
        for a, out in enumerate((at_out, dq_out, dk_out, dv_out)):
            base = ROWS * (6 * a + b)
            panel[base : base + ROWS, :] = local[base : base + ROWS, :]
            x = got[b * 256 + a * LIVE2 : b * 256 + (a + 1) * LIVE2, :]
            for e in range(2):
                rows = pl.ds(base + meta[2 * b + e], LIVE2, stride=R2)
                keep = low if e == 0 else ~low
                panel[rows, :] = panel[rows, :] + jnp.where(keep, x, 0.0)
            copies.append(
                pltpu.make_async_copy(
                    panel.at[block(a, b), :], out.at[:, columns(b)], sems.at[6 * a + b]
                )
            )
            copies[-1].start()
    for copy in copies:
        copy.wait()


SMEM = pl.BlockSpec(memory_space=pltpu.SMEM)
HBM = pl.BlockSpec(memory_space=pltpu.HBM)
VMEM = pl.BlockSpec(memory_space=pltpu.VMEM)
PANEL = pltpu.VMEM((24 * ROWS, 128), F32)
FETCH = [PANEL, pltpu.SemaphoreType.DMA((24,))]


def call(kernel, name, outs, args, flops, mib, scratch=(), hbm=(), out_spec=VMEM):
    shapes = [x if hasattr(x, "memory_space") else jax.ShapeDtypeStruct(x, F32) for x in outs]
    return pl.pallas_call(
        kernel,
        name=name,
        out_shape=shapes,
        in_specs=[SMEM] + [HBM if i in hbm else VMEM for i in range(1, len(args))],
        out_specs=[out_spec] * len(outs),
        scratch_shapes=list(scratch),
        compiler_params=pltpu.CompilerParams(vmem_limit_bytes=mib * 1024 * 1024),
        cost_estimate=pl.CostEstimate(flops=flops, bytes_accessed=4_000_000, transcendentals=0),
    )(*args)


def swap_near(x):
    return lax.all_to_all(x, "blk", 0, 0, tiled=True)


def swap_all(x):
    return lax.all_to_all(x.reshape(128, -1), ALL, 0, 0, tiled=True).reshape(-1, 128)


def body(q, k, v, d, offsets):
    place = jnp.stack([lax.axis_index("seg"), lax.axis_index("blk")]).astype(jnp.int32)
    meta = jnp.concatenate([offsets.reshape(-1), place])
    rows = tuple(pltpu.with_memory_space_constraint(x, pltpu.HBM) for x in (q, k, v, d))
    given = (1, 2, 3, 4)
    (send2,) = call(
        pick_near_kernel, "pick_near", [(2048, 128)], (offsets, *rows), 10**9, 16, FETCH, given
    )
    got2 = swap_near(send2)
    (send3,) = call(
        pick_far_kernel, "pick_far", [(1152, 128)], (meta, *rows), 10**9, 16, FETCH, given
    )
    got3 = swap_all(send3)
    stats1, near1, small1 = call(
        local_forward_kernel,
        "local_forward",
        [(16, 2 * ROWS), (8, 256), (128, 128)],
        (meta, *rows),
        8 * 10**9,
        16,
        FETCH,
        given,
    )
    near2, small2 = call(
        near_forward_kernel, "near_forward", [(8, 256), (128, 128)], (meta, got2), 4 * 10**9, 24
    )
    own3, send_stats = call(
        far_forward_kernel,
        "far_forward",
        [(8, 128), (640, 128)],
        (meta, got3, near1, small1, near2, small2),
        2 * 10**9,
        16,
    )
    stats = swap_all(send_stats)
    (back3,) = call(
        far_backward_kernel, "far_backward", [(1152, 128)], (meta, got3, own3, stats), 3 * 10**9, 16
    )
    home3 = swap_all(back3)
    (back2,) = call(
        near_backward_kernel,
        "near_backward",
        [(2048, 128)],
        (meta, got2, near2, stats),
        8 * 10**9,
        24,
    )
    home2 = swap_near(back2)
    (local,) = call(
        local_backward_kernel,
        "local_backward",
        [PANEL],
        (meta, *rows, stats1, stats, home3),
        14 * 10**9,
        20,
        [pltpu.VMEM((16, 2 * ROWS), F32)] + FETCH,
        given,
    )
    local = pltpu.with_memory_space_constraint(local, pltpu.VMEM)
    return tuple(
        call(
            combine_kernel,
            "combine",
            [(ROWS, HEADS * HD)] * 4,
            (meta, local, home2),
            2 * 10**9,
            16,
            FETCH,
            out_spec=HBM,
        )
    )


def solution(mesh):
    rows = P(ALL, None)
    return jax.shard_map(
        body,
        mesh=mesh,
        in_specs=(rows, rows, rows, rows, P()),
        out_specs=(rows, rows, rows, rows),
        check_vma=False,
    )
```

```python
import functools

import jax
import jax.numpy as jnp
from jax import lax
from jax.experimental import pallas as pl
from jax.experimental.pallas import tpu as pltpu
from jax.sharding import PartitionSpec as P

HEADS = 12
HD = 64
ROWS = 256
LIVE2 = 64
LIVE3 = 8
R2 = 4
R3 = 32
NEG = -1e30
SCALE = HD**-0.5
BF = jnp.bfloat16
F32 = jnp.float32
ALL = ("seg", "blk")
SEG_AT, BLK_AT = 24, 25
FAR_AT, STAT_AT, MESSAGE = 256, 288, 296
PAIR = 72


def nt(a, b):
    return lax.dot_general(a, b, (((1,), (1,)), ((), ())), preferred_element_type=F32)


def nn(a, b):
    return lax.dot_general(a, b, (((1,), (0,)), ((), ())), preferred_element_type=F32)


def tn(a, b):
    return lax.dot_general(a, b, (((0,), (0,)), ((), ())), preferred_element_type=F32)


def exact(a, b, dims=((1,), (0,))):
    return lax.dot_general(
        a, b, (dims, ((), ())), preferred_element_type=F32, precision=lax.Precision.HIGHEST
    )


def iota(shape, axis):
    return lax.broadcasted_iota(jnp.int32, shape, axis)


def split2(x):
    first = x.astype(BF)
    return first, (x - first.astype(F32)).astype(BF)


def split3(x):
    first = x.astype(BF)
    rest = x - first.astype(F32)
    second = rest.astype(BF)
    return first, second, (rest - second.astype(F32)).astype(BF)


def cat(parts):
    return jnp.concatenate(parts, axis=1)


def pack_kq(k, q):
    k0, k1, k2 = split3(k)
    q0, q1, q2 = split3(q * SCALE)
    return cat([k0, k1, k0, k1, k0, k2]), cat([q0, q1, q1, q0, q2, q0])


def pack_vd(v, d):
    v0, v1 = split2(v)
    d0, d1 = split2(d)
    return cat([v0, v1, v0, v1]), cat([d0, d1, d1, d0])


def forward_core(ak, bq, av, bd, mask):
    s = jnp.where(mask, nt(ak, bq), NEG)
    dp = nt(av, bd)
    top = jnp.max(s, axis=0, keepdims=True)
    p = jnp.exp(s - top)
    total = jnp.sum(p, axis=0, keepdims=True)
    cross = jnp.sum(p * dp, axis=0, keepdims=True)
    return top, total, cross / total, p, dp


def backward_core(p, dp, delta, ak, bq, av, bd):
    g = p * (dp - delta)
    p0, p1 = split2(p)
    g0, g1 = split2(g)
    d01, q01, v01, k01 = bd[:, :128], bq[:, :128], av[:, :128], ak[:, :128]
    dv = nn(p0, d01) + nn(p1, d01)
    dk = nn(g0, q01) + nn(g1, q01)
    at = tn(v01, p0) + tn(v01, p1)
    qt = tn(k01, g0) + tn(k01, g1)
    return at[:HD] + at[HD:], (qt[:HD] + qt[HD:]) * SCALE, dk, dv


def fold(x):
    return x + pltpu.roll(x, HD, 1)


def half_mask(rows):
    return iota((rows, 128), 1) < HD


def both(a, b):
    return jnp.where(half_mask(a.shape[0]), a, b)


def merge(levels):
    top = functools.reduce(jnp.maximum, [lse for lse, _ in levels])
    weights = [jnp.exp(lse - top) for lse, _ in levels]
    total = functools.reduce(jnp.add, weights)
    delta = functools.reduce(jnp.add, [w * d for w, (_, d) in zip(weights, levels)])
    return top + jnp.log(total), delta / total


def block(a, b):
    at = ROWS * (6 * a + b)
    return pl.ds(at if isinstance(b, int) else pl.multiple_of(at, ROWS), ROWS)


def columns(b):
    return pl.ds(128 * b if isinstance(b, int) else pl.multiple_of(128 * b, 128), 128)


def inward(refs, panel, sems, b):
    return [
        pltpu.make_async_copy(
            ref.at[:, columns(b)], panel.at[block(a, b), :], sems.at[6 * a + b]
        )
        for a, ref in enumerate(refs)
    ]


def fetch(refs, panel, sems):
    for b in range(6):
        for copy in inward(refs, panel, sems, b):
            copy.start()


def arrive(refs, panel, sems, b):
    for copy in inward(refs, panel, sems, b):
        copy.wait()


def live_positions(near, far, skip_far=False):
    lane = iota((1, 128), 1)
    spot = jnp.where(lane < LIVE2, R2 * lane + near, R3 * (lane - LIVE2) + far)
    end = jnp.where(skip_far, LIVE2, LIVE2 + LIVE3)
    return jnp.where(lane < end, spot, -1)


def halves(x, e):
    return x[:, HD * e : HD * e + HD]


def turn(x):
    return pltpu.roll(x, HD, 1)


def open_kernel(offsets, q, k, v, d, send, live, panel, sems):
    fetch((q, k, v, d), panel, sems)

    def step(b, carry):
        arrive((q, k, v, d), panel, sems, b)
        out = pl.multiple_of(MESSAGE * b, 8)
        rows = []
        for a in range(4):
            base = ROWS * (6 * a + b)
            near = both(
                panel[pl.ds(base + offsets[0, 2 * b], LIVE2, stride=R2), :],
                panel[pl.ds(base + offsets[0, 2 * b + 1], LIVE2, stride=R2), :],
            )
            far = both(
                panel[pl.ds(base + offsets[1, 2 * b], LIVE3, stride=R3), :],
                panel[pl.ds(base + offsets[1, 2 * b + 1], LIVE3, stride=R3), :],
            )
            send[pl.ds(out + LIVE2 * a, LIVE2), :] = near
            send[pl.ds(out + FAR_AT + LIVE3 * a, LIVE3), :] = far
            rows.append((near, far))
        pad = jnp.zeros((56, 128), F32)
        keep = pl.multiple_of(2 * PAIR * b, 8)
        queries, grads = [], []
        for n, (a, group) in enumerate(((0, queries), (3, grads))):
            near, far = rows[a]
            live[pl.ds(keep + PAIR * n, LIVE2), :] = near
            live[pl.ds(keep + PAIR * n + LIVE2, LIVE3), :] = far
            group.append(jnp.concatenate([near, far, pad], axis=0))
        kp, vp = panel[block(1, b), :], panel[block(2, b), :]
        for e in range(2):
            ak, bq = pack_kq(halves(kp, e), halves(queries[0], e))
            av, bd = pack_vd(halves(vp, e), halves(grads[0], e))
            spot = live_positions(offsets[0, 2 * b + e], offsets[1, 2 * b + e])
            top, total, delta, _, _ = forward_core(ak, bq, av, bd, iota((ROWS, 128), 0) <= spot)
            send[pl.ds(out + STAT_AT + 2 * e, 1), :] = top + jnp.log(total)
            send[pl.ds(out + STAT_AT + 2 * e + 1, 1), :] = delta
        return carry

    lax.fori_loop(0, 6, step, 0)


def gather_rows(ref, at, count):
    return jnp.concatenate(
        [ref[MESSAGE * b + at : MESSAGE * b + at + count, :] for b in range(8)], axis=0
    )


def stat_rows(ref, n):
    return ref[pl.ds(STAT_AT + n, 8, stride=MESSAGE), :]


def spread_kernel(meta, got, send):
    k, v = gather_rows(got, FAR_AT + 8, 8), gather_rows(got, FAR_AT + 16, 8)
    kv = both(k, turn(v)), both(turn(k), v)
    for s in range(16):
        send[64 * s : 64 * s + 64, :] = kv[s % 2]


def near_shift(meta, e):
    h = jnp.minimum(2 * meta[BLK_AT] + e, HEADS - 1)
    live = meta[HEADS + h] % R2 == meta[h]
    return live, meta[HEADS + h] // R2


def to_rows(x):
    return jnp.concatenate([x[:, HD * b : HD * b + HD] for b in range(8)], axis=0)


def near_blocks(got):
    qs, ks, vs, ds = [gather_rows(got, a * LIVE2, LIVE2) for a in range(4)]
    for e in range(2):
        ak, bq = pack_kq(halves(ks, e), halves(qs, e))
        av, bd = pack_vd(halves(vs, e), halves(ds, e))
        parts = []
        for j in range(2):
            keys, rows = 256 * (j + 1), slice(256 * j, 256 * j + 256)
            mask = iota((keys, 256), 0) <= iota((keys, 256), 1) + 256 * j
            parts.append((ak[:keys], bq[rows], av[:keys], bd[rows], mask))
        yield parts


def near_forward_kernel(meta, got, own, mine, theirs):
    found = []
    for parts in near_blocks(got):
        lses, deltas = [], []
        for part in parts:
            top, total, delta, _, _ = forward_core(*part)
            lses.append(top + jnp.log(total))
            deltas.append(delta)
        found.append((to_rows(cat(lses)), to_rows(cat(deltas))))
    lse, delta = [cat([found[0][n], found[1][n]]) for n in range(2)]
    own[:, :128] = lse
    own[:, 128:] = delta
    sub, lane = iota((128, 128), 0), iota((128, 128), 1)
    spread = ((sub < 8) & (lane < 64) & (lane % 8 == sub)).astype(F32)
    diagonal = iota((8, 128), 0) == iota((8, 128), 1) // 8
    q, d = gather_rows(got, FAR_AT, 8), gather_rows(got, FAR_AT + 24, 8)
    qd = both(q, turn(d)), both(turn(q), d)
    blocks = []
    for e in range(2):
        live, shift = near_shift(meta, e)
        pick = (sub // HD == e) & (sub % HD // 8 == lane) & (sub % 8 == shift)
        pick = pick.astype(F32)
        merged = merge(
            [
                (turn(stat_rows(got, 2 * e)), turn(stat_rows(got, 2 * e + 1))),
                (jnp.where(live, exact(lse, pick), NEG), exact(delta, pick)),
            ]
        )
        flat = [
            jnp.sum(jnp.where(diagonal, exact(x, spread), 0.0), axis=0, keepdims=True)
            for x in merged
        ]
        blocks.append(jnp.concatenate([qd[e], *flat, jnp.zeros((6, 128), F32)], axis=0))
    first = meta[SEG_AT] % 2 == 0
    mine[...] = jnp.where(first, blocks[0], blocks[1])
    theirs[...] = jnp.where(first, blocks[1], blocks[0])


def far_kernel(meta, kv, mine, pair, send, keep, back):
    first = meta[SEG_AT] % 2 == 0
    x, y = mine[...], pair[...]
    low, high = jnp.where(first, x, y), jnp.where(first, y, x)
    qd = jnp.concatenate([low[:LIVE2], high[:LIVE2]], axis=0)
    known = [both(low[64 + n : 65 + n], turn(high[64 + n : 65 + n])) for n in range(2)]
    ak, bq = pack_kq(kv[:, :HD], qd[:, :HD])
    av, bd = pack_vd(kv[:, HD:], qd[:, HD:])
    start = 64 * (meta[SEG_AT] - meta[SEG_AT] % 2)
    mask = iota((1024, 128), 0) <= iota((1024, 128), 1) + start
    top, total, delta3, p, dp = forward_core(ak, bq, av, bd, mask)
    lse3 = top + jnp.log(total)
    lse, delta = merge([tuple(known), (lse3, delta3)])
    at, qt, dk, dv = backward_core(p * jnp.exp(top - lse), dp, delta, ak, bq, av, bd)
    send[...] = both(fold(dk), fold(dv))
    aq = jnp.concatenate([at, qt], axis=0).T
    stats = (lse3, delta3, lse, delta)
    front = jnp.concatenate([aq[:LIVE2], *stats, jnp.zeros((4, 128), F32)], axis=0)
    rear = jnp.concatenate([aq[LIVE2:], *[turn(x) for x in stats], jnp.zeros((4, 128), F32)], axis=0)
    keep[...] = jnp.where(first, front, rear)
    back[...] = jnp.where(first, rear, front)


def by_head(meta, keep, back):
    first = meta[SEG_AT] % 2 == 0
    x, y = keep[...], back[...]
    return jnp.where(first, x, y), jnp.where(first, y, x)


def near_backward_kernel(meta, got, own, keep, back, out):
    far = by_head(meta, keep, back)
    sub, lane = iota((128, 128), 0), iota((128, 128), 1)
    diagonal = iota((8, 128), 0) == iota((8, 128), 1) // 8
    known = [both(stat_rows(got, n), turn(stat_rows(got, 2 + n))) for n in range(2)]
    third = [jnp.zeros((8, 128), F32), jnp.zeros((8, 128), F32)]
    covered = jnp.zeros((8, 128), jnp.bool_)
    l = iota((8, 128), 1)
    for e in range(2):
        live, shift = near_shift(meta, e)
        covered = covered | ((l // HD == e) & (l % 8 == shift) & live)
        place = (sub < 64) & (sub % 8 == lane % HD // 8) & (lane // HD == e)
        place = place.astype(F32)
        for n in range(2):
            x = jnp.where(diagonal, far[e][64 + n : 65 + n], 0.0)
            third[n] = third[n] + exact(x, place)
    lse, delta = merge(
        [
            tuple(known),
            (own[:, :128], own[:, 128:]),
            (jnp.where(covered, third[0], NEG), jnp.where(covered, third[1], 0.0)),
        ]
    )
    tail = ((sub < 64) & (lane == LIVE2 + sub % 8)).astype(F32)
    for e in range(2):
        for n, x in enumerate((lse, delta)):
            rest = exact(jnp.where(diagonal, far[e][66 + n : 67 + n], 0.0), tail)
            near = x if e == 0 else turn(x)
            out[pl.ds(STAT_AT + 2 * e + n, 8, stride=MESSAGE), :] = both(near, rest)
    ats, qts, dks, dvs = [], [], [], []
    for e, parts in enumerate(near_blocks(got)):
        results = []
        for j, (ak, bq, av, bd, mask) in enumerate(parts):
            at = slice(HD * e, HD * e + HD)
            lse_j = cat([lse[b : b + 1, at] for b in range(4 * j, 4 * j + 4)])
            delta_j = cat([delta[b : b + 1, at] for b in range(4 * j, 4 * j + 4)])
            p = jnp.exp(jnp.where(mask, nt(ak, bq), NEG) - lse_j)
            results.append(backward_core(p, nt(av, bd), delta_j, ak, bq, av, bd))
        ats.append(cat([results[0][0], results[1][0]]))
        qts.append(cat([results[0][1], results[1][1]]))
        for group, n in ((dks, 2), (dvs, 3)):
            x, y = results[0][n], results[1][n]
            group.append(jnp.concatenate([x + y[:256], y[256:]], axis=0))
    finals = (
        jnp.concatenate(ats, axis=0).T,
        jnp.concatenate(qts, axis=0).T,
        both(fold(dks[0]), fold(dks[1])),
        both(fold(dvs[0]), fold(dvs[1])),
    )
    for a, x in enumerate(finals):
        for b in range(8):
            at = MESSAGE * b + a * LIVE2
            out[at : at + LIVE2, :] = x[LIVE2 * b : LIVE2 * b + LIVE2]


def merge_kernel(meta, near, parts, keep, back, out):
    aq = by_head(meta, keep, back)
    kv = []
    for e in range(2):
        total = parts[64 * e : 64 * e + 64, :]
        for s in range(e + 2, 16, 2):
            total = total + parts[64 * s : 64 * s + 64, :]
        kv.append(total)
    aq = [x[:LIVE2] for x in aq]
    far = (
        both(aq[0], turn(aq[1])),
        both(turn(aq[0]), aq[1]),
        both(kv[0], turn(kv[1])),
        both(turn(kv[0]), kv[1]),
    )
    for b in range(8):
        base = MESSAGE * b
        out[base : base + FAR_AT, :] = near[base : base + FAR_AT, :]
        out[base + STAT_AT : base + MESSAGE, :] = near[base + STAT_AT : base + MESSAGE, :]
        for a, x in enumerate(far):
            out[base + FAR_AT + 8 * a : base + FAR_AT + 8 * a + 8, :] = x[8 * b : 8 * b + 8]


def outward(panel, out, sems, a, b):
    return pltpu.make_async_copy(panel.at[block(a, b), :], out.at[block(a, b), :], sems.at[6 * a + b])


def local_kernel(meta, q, k, v, d, out, panel, sems, result, out_sems):
    fetch((q, k, v, d), panel, sems)
    mask = iota((ROWS, ROWS), 0) <= iota((ROWS, ROWS), 1)
    row = iota((1, ROWS), 1)

    def step(b, carry):
        arrive((q, k, v, d), panel, sems, b)
        qp, kp, vp, dp = [panel[block(a, b), :] for a in range(4)]
        res = []
        for e in range(2):
            ak, bq = pack_kq(halves(kp, e), halves(qp, e))
            av, bd = pack_vd(halves(vp, e), halves(dp, e))
            _, total, delta, p, w = forward_core(ak, bq, av, bd, mask)
            h = 2 * b + e
            live = (row % R2 == meta[h]) | (row % R3 == meta[HEADS + h])
            p = p * jnp.where(live, 0.0, 1.0 / total)
            res.append(backward_core(p, w, delta, ak, bq, av, bd))
        result[block(0, b), :] = jnp.concatenate([res[0][0], res[1][0]], axis=0).T
        result[block(1, b), :] = jnp.concatenate([res[0][1], res[1][1]], axis=0).T
        result[block(2, b), :] = both(fold(res[0][2]), fold(res[1][2]))
        result[block(3, b), :] = both(fold(res[0][3]), fold(res[1][3]))
        for a in range(4):
            outward(result, out, out_sems, a, b).start()
        return carry

    lax.fori_loop(0, 6, step, 0)
    for b in range(6):
        for a in range(4):
            outward(result, out, out_sems, a, b).wait()


def close_kernel(meta, k, v, local, live, got, at_out, dq_out, dk_out, dv_out, kv, sems, panel, in_sems, out_sems):
    outs = (at_out, dq_out, dk_out, dv_out)
    for b in range(6):
        for copy in inward((k, v), kv, sems, b):
            copy.start()
        for a in range(4):
            outward(local, panel, in_sems, a, b).start()
    low2, low3 = half_mask(LIVE2), half_mask(LIVE3)

    def home(a, b, out):
        return pltpu.make_async_copy(
            panel.at[block(a, b), :], out.at[:, columns(b)], out_sems.at[6 * a + b]
        )

    def step(b, carry):
        arrive((k, v), kv, sems, b)
        kp, vp = kv[block(0, b), :], kv[block(1, b), :]
        pad = jnp.zeros((56, 128), F32)
        keep = pl.multiple_of(2 * PAIR * b, 8)
        qp, dp = [
            jnp.concatenate([live[pl.ds(keep + PAIR * n, PAIR), :], pad], axis=0) for n in range(2)
        ]
        base = pl.multiple_of(MESSAGE * b, 8)
        res = []
        for e in range(2):
            h = 2 * b + e
            near, far = meta[h], meta[HEADS + h]
            ak, bq = pack_kq(halves(kp, e), halves(qp, e))
            av, bd = pack_vd(halves(vp, e), halves(dp, e))
            mask = iota((ROWS, 128), 0) <= live_positions(near, far, far % R2 == near)
            lse = got[pl.ds(base + STAT_AT + 2 * e, 1), :]
            delta = got[pl.ds(base + STAT_AT + 2 * e + 1, 1), :]
            p = jnp.exp(jnp.where(mask, nt(ak, bq) - lse, NEG))
            res.append(backward_core(p, nt(av, bd), delta, ak, bq, av, bd))
        rows = [jnp.concatenate([res[0][n], res[1][n]], axis=0).T for n in range(2)]
        dense = [both(fold(res[0][n]), fold(res[1][n])) for n in (2, 3)]
        for a, out in enumerate(outs):
            outward(local, panel, in_sems, a, b).wait()
            near = got[pl.ds(base + LIVE2 * a, LIVE2), :]
            far = got[pl.ds(base + FAR_AT + LIVE3 * a, LIVE3), :]
            if a < 2:
                near = near + rows[a][:LIVE2]
                far = far + rows[a][LIVE2 : LIVE2 + LIVE3]
            else:
                panel[block(a, b), :] = panel[block(a, b), :] + dense[a - 2]
            at = ROWS * (6 * a + b)
            for e in range(2):
                spot = pl.ds(at + meta[2 * b + e], LIVE2, stride=R2)
                panel[spot, :] = panel[spot, :] + jnp.where(low2 if e == 0 else ~low2, near, 0.0)
                spot = pl.ds(at + meta[HEADS + 2 * b + e], LIVE3, stride=R3)
                panel[spot, :] = panel[spot, :] + jnp.where(low3 if e == 0 else ~low3, far, 0.0)
            home(a, b, out).start()
        return carry

    lax.fori_loop(0, 6, step, 0)
    for b in range(6):
        for a, out in enumerate(outs):
            home(a, b, out).wait()


SMEM = pl.BlockSpec(memory_space=pltpu.SMEM)
HBM = pl.BlockSpec(memory_space=pltpu.HBM)
VMEM = pl.BlockSpec(memory_space=pltpu.VMEM)
PANEL = pltpu.VMEM((24 * ROWS, 128), F32)
COPIES = pltpu.SemaphoreType.DMA((24,))


def call(kernel, name, outs, args, flops, mib, scratch=(), hbm=(), out_spec=VMEM):
    return pl.pallas_call(
        kernel,
        name=name,
        out_shape=[jax.ShapeDtypeStruct(x, F32) if isinstance(x, tuple) else x for x in outs],
        in_specs=[SMEM] + [HBM if i in hbm else VMEM for i in range(1, len(args))],
        out_specs=[out_spec] * len(outs),
        scratch_shapes=list(scratch),
        compiler_params=pltpu.CompilerParams(vmem_limit_bytes=mib * 1024 * 1024),
        cost_estimate=pl.CostEstimate(flops=flops, bytes_accessed=4_000_000, transcendentals=0),
    )(*args)


def in_hbm(x):
    return pltpu.with_memory_space_constraint(x, pltpu.HBM)


def swap(x, axis):
    return lax.all_to_all(x, axis, 0, 0, tiled=True)


def swap_cores(x):
    return lax.ppermute(x, "seg", [(s, s ^ 1) for s in range(lax.axis_size("seg"))])


def body(q, k, v, d, offsets):
    place = jnp.stack([lax.axis_index("seg"), lax.axis_index("blk")]).astype(jnp.int32)
    meta = jnp.concatenate([offsets.reshape(-1), place])
    rows = tuple(in_hbm(x) for x in (q, k, v, d))
    given = (1, 2, 3, 4)
    message, pair, far = (8 * MESSAGE, 128), (PAIR, 128), (1024, 128)
    send, live = call(
        open_kernel,
        "open",
        [message, (12 * PAIR, 128)],
        (offsets, *rows),
        3 * 10**9,
        16,
        [PANEL, COPIES],
        given,
    )
    got = swap(send, "blk")
    (keys,) = call(spread_kernel, "spread", [far], (meta, got), 10**8, 8)
    all_keys = swap(keys, "seg")
    own, mine, theirs = call(
        near_forward_kernel, "near_forward", [(8, 256), pair, pair], (meta, got), 4 * 10**9, 24
    )
    partner = swap_cores(theirs)
    parts, keep, back = call(
        far_kernel, "far", [far, pair, pair], (meta, all_keys, mine, partner), 4 * 10**9, 24
    )
    sums = swap(parts, "seg")
    back = swap_cores(back)
    (near,) = call(
        near_backward_kernel,
        "near_backward",
        [message],
        (meta, got, own, keep, back),
        8 * 10**9,
        24,
    )
    (reply,) = call(merge_kernel, "merge", [message], (meta, near, sums, keep, back), 10**8, 12)
    home = swap(reply, "blk")
    (local,) = call(
        local_kernel,
        "local",
        [pltpu.HBM((24 * ROWS, 128), F32)],
        (meta, *rows),
        16 * 10**9,
        24,
        [PANEL, COPIES, PANEL, COPIES],
        given,
        HBM,
    )
    return tuple(
        call(
            close_kernel,
            "close",
            [(ROWS, HEADS * HD)] * 4,
            (meta, rows[1], rows[2], in_hbm(local), live, home),
            6 * 10**9,
            24,
            [pltpu.VMEM((12 * ROWS, 128), F32), pltpu.SemaphoreType.DMA((12,)), PANEL, COPIES, COPIES],
            (1, 2, 3),
            HBM,
        )
    )


def solution(mesh):
    rows = P(ALL, None)
    return jax.shard_map(
        body,
        mesh=mesh,
        in_specs=(rows, rows, rows, rows, P()),
        out_specs=(rows, rows, rows, rows),
        check_vma=False,
    )
```

```python
import functools

import jax
import jax.numpy as jnp
from jax import lax
from jax.experimental import pallas as pl
from jax.experimental.pallas import tpu as pltpu
from jax.sharding import PartitionSpec as P

HEADS = 12
HD = 64
ROWS = 256
LIVE2 = 64
LIVE3 = 8
R2 = 4
R3 = 32
NEG = -1e30
SCALE = HD**-0.5
BF = jnp.bfloat16
F32 = jnp.float32
ALL = ("seg", "blk")
SEG_AT, BLK_AT = 24, 25
FAR_AT, STAT_AT, MESSAGE = 256, 288, 296
PAIR = 72


def nt(a, b):
    return lax.dot_general(a, b, (((1,), (1,)), ((), ())), preferred_element_type=F32)


def nn(a, b):
    return lax.dot_general(a, b, (((1,), (0,)), ((), ())), preferred_element_type=F32)


def tn(a, b):
    return lax.dot_general(a, b, (((0,), (0,)), ((), ())), preferred_element_type=F32)


def exact(a, b, dims=((1,), (0,))):
    return lax.dot_general(
        a, b, (dims, ((), ())), preferred_element_type=F32, precision=lax.Precision.HIGHEST
    )


def iota(shape, axis):
    return lax.broadcasted_iota(jnp.int32, shape, axis)


def split2(x):
    first = x.astype(BF)
    return first, (x - first.astype(F32)).astype(BF)


def split3(x):
    first = x.astype(BF)
    rest = x - first.astype(F32)
    second = rest.astype(BF)
    return first, second, (rest - second.astype(F32)).astype(BF)


def cat(parts):
    return jnp.concatenate(parts, axis=1)


def pack_kq(k, q):
    k0, k1, k2 = split3(k)
    q0, q1, q2 = split3(q * SCALE)
    return cat([k0, k1, k0, k1, k0, k2]), cat([q0, q1, q1, q0, q2, q0])


def pack_vd(v, d):
    v0, v1 = split2(v)
    d0, d1 = split2(d)
    return cat([v0, v1, v0, v1]), cat([d0, d1, d1, d0])


def forward_core(ak, bq, av, bd, mask):
    s = jnp.where(mask, nt(ak, bq), NEG)
    dp = nt(av, bd)
    top = jnp.max(s, axis=0, keepdims=True)
    p = jnp.exp(s - top)
    total = jnp.sum(p, axis=0, keepdims=True)
    cross = jnp.sum(p * dp, axis=0, keepdims=True)
    return top, total, cross / total, p, dp


def backward_core(p, dp, delta, ak, bq, av, bd):
    g = p * (dp - delta)
    p0, p1 = split2(p)
    g0, g1 = split2(g)
    d01, q01, v01, k01 = bd[:, :128], bq[:, :128], av[:, :128], ak[:, :128]
    dv = nn(p0, d01) + nn(p1, d01)
    dk = nn(g0, q01) + nn(g1, q01)
    at = tn(v01, p0) + tn(v01, p1)
    qt = tn(k01, g0) + tn(k01, g1)
    return at[:HD] + at[HD:], (qt[:HD] + qt[HD:]) * SCALE, dk, dv


def fold(x):
    return x + pltpu.roll(x, HD, 1)


def half_mask(rows):
    return iota((rows, 128), 1) < HD


def both(a, b):
    return jnp.where(half_mask(a.shape[0]), a, b)


def merge(levels):
    top = functools.reduce(jnp.maximum, [lse for lse, _ in levels])
    weights = [jnp.exp(lse - top) for lse, _ in levels]
    total = functools.reduce(jnp.add, weights)
    delta = functools.reduce(jnp.add, [w * d for w, (_, d) in zip(weights, levels)])
    return top + jnp.log(total), delta / total


def block(a, b):
    at = ROWS * (6 * a + b)
    return pl.ds(at if isinstance(b, int) else pl.multiple_of(at, ROWS), ROWS)


def columns(b):
    return pl.ds(128 * b if isinstance(b, int) else pl.multiple_of(128 * b, 128), 128)


def inward(refs, panel, sems, b):
    return [
        pltpu.make_async_copy(
            ref.at[:, columns(b)], panel.at[block(a, b), :], sems.at[6 * a + b]
        )
        for a, ref in enumerate(refs)
    ]


def fetch(refs, panel, sems):
    for b in range(6):
        for copy in inward(refs, panel, sems, b):
            copy.start()


def arrive(refs, panel, sems, b):
    for copy in inward(refs, panel, sems, b):
        copy.wait()


def near_positions(meta, b):
    lane = iota((1, 128), 1)
    return R2 * (lane % LIVE2) + jnp.where(lane < LIVE2, meta[2 * b], meta[2 * b + 1])


def far_positions(meta, alone):
    lane = iota((1, 128), 1)
    spot = jnp.full((1, 128), -1, jnp.int32)
    for h in range(HEADS):
        near, far = meta[h], meta[HEADS + h]
        start = jnp.where(far % R2 == near, -1, far) if alone else far
        here = lane // LIVE3 == h
        spot = jnp.where(here & (start >= 0), start + R3 * (lane % LIVE3), spot)
    return spot


def apart(x):
    low = half_mask(x.shape[0])
    return [jnp.where(low, x, 0.0), jnp.where(low, 0.0, x)]


def live_block(near, far, b):
    parts = apart(near)
    if b:
        parts.append(jnp.zeros((16 * b, 128), F32))
    parts += apart(far)
    parts.append(jnp.zeros((112 - 16 * b, 128), F32))
    return jnp.concatenate(parts, axis=0)


def live_products(k, v, q, d):
    k0, k1, k2 = split3(k)
    q0, q1, q2 = split3(q * SCALE)
    v0, v1 = split2(v)
    d0, d1 = split2(d)
    s = nt(cat([k0, k1, k0, k1, k0, k2]), cat([q0, q1, q1, q0, q2, q0]))
    return s, nt(cat([v0, v1, v0, v1]), cat([d0, d1, d1, d0]))


def live_forward(s, dp, spot):
    s = jnp.where(iota((ROWS, 128), 0) <= spot, s, NEG)
    top = jnp.max(s, axis=0, keepdims=True)
    p = jnp.exp(s - top)
    total = jnp.sum(p, axis=0, keepdims=True)
    delta = jnp.sum(p * dp, axis=0, keepdims=True) / total
    return top + jnp.log(total), delta, p / total


def halves(x, e):
    return x[:, HD * e : HD * e + HD]


def turn(x):
    return pltpu.roll(x, HD, 1)


class Flat:
    def __init__(self, ref):
        self.ref = ref

    def __getitem__(self, i):
        return self.ref[i // HEADS, i % HEADS]


def open_kernel(offsets, q, k, v, d, out, live, panel, sems, send, out_sems, shifts, shift_sem):
    shifting = pltpu.make_async_copy(offsets, shifts, shift_sem)
    shifting.start()
    fetch((q, k, v, d), panel, sems)
    shifting.wait()
    meta = Flat(shifts)
    copies, rows = [], []

    def leave(at, count):
        at = pl.ds(at, count)
        copies.append(pltpu.make_async_copy(send.at[at, :], out.at[at, :], out_sems.at[len(copies)]))
        copies[-1].start()

    for b in range(6):
        arrive((q, k, v, d), panel, sems, b)
        at = MESSAGE * b
        found = []
        for a in range(4):
            base = ROWS * (6 * a + b)
            near = both(
                panel[pl.ds(base + meta[2 * b], LIVE2, stride=R2), :],
                panel[pl.ds(base + meta[2 * b + 1], LIVE2, stride=R2), :],
            )
            far = both(
                panel[pl.ds(base + meta[HEADS + 2 * b], LIVE3, stride=R3), :],
                panel[pl.ds(base + meta[HEADS + 2 * b + 1], LIVE3, stride=R3), :],
            )
            send[at + LIVE2 * a : at + LIVE2 * a + LIVE2, :] = near
            send[at + FAR_AT + LIVE3 * a : at + FAR_AT + LIVE3 * a + LIVE3, :] = far
            found.append((near, far))
        leave(at, STAT_AT)
        for n, (near, far) in enumerate((found[0], found[3])):
            keep = PAIR * (2 * b + n)
            live[keep : keep + LIVE2, :] = near
            live[keep + LIVE2 : keep + PAIR, :] = far
        rows.append((found[0], found[3]))
    far_s = far_dp = jnp.zeros((ROWS, 128), F32)
    known = []
    for b in range(6):
        s, dp = live_products(
            panel[block(1, b), :],
            panel[block(2, b), :],
            live_block(*rows[b][0], b),
            live_block(*rows[b][1], b),
        )
        far_s, far_dp = far_s + s[:, 128:], far_dp + dp[:, 128:]
        known.append(live_forward(s[:, :128], dp[:, :128], near_positions(meta, b))[:2])
    far = live_forward(far_s, far_dp, far_positions(meta, False))[:2]
    for b in range(6):
        at = MESSAGE * b + STAT_AT
        turned = [pltpu.roll(x, (128 - 16 * b) % 128, 1) for x in far]
        send[at : at + 8, :] = jnp.concatenate([*known[b], *turned, jnp.zeros((4, 128), F32)], axis=0)
        leave(at, 8)
    for copy in copies:
        copy.wait()


def live_kernel(meta, k, v, live, weights, slopes, out_rows, stats, panel, sems, kept, rows_kept, out_sems):
    fetch((k, v), panel, sems)
    stats[...] = jnp.zeros_like(stats)
    far_s = far_dp = jnp.zeros((ROWS, 128), F32)
    copies = []

    def record(n, s, dp, spot):
        lse, delta, p = live_forward(s, dp, spot)
        pair = cat(split2(p)), cat(split2(p * (dp - delta)))
        for m, (x, out) in enumerate(zip(pair, (weights, slopes))):
            at = pl.ds(ROWS * n, ROWS)
            kept[m, at, :] = x
            copies.append(pltpu.make_async_copy(kept.at[m, at, :], out.at[at, :], out_sems.at[7 * m + n]))
            copies[-1].start()
        stats[n : n + 1, :] = lse
        stats[8 + n : 9 + n, :] = delta
        return pair

    def products(b, p, h):
        kb, vb = cat(split2(panel[block(0, b), :] * SCALE)), cat(split2(panel[block(1, b), :]))
        both_sides = tn(p, cat([vb, kb]))
        for n, x in enumerate((both_sides[:, :256], tn(h, kb), both_sides[:, 256:])):
            yield 6 * PAIR * n + PAIR * b, x[:128, :128] + x[:128, 128:] + x[128:, :128] + x[128:, 128:]

    for b in range(6):
        arrive((k, v), panel, sems, b)
    for b in range(6):
        rows = []
        for n in range(2):
            keep = PAIR * (2 * b + n)
            rows.append((live[keep : keep + LIVE2, :], live[keep + LIVE2 : keep + PAIR, :]))
        s, dp = live_products(
            panel[block(0, b), :],
            panel[block(1, b), :],
            live_block(*rows[0], b),
            live_block(*rows[1], b),
        )
        far_s, far_dp = far_s + s[:, 128:], far_dp + dp[:, 128:]
        p, h = record(b, s[:, :128], dp[:, :128], near_positions(meta, b))
        for at, x in products(b, p, h):
            rows_kept[at : at + LIVE2, :] = both(x[:LIVE2], x[LIVE2:])
    p, h = record(6, far_s, far_dp, far_positions(meta, True))
    for b in range(6):
        for at, x in products(b, p, h):
            low, high = x[16 * b : 16 * b + 8], x[16 * b + 8 : 16 * b + 16]
            rows_kept[at + LIVE2 : at + PAIR, :] = both(low, high)
    copies.append(pltpu.make_async_copy(rows_kept, out_rows, out_sems.at[14]))
    copies[-1].start()
    for copy in copies:
        copy.wait()


def gather_rows(ref, at, count):
    return jnp.concatenate(
        [ref[MESSAGE * b + at : MESSAGE * b + at + count, :] for b in range(8)], axis=0
    )


def stat_rows(ref, n):
    return ref[pl.ds(STAT_AT + n, 8, stride=MESSAGE), :]


def spread_kernel(meta, got, out, kv, sems):
    k, v = gather_rows(got, FAR_AT + 8, 8), gather_rows(got, FAR_AT + 16, 8)
    kv[0] = both(k, turn(v))
    kv[1] = both(turn(k), v)
    copies = [
        pltpu.make_async_copy(kv.at[s % 2], out.at[pl.ds(64 * s, 64), :], sems.at[s])
        for s in range(16)
    ]
    for copy in copies:
        copy.start()
    for copy in copies:
        copy.wait()


def near_shift(meta, e):
    h = jnp.minimum(2 * meta[BLK_AT] + e, HEADS - 1)
    live = meta[HEADS + h] % R2 == meta[h]
    return live, meta[HEADS + h] // R2


def to_rows(x):
    return jnp.concatenate([x[:, HD * b : HD * b + HD] for b in range(8)], axis=0)


def near_blocks(got):
    qs, ks, vs, ds = [gather_rows(got, a * LIVE2, LIVE2) for a in range(4)]
    for e in range(2):
        ak, bq = pack_kq(halves(ks, e), halves(qs, e))
        av, bd = pack_vd(halves(vs, e), halves(ds, e))
        parts = []
        for j in range(2):
            keys, rows = 256 * (j + 1), slice(256 * j, 256 * j + 256)
            mask = iota((keys, 256), 0) <= iota((keys, 256), 1) + 256 * j
            parts.append((ak[:keys], bq[rows], av[:keys], bd[rows], mask))
        yield parts


def near_forward_kernel(meta, got, own, mine, theirs):
    found = []
    for parts in near_blocks(got):
        lses, deltas = [], []
        for part in parts:
            top, total, delta, _, _ = forward_core(*part)
            lses.append(top + jnp.log(total))
            deltas.append(delta)
        found.append((to_rows(cat(lses)), to_rows(cat(deltas))))
    lse, delta = [cat([found[0][n], found[1][n]]) for n in range(2)]
    own[:, :128] = lse
    own[:, 128:] = delta
    sub, lane = iota((128, 128), 0), iota((128, 128), 1)
    spread = ((sub < 8) & (lane < 64) & (lane % 8 == sub)).astype(F32)
    diagonal = iota((8, 128), 0) == iota((8, 128), 1) // 8
    q, d = gather_rows(got, FAR_AT, 8), gather_rows(got, FAR_AT + 24, 8)
    qd = both(q, turn(d)), both(turn(q), d)
    blocks = []
    for e in range(2):
        live, shift = near_shift(meta, e)
        pick = (sub // HD == e) & (sub % HD // 8 == lane) & (sub % 8 == shift)
        pick = pick.astype(F32)
        merged = merge(
            [
                tuple(pltpu.roll(stat_rows(got, 2 + n), 120 * e, 1) for n in range(2)),
                (jnp.where(live, exact(lse, pick), NEG), exact(delta, pick)),
            ]
        )
        flat = [
            jnp.sum(jnp.where(diagonal, exact(x, spread), 0.0), axis=0, keepdims=True)
            for x in merged
        ]
        blocks.append(jnp.concatenate([qd[e], *flat, jnp.zeros((6, 128), F32)], axis=0))
    first = meta[SEG_AT] % 2 == 0
    mine[...] = jnp.where(first, blocks[0], blocks[1])
    theirs[...] = jnp.where(first, blocks[1], blocks[0])


def far_kernel(meta, kv, mine, pair, send, keep, back):
    first = meta[SEG_AT] % 2 == 0
    x, y = mine[...], pair[...]
    low, high = jnp.where(first, x, y), jnp.where(first, y, x)
    qd = jnp.concatenate([low[:LIVE2], high[:LIVE2]], axis=0)
    known = [both(low[64 + n : 65 + n], turn(high[64 + n : 65 + n])) for n in range(2)]
    ak, bq = pack_kq(kv[:, :HD], qd[:, :HD])
    av, bd = pack_vd(kv[:, HD:], qd[:, HD:])
    start = 64 * (meta[SEG_AT] - meta[SEG_AT] % 2)
    mask = iota((1024, 128), 0) <= iota((1024, 128), 1) + start
    top, total, delta3, p, dp = forward_core(ak, bq, av, bd, mask)
    lse3 = top + jnp.log(total)
    lse, delta = merge([tuple(known), (lse3, delta3)])
    at, qt, dk, dv = backward_core(p * jnp.exp(top - lse), dp, delta, ak, bq, av, bd)
    send[...] = both(fold(dk), fold(dv))
    aq = jnp.concatenate([at, qt], axis=0).T
    stats = (lse3, delta3, lse, delta)
    front = jnp.concatenate([aq[:LIVE2], *stats, jnp.zeros((4, 128), F32)], axis=0)
    rear = jnp.concatenate([aq[LIVE2:], *[turn(x) for x in stats], jnp.zeros((4, 128), F32)], axis=0)
    keep[...] = jnp.where(first, front, rear)
    back[...] = jnp.where(first, rear, front)


def by_head(meta, keep, back):
    first = meta[SEG_AT] % 2 == 0
    x, y = keep[...], back[...]
    return jnp.where(first, x, y), jnp.where(first, y, x)


def near_backward_kernel(meta, got, own, keep, back, out):
    far = by_head(meta, keep, back)
    sub, lane = iota((128, 128), 0), iota((128, 128), 1)
    diagonal = iota((8, 128), 0) == iota((8, 128), 1) // 8
    known = [stat_rows(got, n) for n in range(2)]
    third = [jnp.zeros((8, 128), F32), jnp.zeros((8, 128), F32)]
    covered = jnp.zeros((8, 128), jnp.bool_)
    l = iota((8, 128), 1)
    for e in range(2):
        live, shift = near_shift(meta, e)
        covered = covered | ((l // HD == e) & (l % 8 == shift) & live)
        place = (sub < 64) & (sub % 8 == lane % HD // 8) & (lane // HD == e)
        place = place.astype(F32)
        for n in range(2):
            x = jnp.where(diagonal, far[e][64 + n : 65 + n], 0.0)
            third[n] = third[n] + exact(x, place)
    lse, delta = merge(
        [
            tuple(known),
            (own[:, :128], own[:, 128:]),
            (jnp.where(covered, third[0], NEG), jnp.where(covered, third[1], 0.0)),
        ]
    )
    for n, x in enumerate((lse, delta)):
        rest = jnp.zeros((8, 128), F32)
        for e in range(2):
            tail = ((sub < 64) & (lane == LIVE3 * e + sub % 8)).astype(F32)
            rest = rest + exact(jnp.where(diagonal, far[e][66 + n : 67 + n], 0.0), tail)
        out[pl.ds(STAT_AT + n, 8, stride=MESSAGE), :] = x
        out[pl.ds(STAT_AT + 2 + n, 8, stride=MESSAGE), :] = rest
    ats, qts, dks, dvs = [], [], [], []
    for e, parts in enumerate(near_blocks(got)):
        results = []
        for j, (ak, bq, av, bd, mask) in enumerate(parts):
            at = slice(HD * e, HD * e + HD)
            lse_j = cat([lse[b : b + 1, at] for b in range(4 * j, 4 * j + 4)])
            delta_j = cat([delta[b : b + 1, at] for b in range(4 * j, 4 * j + 4)])
            p = jnp.exp(jnp.where(mask, nt(ak, bq), NEG) - lse_j)
            results.append(backward_core(p, nt(av, bd), delta_j, ak, bq, av, bd))
        ats.append(cat([results[0][0], results[1][0]]))
        qts.append(cat([results[0][1], results[1][1]]))
        for group, n in ((dks, 2), (dvs, 3)):
            x, y = results[0][n], results[1][n]
            group.append(jnp.concatenate([x + y[:256], y[256:]], axis=0))
    finals = (
        jnp.concatenate(ats, axis=0).T,
        jnp.concatenate(qts, axis=0).T,
        both(fold(dks[0]), fold(dks[1])),
        both(fold(dvs[0]), fold(dvs[1])),
    )
    for a, x in enumerate(finals):
        for b in range(8):
            at = MESSAGE * b + a * LIVE2
            out[at : at + LIVE2, :] = x[LIVE2 * b : LIVE2 * b + LIVE2]


def merge_kernel(meta, near, parts, keep, back, out):
    aq = by_head(meta, keep, back)
    kv = []
    for e in range(2):
        total = parts[64 * e : 64 * e + 64, :]
        for s in range(e + 2, 16, 2):
            total = total + parts[64 * s : 64 * s + 64, :]
        kv.append(total)
    aq = [x[:LIVE2] for x in aq]
    far = (
        both(aq[0], turn(aq[1])),
        both(turn(aq[0]), aq[1]),
        both(kv[0], turn(kv[1])),
        both(turn(kv[0]), kv[1]),
    )
    for b in range(8):
        base = MESSAGE * b
        out[base : base + FAR_AT, :] = near[base : base + FAR_AT, :]
        out[base + STAT_AT : base + MESSAGE, :] = near[base + STAT_AT : base + MESSAGE, :]
        for a, x in enumerate(far):
            out[base + FAR_AT + 8 * a : base + FAR_AT + 8 * a + 8, :] = x[8 * b : 8 * b + 8]


def local_kernel(meta, q, k, v, d, at_out, dq_out, dk_out, dv_out, panel, sems):
    fetch((q, k, v, d), panel, sems)
    mask = iota((ROWS, ROWS), 0) <= iota((ROWS, ROWS), 1)
    row = iota((1, ROWS), 1)

    def step(b, carry):
        arrive((q, k, v, d), panel, sems, b)
        qp, kp, vp, dp = [panel[block(a, b), :] for a in range(4)]
        res = []
        for e in range(2):
            ak, bq = pack_kq(halves(kp, e), halves(qp, e))
            av, bd = pack_vd(halves(vp, e), halves(dp, e))
            _, total, delta, p, w = forward_core(ak, bq, av, bd, mask)
            h = 2 * b + e
            live = (row % R2 == meta[h]) | (row % R3 == meta[HEADS + h])
            p = p * jnp.where(live, 0.0, 1.0 / total)
            res.append(backward_core(p, w, delta, ak, bq, av, bd))
        at_out[block(0, b), :] = jnp.concatenate([res[0][0], res[1][0]], axis=0).T
        dq_out[block(0, b), :] = jnp.concatenate([res[0][1], res[1][1]], axis=0).T
        dk_out[block(0, b), :] = both(fold(res[0][2]), fold(res[1][2]))
        dv_out[block(0, b), :] = both(fold(res[0][3]), fold(res[1][3]))
        return carry

    lax.fori_loop(0, 6, step, 0)


def close_kernel(
    meta, at1, dq1, dk1, dv1, live, weights, slopes, products, stats, got,
    at_out, dq_out, dk_out, dv_out, panel, sems, held, held_sem,
):
    coming = pltpu.make_async_copy(products, held, held_sem)
    coming.start()
    outs, local = (at_out, dq_out, dk_out, dv_out), (at1, dq1, dk1, dv1)
    first = iota((1, 128), 1) < 16
    far = [jnp.zeros((1, 128), F32), jnp.zeros((1, 128), F32)]
    scales, shifts = [], []
    for b in range(7):
        if b < 6:
            at = MESSAGE * b + STAT_AT
            lse, delta = got[at : at + 1, :], got[at + 1 : at + 2, :]
            for n in range(2):
                x = jnp.where(first, got[at + 2 + n : at + 3 + n, :], 0.0)
                far[n] = far[n] + pltpu.roll(x, 16 * b, 1)
        else:
            lse, delta = far
        scales.append(jnp.exp(stats[b : b + 1, :] - lse))
        shifts.append(delta - stats[8 + b : 9 + b, :])
    zero = jnp.zeros((1, 128), F32)
    table = jnp.concatenate([*scales, zero, *shifts, zero], axis=0).T
    low2, low3 = half_mask(LIVE2), half_mask(LIVE3)
    far_p, far_h = weights[6 * ROWS :, :], slopes[6 * ROWS :, :]
    copies = []
    for b in range(6):
        rows = []
        for n in range(2):
            keep = PAIR * (2 * b + n)
            rows.append((live[keep : keep + LIVE2, :], live[keep + LIVE2 : keep + PAIR, :]))
        scale = jnp.concatenate([table[:, b : b + 1], table[:, 6:7]], axis=0)
        shift = jnp.concatenate([table[:, 8 + b : 9 + b], table[:, 14:15]], axis=0)
        d = live_block(*rows[1], b) * scale
        q = live_block(*rows[0], b) * (scale * SCALE)
        d, q, t = [cat(split2(x)) for x in (d, q, q * (-shift))]
        own_p, own_h = weights[ROWS * b : ROWS * b + ROWS, :], slopes[ROWS * b : ROWS * b + ROWS, :]
        dense = [jnp.zeros((ROWS, 256), F32), jnp.zeros((ROWS, 256), F32)]
        for n in range(2):
            at = slice(128 * n, 128 * n + 128)
            p, h = cat([own_p[:, at], far_p[:, at]]), cat([own_h[:, at], far_h[:, at]])
            dense[0] = dense[0] + nn(h, q) + nn(p, t)
            dense[1] = dense[1] + nn(p, d)
        spread = [
            (
                jnp.where(low2, table[:LIVE2, n + b : n + b + 1], table[LIVE2:, n + b : n + b + 1]),
                jnp.where(
                    low3,
                    table[16 * b : 16 * b + 8, n + 6 : n + 7],
                    table[16 * b + 8 : 16 * b + 16, n + 6 : n + 7],
                ),
            )
            for n in (0, 8)
        ]
        for a in (2, 3, 0, 1):
            if b == 0 and a == 0:
                coming.wait()
            at = MESSAGE * b + LIVE2 * a
            near = got[at : at + LIVE2, :]
            at = MESSAGE * b + FAR_AT + LIVE3 * a
            far = got[at : at + LIVE3, :]
            base = ROWS * (6 * a + b)
            kept = local[a][ROWS * b : ROWS * b + ROWS, :]
            if a == 0:
                z = held[PAIR * b : PAIR * b + PAIR, :]
                near = near + spread[0][0] * z[:LIVE2]
                far = far + spread[0][1] * z[LIVE2:]
            elif a == 1:
                x, y = [held[PAIR * (6 * n + b) : PAIR * (6 * n + b + 1), :] for n in (1, 2)]
                near = near + spread[0][0] * (x[:LIVE2] - spread[1][0] * y[:LIVE2])
                far = far + spread[0][1] * (x[LIVE2:] - spread[1][1] * y[LIVE2:])
            else:
                x = dense[a - 2]
                kept = kept + (x[:, :128] + x[:, 128:])
            panel[base : base + ROWS, :] = kept
            for e in range(2):
                spot = pl.ds(base + meta[2 * b + e], LIVE2, stride=R2)
                panel[spot, :] = panel[spot, :] + jnp.where(low2 if e == 0 else ~low2, near, 0.0)
                spot = pl.ds(base + meta[HEADS + 2 * b + e], LIVE3, stride=R3)
                panel[spot, :] = panel[spot, :] + jnp.where(low3 if e == 0 else ~low3, far, 0.0)
            copies.append(
                pltpu.make_async_copy(
                    panel.at[block(a, b), :], outs[a].at[:, columns(b)], sems.at[6 * a + b]
                )
            )
            copies[-1].start()
    for copy in copies:
        copy.wait()


SMEM = pl.BlockSpec(memory_space=pltpu.SMEM)
HBM = pl.BlockSpec(memory_space=pltpu.HBM)
VMEM = pl.BlockSpec(memory_space=pltpu.VMEM)
PANEL = pltpu.VMEM((24 * ROWS, 128), F32)
COPIES = pltpu.SemaphoreType.DMA((24,))


def call(kernel, name, outs, args, flops, mib, scratch=(), hbm=(), out_spec=VMEM):
    return pl.pallas_call(
        kernel,
        name=name,
        out_shape=[jax.ShapeDtypeStruct(x, F32) if isinstance(x, tuple) else x for x in outs],
        in_specs=[HBM if i in hbm else VMEM if i else SMEM for i in range(len(args))],
        out_specs=out_spec if isinstance(out_spec, list) else [out_spec] * len(outs),
        scratch_shapes=list(scratch),
        compiler_params=pltpu.CompilerParams(vmem_limit_bytes=mib * 1024 * 1024),
        cost_estimate=pl.CostEstimate(flops=flops, bytes_accessed=100_000, transcendentals=0),
    )(*args)


def in_hbm(x):
    return pltpu.with_memory_space_constraint(x, pltpu.HBM)


def swap(x, axis):
    return lax.all_to_all(x, axis, 0, 0, tiled=True)


def swap_cores(x):
    return lax.ppermute(x, "seg", [(s, s ^ 1) for s in range(lax.axis_size("seg"))])


def body(q, k, v, d, offsets):
    place = jnp.stack([lax.axis_index("seg"), lax.axis_index("blk")]).astype(jnp.int32)
    meta = jnp.concatenate([offsets.reshape(-1), place])
    rows = tuple(in_hbm(x) for x in (q, k, v, d))
    given = (1, 2, 3, 4)
    message, pair, far = (8 * MESSAGE, 128), (PAIR, 128), (1024, 128)
    send, live = call(
        open_kernel,
        "open",
        [pltpu.HBM(message, F32), (12 * PAIR, 128)],
        (in_hbm(offsets), *rows),
        10**8,
        16,
        [
            PANEL,
            COPIES,
            pltpu.VMEM(message, F32),
            pltpu.SemaphoreType.DMA((12,)),
            pltpu.SMEM((2, HEADS), jnp.int32),
            pltpu.SemaphoreType.DMA,
        ],
        (0, *given),
        [HBM, VMEM],
    )
    got = swap(send, "blk")
    local = call(
        local_kernel,
        "local",
        [(6 * ROWS, 128)] * 4,
        (meta, *rows),
        10**8,
        24,
        [PANEL, COPIES],
        given,
    )
    got, *local = lax.optimization_barrier((got, *local))
    (keys,) = call(
        spread_kernel,
        "spread",
        [pltpu.HBM(far, F32)],
        (meta, got),
        10**8,
        8,
        [pltpu.VMEM((2, 64, 128), F32), pltpu.SemaphoreType.DMA((16,))],
        out_spec=HBM,
    )
    all_keys = swap(keys, "seg")
    own, mine, theirs = call(
        near_forward_kernel, "near_forward", [(8, 256), pair, pair], (meta, got), 10**8, 24
    )
    rest = call(
        live_kernel,
        "live",
        [pltpu.HBM((7 * ROWS, 256), BF)] * 2 + [pltpu.HBM((18 * PAIR, 128), F32), (16, 128)],
        (meta, rows[1], rows[2], live),
        10**8,
        16,
        [
            pltpu.VMEM((12 * ROWS, 128), F32),
            pltpu.SemaphoreType.DMA((12,)),
            pltpu.VMEM((2, 7 * ROWS, 256), BF),
            pltpu.VMEM((18 * PAIR, 128), F32),
            pltpu.SemaphoreType.DMA((15,)),
        ],
        (1, 2),
        [HBM] * 3 + [VMEM],
    )
    all_keys, *rest = lax.optimization_barrier((all_keys, *rest))
    rest[2] = in_hbm(rest[2])
    partner = swap_cores(theirs)
    parts, keep, back = call(
        far_kernel, "far", [far, pair, pair], (meta, all_keys, mine, partner), 10**8, 24
    )
    sums = swap(parts, "seg")
    back = swap_cores(back)
    (near,) = call(
        near_backward_kernel,
        "near_backward",
        [message],
        (meta, got, own, keep, back),
        10**8,
        24,
    )
    (reply,) = call(merge_kernel, "merge", [message], (meta, near, sums, keep, back), 10**8, 12)
    home = swap(reply, "blk")
    return tuple(
        call(
            close_kernel,
            "close",
            [(ROWS, HEADS * HD)] * 4,
            (meta, *local, live, *rest, home),
            10**8,
            16,
            [PANEL, COPIES, pltpu.VMEM((18 * PAIR, 128), F32), pltpu.SemaphoreType.DMA],
            (8,),
            HBM,
        )
    )


def solution(mesh):
    rows = P(ALL, None)
    return jax.shard_map(
        body,
        mesh=mesh,
        in_specs=(rows, rows, rows, rows, P()),
        out_specs=(rows, rows, rows, rows),
        check_vma=False,
    )
```

```python
import functools

import jax
import jax.numpy as jnp
from jax import lax
from jax.experimental import pallas as pl
from jax.experimental.pallas import tpu as pltpu
from jax.sharding import PartitionSpec as P

HEADS = 12
HD = 64
ROWS = 256
LIVE2 = 64
LIVE3 = 8
R2 = 4
R3 = 32
NEG = -1e30
SCALE = HD**-0.5
BF = jnp.bfloat16
F32 = jnp.float32
ALL = ("seg", "blk")
SEG_AT, BLK_AT = 24, 25
FAR_AT, STAT_AT, MESSAGE = 256, 288, 296
PAIR = 72
ROW_AT = 14 * ROWS


def nt(a, b):
    return lax.dot_general(a, b, (((1,), (1,)), ((), ())), preferred_element_type=F32)


def nn(a, b):
    return lax.dot_general(a, b, (((1,), (0,)), ((), ())), preferred_element_type=F32)


def tn(a, b):
    return lax.dot_general(a, b, (((0,), (0,)), ((), ())), preferred_element_type=F32)


def exact(a, b, dims=((1,), (0,))):
    return lax.dot_general(
        a, b, (dims, ((), ())), preferred_element_type=F32, precision=lax.Precision.HIGHEST
    )


def iota(shape, axis):
    return lax.broadcasted_iota(jnp.int32, shape, axis)


def split2(x):
    first = x.astype(BF)
    return first, (x - first.astype(F32)).astype(BF)


def split3(x):
    first = x.astype(BF)
    rest = x - first.astype(F32)
    second = rest.astype(BF)
    return first, second, (rest - second.astype(F32)).astype(BF)


def cat(parts):
    return jnp.concatenate(parts, axis=1)


def pack_kq(k, q):
    k0, k1, k2 = split3(k)
    q0, q1, q2 = split3(q * SCALE)
    return cat([k0, k1, k0, k1, k0, k2]), cat([q0, q1, q1, q0, q2, q0])


def pack_vd(v, d):
    v0, v1 = split2(v)
    d0, d1 = split2(d)
    return cat([v0, v1, v0, v1]), cat([d0, d1, d1, d0])


def forward_core(ak, bq, av, bd, mask):
    s = jnp.where(mask, nt(ak, bq), NEG)
    dp = nt(av, bd)
    top = jnp.max(s, axis=0, keepdims=True)
    p = jnp.exp(s - top)
    total = jnp.sum(p, axis=0, keepdims=True)
    cross = jnp.sum(p * dp, axis=0, keepdims=True)
    return top, total, cross / total, p, dp


def backward_core(p, dp, delta, ak, bq, av, bd):
    g = p * (dp - delta)
    p0, p1 = split2(p)
    g0, g1 = split2(g)
    d01, q01, v01, k01 = bd[:, :128], bq[:, :128], av[:, :128], ak[:, :128]
    dv = nn(p0, d01) + nn(p1, d01)
    dk = nn(g0, q01) + nn(g1, q01)
    at = tn(v01, p0) + tn(v01, p1)
    qt = tn(k01, g0) + tn(k01, g1)
    return at[:HD] + at[HD:], (qt[:HD] + qt[HD:]) * SCALE, dk, dv


def fold(x):
    return x + pltpu.roll(x, HD, 1)


def half_mask(rows):
    return iota((rows, 128), 1) < HD


def both(a, b):
    return jnp.where(half_mask(a.shape[0]), a, b)


def merge(levels):
    top = functools.reduce(jnp.maximum, [lse for lse, _ in levels])
    weights = [jnp.exp(lse - top) for lse, _ in levels]
    total = functools.reduce(jnp.add, weights)
    delta = functools.reduce(jnp.add, [w * d for w, (_, d) in zip(weights, levels)])
    return top + jnp.log(total), delta / total


def block(a, b):
    at = ROWS * (6 * a + b)
    return pl.ds(at if isinstance(b, int) else pl.multiple_of(at, ROWS), ROWS)


def columns(b):
    return pl.ds(128 * b if isinstance(b, int) else pl.multiple_of(128 * b, 128), 128)


def inward(refs, panel, sems, b):
    return [
        pltpu.make_async_copy(
            ref.at[:, columns(b)], panel.at[block(a, b), :], sems.at[6 * a + b]
        )
        for a, ref in enumerate(refs)
    ]


def fetch(refs, panel, sems):
    for b in range(6):
        for copy in inward(refs, panel, sems, b):
            copy.start()


def arrive(refs, panel, sems, b):
    for copy in inward(refs, panel, sems, b):
        copy.wait()


def near_positions(meta, b):
    lane = iota((1, 128), 1)
    return R2 * (lane % LIVE2) + jnp.where(lane < LIVE2, meta[2 * b], meta[2 * b + 1])


def far_positions(meta, alone):
    lane = iota((1, 128), 1)
    spot = jnp.full((1, 128), -1, jnp.int32)
    for h in range(HEADS):
        near, far = meta[h], meta[HEADS + h]
        start = jnp.where(far % R2 == near, -1, far) if alone else far
        here = lane // LIVE3 == h
        spot = jnp.where(here & (start >= 0), start + R3 * (lane % LIVE3), spot)
    return spot


def pieces(x, count):
    out = []
    for _ in range(count - 1):
        out.append(x.astype(BF).astype(F32))
        x = x - out[-1]
    return [*out, x]


def place(near, far, b):
    def apart(x):
        low = half_mask(x.shape[0])
        return [jnp.where(low, x, 0.0), jnp.where(low, 0.0, x)]

    rows = [x.astype(BF) for x in apart(near)]
    if b:
        rows.append(jnp.zeros((16 * b, 128), BF))
    rows.append(jnp.concatenate(apart(far), axis=0).astype(BF))
    rows.append(jnp.zeros((112 - 16 * b, 128), BF))
    return jnp.concatenate(rows, axis=0)


def live_pieces(near, far, b, count):
    return [place(x, y, b) for x, y in zip(pieces(near, count), pieces(far, count))]


def live_products(k, v, q, d, b):
    k0, k1, k2 = split3(k)
    q0, q1, q2 = live_pieces(q[0] * SCALE, q[1] * SCALE, b, 3)
    v0, v1 = split2(v)
    d0, d1 = live_pieces(*d, b, 2)
    s = nt(cat([k0, k1, k0, k1, k0, k2]), cat([q0, q1, q1, q0, q2, q0]))
    return s, nt(cat([v0, v1, v0, v1]), cat([d0, d1, d1, d0]))


def live_forward(s, dp, spot):
    s = jnp.where(iota((ROWS, 128), 0) <= spot, s, NEG)
    top = jnp.max(s, axis=0, keepdims=True)
    p = jnp.exp(s - top)
    total = jnp.sum(p, axis=0, keepdims=True)
    delta = jnp.sum(p * dp, axis=0, keepdims=True) / total
    return top + jnp.log(total), delta, p / total


def halves(x, e):
    return x[:, HD * e : HD * e + HD]


def turn(x):
    return pltpu.roll(x, HD, 1)


class Flat:
    def __init__(self, ref):
        self.ref = ref

    def __getitem__(self, i):
        return self.ref[i // HEADS, i % HEADS]


def open_kernel(offsets, q, k, v, d, out, live, panel, sems, send, out_sems, shifts, shift_sem):
    shifting = pltpu.make_async_copy(offsets, shifts, shift_sem)
    shifting.start()
    fetch((q, k, v, d), panel, sems)
    shifting.wait()
    meta = Flat(shifts)
    copies, rows = [], []

    def leave(at, count):
        at = pl.ds(at, count)
        copies.append(pltpu.make_async_copy(send.at[at, :], out.at[at, :], out_sems.at[len(copies)]))
        copies[-1].start()

    for b in range(6):
        arrive((q, k, v, d), panel, sems, b)
        at = MESSAGE * b
        found = []
        for a in range(4):
            base = ROWS * (6 * a + b)
            near = both(
                panel[pl.ds(base + meta[2 * b], LIVE2, stride=R2), :],
                panel[pl.ds(base + meta[2 * b + 1], LIVE2, stride=R2), :],
            )
            far = both(
                panel[pl.ds(base + meta[HEADS + 2 * b], LIVE3, stride=R3), :],
                panel[pl.ds(base + meta[HEADS + 2 * b + 1], LIVE3, stride=R3), :],
            )
            send[at + LIVE2 * a : at + LIVE2 * a + LIVE2, :] = near
            send[at + FAR_AT + LIVE3 * a : at + FAR_AT + LIVE3 * a + LIVE3, :] = far
            found.append((near, far))
        leave(at, STAT_AT)
        for n, (near, far) in enumerate((found[0], found[3])):
            keep = PAIR * (2 * b + n)
            live[keep : keep + LIVE2, :] = near
            live[keep + LIVE2 : keep + PAIR, :] = far
        rows.append((found[0], found[3]))
    far_s = far_dp = jnp.zeros((ROWS, 128), F32)
    known = []
    for b in range(6):
        s, dp = live_products(
            panel[block(1, b), :],
            panel[block(2, b), :],
            *rows[b],
            b,
        )
        far_s, far_dp = far_s + s[:, 128:], far_dp + dp[:, 128:]
        known.append(live_forward(s[:, :128], dp[:, :128], near_positions(meta, b))[:2])
    far = live_forward(far_s, far_dp, far_positions(meta, False))[:2]
    for b in range(6):
        at = MESSAGE * b + STAT_AT
        turned = [pltpu.roll(x, (128 - 16 * b) % 128, 1) for x in far]
        send[at : at + 8, :] = jnp.concatenate([*known[b], *turned, jnp.zeros((4, 128), F32)], axis=0)
        leave(at, 8)
    for copy in copies:
        copy.wait()


def live_kernel(meta, k, v, live, weights, stats, panel, sems, kept, out_sems):
    fetch((k, v), panel, sems)
    stats[...] = jnp.zeros_like(stats)
    far_s = far_dp = jnp.zeros((ROWS, 128), F32)
    copies = []

    def record(n, s, dp, spot):
        lse, delta, p = live_forward(s, dp, spot)
        pair = cat(split2(p)), cat(split2(p * (dp - delta)))
        for m, x in enumerate(pair):
            at = pl.ds(ROWS * (7 * m + n), ROWS)
            kept[at, :] = x
            copies.append(pltpu.make_async_copy(kept.at[at, :], weights.at[at, :], out_sems.at[7 * m + n]))
            copies[-1].start()
        stats[n : n + 1, :] = lse
        stats[8 + n : 9 + n, :] = delta
        return pair

    def products(b, p, h):
        kb, vb = cat(split2(panel[block(0, b), :] * SCALE)), cat(split2(panel[block(1, b), :]))
        both_sides = tn(p, cat([vb, kb]))
        for n, x in enumerate((both_sides[:, :256], tn(h, kb), both_sides[:, 256:])):
            yield ROW_AT + 80 * (6 * n + b), x[:128, :128] + x[:128, 128:] + x[128:, :128] + x[128:, 128:]

    for b in range(6):
        arrive((k, v), panel, sems, b)
    for b in range(6):
        rows = []
        for n in range(2):
            keep = PAIR * (2 * b + n)
            rows.append((live[keep : keep + LIVE2, :], live[keep + LIVE2 : keep + PAIR, :]))
        s, dp = live_products(
            panel[block(0, b), :],
            panel[block(1, b), :],
            *rows,
            b,
        )
        far_s, far_dp = far_s + s[:, 128:], far_dp + dp[:, 128:]
        p, h = record(b, s[:, :128], dp[:, :128], near_positions(meta, b))
        for at, x in products(b, p, h):
            kept[at : at + LIVE2, :] = cat(split2(both(x[:LIVE2], x[LIVE2:])))
    p, h = record(6, far_s, far_dp, far_positions(meta, True))
    for b in range(6):
        for at, x in products(b, p, h):
            low, high = x[16 * b : 16 * b + 8], x[16 * b + 8 : 16 * b + 16]
            x = jnp.concatenate([both(low, high), jnp.zeros((8, 128), F32)], axis=0)
            kept[at + LIVE2 : at + 80, :] = cat(split2(x))
    at = pl.ds(ROW_AT, 18 * 80)
    copies.append(pltpu.make_async_copy(kept.at[at, :], weights.at[at, :], out_sems.at[14]))
    copies[-1].start()
    for copy in copies:
        copy.wait()


def gather_rows(ref, at, count):
    return jnp.concatenate(
        [ref[MESSAGE * b + at : MESSAGE * b + at + count, :] for b in range(8)], axis=0
    )


def stat_rows(ref, n):
    return ref[pl.ds(STAT_AT + n, 8, stride=MESSAGE), :]


def spread_kernel(meta, got, out, kv, sems):
    k, v = gather_rows(got, FAR_AT + 8, 8), gather_rows(got, FAR_AT + 16, 8)
    kv[0] = both(k, turn(v))
    kv[1] = both(turn(k), v)
    copies = [
        pltpu.make_async_copy(kv.at[s % 2], out.at[pl.ds(64 * s, 64), :], sems.at[s])
        for s in range(16)
    ]
    for copy in copies:
        copy.start()
    for copy in copies:
        copy.wait()


def near_shift(meta, e):
    h = jnp.minimum(2 * meta[BLK_AT] + e, HEADS - 1)
    live = meta[HEADS + h] % R2 == meta[h]
    return live, meta[HEADS + h] // R2


def to_rows(x):
    return jnp.concatenate([x[:, HD * b : HD * b + HD] for b in range(8)], axis=0)


def near_blocks(got):
    qs, ks, vs, ds = [gather_rows(got, a * LIVE2, LIVE2) for a in range(4)]
    for e in range(2):
        ak, bq = pack_kq(halves(ks, e), halves(qs, e))
        av, bd = pack_vd(halves(vs, e), halves(ds, e))
        parts = []
        for j in range(2):
            keys, rows = 256 * (j + 1), slice(256 * j, 256 * j + 256)
            mask = iota((keys, 256), 0) <= iota((keys, 256), 1) + 256 * j
            parts.append((ak[:keys], bq[rows], av[:keys], bd[rows], mask))
        yield parts


def near_forward_kernel(meta, got, own, mine, theirs):
    found = []
    for parts in near_blocks(got):
        lses, deltas = [], []
        for part in parts:
            top, total, delta, _, _ = forward_core(*part)
            lses.append(top + jnp.log(total))
            deltas.append(delta)
        found.append((to_rows(cat(lses)), to_rows(cat(deltas))))
    lse, delta = [cat([found[0][n], found[1][n]]) for n in range(2)]
    own[:, :128] = lse
    own[:, 128:] = delta
    sub, lane = iota((128, 128), 0), iota((128, 128), 1)
    spread = ((sub < 8) & (lane < 64) & (lane % 8 == sub)).astype(F32)
    diagonal = iota((8, 128), 0) == iota((8, 128), 1) // 8
    q, d = gather_rows(got, FAR_AT, 8), gather_rows(got, FAR_AT + 24, 8)
    qd = both(q, turn(d)), both(turn(q), d)
    blocks = []
    for e in range(2):
        live, shift = near_shift(meta, e)
        pick = (sub // HD == e) & (sub % HD // 8 == lane) & (sub % 8 == shift)
        pick = pick.astype(F32)
        merged = merge(
            [
                tuple(pltpu.roll(stat_rows(got, 2 + n), 120 * e, 1) for n in range(2)),
                (jnp.where(live, exact(lse, pick), NEG), exact(delta, pick)),
            ]
        )
        flat = [
            jnp.sum(jnp.where(diagonal, exact(x, spread), 0.0), axis=0, keepdims=True)
            for x in merged
        ]
        blocks.append(jnp.concatenate([qd[e], *flat, jnp.zeros((6, 128), F32)], axis=0))
    first = meta[SEG_AT] % 2 == 0
    mine[...] = jnp.where(first, blocks[0], blocks[1])
    theirs[...] = jnp.where(first, blocks[1], blocks[0])


def far_kernel(meta, kv, mine, pair, send, keep, back, parts, sem):
    first = meta[SEG_AT] % 2 == 0
    x, y = mine[...], pair[...]
    low, high = jnp.where(first, x, y), jnp.where(first, y, x)
    qd = jnp.concatenate([low[:LIVE2], high[:LIVE2]], axis=0)
    known = [both(low[64 + n : 65 + n], turn(high[64 + n : 65 + n])) for n in range(2)]
    ak, bq = pack_kq(kv[:, :HD], qd[:, :HD])
    av, bd = pack_vd(kv[:, HD:], qd[:, HD:])
    start = 64 * (meta[SEG_AT] - meta[SEG_AT] % 2)
    mask = iota((1024, 128), 0) <= iota((1024, 128), 1) + start
    top, total, delta3, p, dp = forward_core(ak, bq, av, bd, mask)
    lse3 = top + jnp.log(total)
    lse, delta = merge([tuple(known), (lse3, delta3)])
    at, qt, dk, dv = backward_core(p * jnp.exp(top - lse), dp, delta, ak, bq, av, bd)
    parts[...] = both(fold(dk), fold(dv))
    leaving = pltpu.make_async_copy(parts, send, sem)
    leaving.start()
    aq = jnp.concatenate([at, qt], axis=0).T
    stats = (lse3, delta3, lse, delta)
    front = jnp.concatenate([aq[:LIVE2], *stats, jnp.zeros((4, 128), F32)], axis=0)
    rear = jnp.concatenate([aq[LIVE2:], *[turn(x) for x in stats], jnp.zeros((4, 128), F32)], axis=0)
    keep[...] = jnp.where(first, front, rear)
    back[...] = jnp.where(first, rear, front)
    leaving.wait()


def by_head(meta, keep, back):
    first = meta[SEG_AT] % 2 == 0
    x, y = keep[...], back[...]
    return jnp.where(first, x, y), jnp.where(first, y, x)


def near_backward_kernel(meta, got, own, keep, back, out):
    far = by_head(meta, keep, back)
    sub, lane = iota((128, 128), 0), iota((128, 128), 1)
    diagonal = iota((8, 128), 0) == iota((8, 128), 1) // 8
    known = [stat_rows(got, n) for n in range(2)]
    third = [jnp.zeros((8, 128), F32), jnp.zeros((8, 128), F32)]
    covered = jnp.zeros((8, 128), jnp.bool_)
    l = iota((8, 128), 1)
    for e in range(2):
        live, shift = near_shift(meta, e)
        covered = covered | ((l // HD == e) & (l % 8 == shift) & live)
        place = (sub < 64) & (sub % 8 == lane % HD // 8) & (lane // HD == e)
        place = place.astype(F32)
        for n in range(2):
            x = jnp.where(diagonal, far[e][64 + n : 65 + n], 0.0)
            third[n] = third[n] + exact(x, place)
    lse, delta = merge(
        [
            tuple(known),
            (own[:, :128], own[:, 128:]),
            (jnp.where(covered, third[0], NEG), jnp.where(covered, third[1], 0.0)),
        ]
    )
    for n, x in enumerate((lse, delta)):
        rest = jnp.zeros((8, 128), F32)
        for e in range(2):
            tail = ((sub < 64) & (lane == LIVE3 * e + sub % 8)).astype(F32)
            rest = rest + exact(jnp.where(diagonal, far[e][66 + n : 67 + n], 0.0), tail)
        out[pl.ds(STAT_AT + n, 8, stride=MESSAGE), :] = x
        out[pl.ds(STAT_AT + 2 + n, 8, stride=MESSAGE), :] = rest
    ats, qts, dks, dvs = [], [], [], []
    for e, parts in enumerate(near_blocks(got)):
        results = []
        for j, (ak, bq, av, bd, mask) in enumerate(parts):
            at = slice(HD * e, HD * e + HD)
            lse_j = cat([lse[b : b + 1, at] for b in range(4 * j, 4 * j + 4)])
            delta_j = cat([delta[b : b + 1, at] for b in range(4 * j, 4 * j + 4)])
            p = jnp.exp(jnp.where(mask, nt(ak, bq), NEG) - lse_j)
            results.append(backward_core(p, nt(av, bd), delta_j, ak, bq, av, bd))
        ats.append(cat([results[0][0], results[1][0]]))
        qts.append(cat([results[0][1], results[1][1]]))
        for group, n in ((dks, 2), (dvs, 3)):
            x, y = results[0][n], results[1][n]
            group.append(jnp.concatenate([x + y[:256], y[256:]], axis=0))
    finals = (
        jnp.concatenate(ats, axis=0).T,
        jnp.concatenate(qts, axis=0).T,
        both(fold(dks[0]), fold(dks[1])),
        both(fold(dvs[0]), fold(dvs[1])),
    )
    for a, x in enumerate(finals):
        for b in range(8):
            at = MESSAGE * b + a * LIVE2
            out[at : at + LIVE2, :] = x[LIVE2 * b : LIVE2 * b + LIVE2]


def merge_kernel(meta, near, parts, keep, back, out):
    aq = by_head(meta, keep, back)
    kv = []
    for e in range(2):
        total = parts[64 * e : 64 * e + 64, :]
        for s in range(e + 2, 16, 2):
            total = total + parts[64 * s : 64 * s + 64, :]
        kv.append(total)
    aq = [x[:LIVE2] for x in aq]
    far = (
        both(aq[0], turn(aq[1])),
        both(turn(aq[0]), aq[1]),
        both(kv[0], turn(kv[1])),
        both(turn(kv[0]), kv[1]),
    )
    for b in range(8):
        base = MESSAGE * b
        out[base : base + FAR_AT, :] = near[base : base + FAR_AT, :]
        out[base + STAT_AT : base + MESSAGE, :] = near[base + STAT_AT : base + MESSAGE, :]
        for a, x in enumerate(far):
            out[base + FAR_AT + 8 * a : base + FAR_AT + 8 * a + 8, :] = x[8 * b : 8 * b + 8]


def local_kernel(meta, q, k, v, d, at_out, dq_out, dk_out, dv_out, panel, sems):
    fetch((q, k, v, d), panel, sems)
    mask = iota((ROWS, ROWS), 0) <= iota((ROWS, ROWS), 1)
    row = iota((1, ROWS), 1)

    def step(b, carry):
        arrive((q, k, v, d), panel, sems, b)
        qp, kp, vp, dp = [panel[block(a, b), :] for a in range(4)]
        res = []
        for e in range(2):
            ak, bq = pack_kq(halves(kp, e), halves(qp, e))
            av, bd = pack_vd(halves(vp, e), halves(dp, e))
            _, total, delta, p, w = forward_core(ak, bq, av, bd, mask)
            h = 2 * b + e
            live = (row % R2 == meta[h]) | (row % R3 == meta[HEADS + h])
            p = p * jnp.where(live, 0.0, 1.0 / total)
            res.append(backward_core(p, w, delta, ak, bq, av, bd))
        at_out[block(0, b), :] = jnp.concatenate([res[0][0], res[1][0]], axis=0).T
        dq_out[block(0, b), :] = jnp.concatenate([res[0][1], res[1][1]], axis=0).T
        dk_out[block(0, b), :] = both(fold(res[0][2]), fold(res[1][2]))
        dv_out[block(0, b), :] = both(fold(res[0][3]), fold(res[1][3]))
        return carry

    lax.fori_loop(0, 6, step, 0)


def close_kernel(
    meta, at1, dq1, dk1, dv1, live, weights, stats, got,
    at_out, dq_out, dk_out, dv_out, panel, sems,
):
    outs, local = (at_out, dq_out, dk_out, dv_out), (at1, dq1, dk1, dv1)

    def products(n):
        x = weights[ROW_AT + 80 * n : ROW_AT + 80 * n + 80, :].astype(F32)
        return (x[:, :128] + x[:, 128:])[:PAIR]

    first = iota((1, 128), 1) < 16
    far = [jnp.zeros((1, 128), F32), jnp.zeros((1, 128), F32)]
    scales, shifts = [], []
    for b in range(7):
        if b < 6:
            at = MESSAGE * b + STAT_AT
            lse, delta = got[at : at + 1, :], got[at + 1 : at + 2, :]
            for n in range(2):
                x = jnp.where(first, got[at + 2 + n : at + 3 + n, :], 0.0)
                far[n] = far[n] + pltpu.roll(x, 16 * b, 1)
        else:
            lse, delta = far
        scales.append(jnp.exp(stats[b : b + 1, :] - lse))
        shifts.append(delta - stats[8 + b : 9 + b, :])
    zero = jnp.zeros((1, 128), F32)
    table = jnp.concatenate([*scales, zero, *shifts, zero], axis=0).T
    low2, low3 = half_mask(LIVE2), half_mask(LIVE3)
    far_p, far_h = weights[6 * ROWS : 7 * ROWS, :], weights[13 * ROWS : ROW_AT, :]
    copies, spreads = [], []

    def finish(a, b, near, far, kept):
        base = ROWS * (6 * a + b)
        panel[base : base + ROWS, :] = kept
        for e in range(2):
            spot = pl.ds(base + meta[2 * b + e], LIVE2, stride=R2)
            panel[spot, :] = panel[spot, :] + jnp.where(low2 if e == 0 else ~low2, near, 0.0)
            spot = pl.ds(base + meta[HEADS + 2 * b + e], LIVE3, stride=R3)
            panel[spot, :] = panel[spot, :] + jnp.where(low3 if e == 0 else ~low3, far, 0.0)
        copies.append(
            pltpu.make_async_copy(
                panel.at[block(a, b), :], outs[a].at[:, columns(b)], sems.at[6 * a + b]
            )
        )
        copies[-1].start()

    def arrived(a, b):
        near, far = MESSAGE * b + LIVE2 * a, MESSAGE * b + FAR_AT + LIVE3 * a
        return got[near : near + LIVE2, :], got[far : far + LIVE3, :]

    for b in range(6):
        spread = [
            (
                jnp.where(low2, table[:LIVE2, n + b : n + b + 1], table[LIVE2:, n + b : n + b + 1]),
                jnp.where(
                    low3,
                    table[16 * b : 16 * b + 8, n + 6 : n + 7],
                    table[16 * b + 8 : 16 * b + 16, n + 6 : n + 7],
                ),
            )
            for n in (0, 8)
        ]
        spreads.append(spread)
        z, x, y = products(b), products(6 + b), products(12 + b)
        for a in range(2):
            near, far = arrived(a, b)
            if a == 0:
                near, far = near + spread[0][0] * z[:LIVE2], far + spread[0][1] * z[LIVE2:]
            else:
                near = near + spread[0][0] * (x[:LIVE2] - spread[1][0] * y[:LIVE2])
                far = far + spread[0][1] * (x[LIVE2:] - spread[1][1] * y[LIVE2:])
            finish(a, b, near, far, local[a][ROWS * b : ROWS * b + ROWS, :])
    for b in range(6):
        rows = []
        for n in range(2):
            keep = PAIR * (2 * b + n)
            rows.append((live[keep : keep + LIVE2, :], live[keep + LIVE2 : keep + PAIR, :]))
        d = [x * w for x, w in zip(rows[1], spreads[b][0])]
        q = [x * (w * SCALE) for x, w in zip(rows[0], spreads[b][0])]
        t = [-x * w for x, w in zip(q, spreads[b][1])]
        d, q, t = [cat(live_pieces(*x, b, 2)) for x in (d, q, t)]
        own_p, own_h = [weights[ROWS * n : ROWS * n + ROWS, :] for n in (b, 7 + b)]
        dense = [jnp.zeros((ROWS, 256), F32), jnp.zeros((ROWS, 256), F32)]
        for n in range(2):
            at = slice(128 * n, 128 * n + 128)
            p, h = cat([own_p[:, at], far_p[:, at]]), cat([own_h[:, at], far_h[:, at]])
            dense[0] = dense[0] + nn(h, q) + nn(p, t)
            dense[1] = dense[1] + nn(p, d)
        for a, x in zip((2, 3), dense):
            kept = local[a][ROWS * b : ROWS * b + ROWS, :] + (x[:, :128] + x[:, 128:])
            finish(a, b, *arrived(a, b), kept)
    for copy in copies:
        copy.wait()


SMEM = pl.BlockSpec(memory_space=pltpu.SMEM)
HBM = pl.BlockSpec(memory_space=pltpu.HBM)
VMEM = pl.BlockSpec(memory_space=pltpu.VMEM)
PANEL = pltpu.VMEM((24 * ROWS, 128), F32)
COPIES = pltpu.SemaphoreType.DMA((24,))


def call(kernel, name, outs, args, flops, mib, scratch=(), hbm=(), out_spec=VMEM):
    return pl.pallas_call(
        kernel,
        name=name,
        out_shape=[jax.ShapeDtypeStruct(x, F32) if isinstance(x, tuple) else x for x in outs],
        in_specs=[HBM if i in hbm else VMEM if i else SMEM for i in range(len(args))],
        out_specs=out_spec if isinstance(out_spec, list) else [out_spec] * len(outs),
        scratch_shapes=list(scratch),
        compiler_params=pltpu.CompilerParams(vmem_limit_bytes=mib * 1024 * 1024),
        cost_estimate=pl.CostEstimate(flops=flops, bytes_accessed=100_000, transcendentals=0),
    )(*args)


def in_hbm(x):
    return pltpu.with_memory_space_constraint(x, pltpu.HBM)


def swap(x, axis):
    return lax.all_to_all(x, axis, 0, 0, tiled=True)


def swap_cores(x):
    return lax.ppermute(x, "seg", [(s, s ^ 1) for s in range(lax.axis_size("seg"))])


def body(q, k, v, d, offsets):
    place = jnp.stack([lax.axis_index("seg"), lax.axis_index("blk")]).astype(jnp.int32)
    meta = jnp.concatenate([offsets.reshape(-1), place])
    rows = tuple(in_hbm(x) for x in (q, k, v, d))
    given = (1, 2, 3, 4)
    message, pair, far = (8 * MESSAGE, 128), (PAIR, 128), (1024, 128)
    send, live = call(
        open_kernel,
        "open",
        [pltpu.HBM(message, F32), (12 * PAIR, 128)],
        (in_hbm(offsets), *rows),
        10**8,
        16,
        [
            PANEL,
            COPIES,
            pltpu.VMEM(message, F32),
            pltpu.SemaphoreType.DMA((12,)),
            pltpu.SMEM((2, HEADS), jnp.int32),
            pltpu.SemaphoreType.DMA,
        ],
        (0, *given),
        [HBM, VMEM],
    )
    got = swap(send, "blk")
    local = call(
        local_kernel,
        "local",
        [(6 * ROWS, 128)] * 4,
        (meta, *rows),
        10**8,
        24,
        [PANEL, COPIES],
        given,
    )
    got, *local = lax.optimization_barrier((got, *local))
    (keys,) = call(
        spread_kernel,
        "spread",
        [pltpu.HBM(far, F32)],
        (meta, got),
        10**8,
        8,
        [pltpu.VMEM((2, 64, 128), F32), pltpu.SemaphoreType.DMA((16,))],
        out_spec=HBM,
    )
    all_keys = swap(keys, "seg")
    own, mine, theirs = call(
        near_forward_kernel, "near_forward", [(8, 256), pair, pair], (meta, got), 10**8, 24
    )
    rest = call(
        live_kernel,
        "live",
        [pltpu.HBM((ROW_AT + 18 * 80, 256), BF), (16, 128)],
        (meta, rows[1], rows[2], live),
        10**8,
        16,
        [
            pltpu.VMEM((12 * ROWS, 128), F32),
            pltpu.SemaphoreType.DMA((12,)),
            pltpu.VMEM((ROW_AT + 18 * 80, 256), BF),
            pltpu.SemaphoreType.DMA((15,)),
        ],
        (1, 2),
        [HBM, VMEM],
    )
    all_keys, *rest = lax.optimization_barrier((all_keys, *rest))
    partner = swap_cores(theirs)
    parts, keep, back = call(
        far_kernel,
        "far",
        [pltpu.HBM(far, F32), pair, pair],
        (meta, all_keys, mine, partner),
        10**8,
        24,
        [pltpu.VMEM(far, F32), pltpu.SemaphoreType.DMA],
        out_spec=[HBM, VMEM, VMEM],
    )
    sums = swap(parts, "seg")
    back = swap_cores(back)
    (near,) = call(
        near_backward_kernel,
        "near_backward",
        [message],
        (meta, got, own, keep, back),
        10**8,
        24,
    )
    (reply,) = call(merge_kernel, "merge", [message], (meta, near, sums, keep, back), 2 * 10**10, 12)
    home = swap(reply, "blk")
    return tuple(
        call(
            close_kernel,
            "close",
            [(ROWS, HEADS * HD)] * 4,
            (meta, *local, live, *rest, home),
            10**8,
            16,
            [PANEL, COPIES],
            out_spec=HBM,
        )
    )


def solution(mesh):
    rows = P(ALL, None)
    return jax.shard_map(
        body,
        mesh=mesh,
        in_specs=(rows, rows, rows, rows, P()),
        out_specs=(rows, rows, rows, rows),
        check_vma=False,
    )
```

```python
import functools

import jax
import jax.numpy as jnp
from jax import lax
from jax.experimental import pallas as pl
from jax.experimental.pallas import tpu as pltpu
from jax.sharding import PartitionSpec as P

HEADS = 12
HD = 64
ROWS = 256
LIVE2 = 64
LIVE3 = 8
R2 = 4
R3 = 32
NEG = -1e30
SCALE = HD**-0.5
BF = jnp.bfloat16
F32 = jnp.float32
ALL = ("seg", "blk")
SEG_AT, BLK_AT = 24, 25
FAR_AT, STAT_AT, MESSAGE = 256, 288, 296
PAIR = 72
ROW_AT = 14 * ROWS


def nt(a, b):
    return lax.dot_general(a, b, (((1,), (1,)), ((), ())), preferred_element_type=F32)


def nn(a, b):
    return lax.dot_general(a, b, (((1,), (0,)), ((), ())), preferred_element_type=F32)


def tn(a, b):
    return lax.dot_general(a, b, (((0,), (0,)), ((), ())), preferred_element_type=F32)


def exact(a, b, dims=((1,), (0,))):
    return lax.dot_general(
        a, b, (dims, ((), ())), preferred_element_type=F32, precision=lax.Precision.HIGHEST
    )


def iota(shape, axis):
    return lax.broadcasted_iota(jnp.int32, shape, axis)


def split2(x):
    first = x.astype(BF)
    return first, (x - first.astype(F32)).astype(BF)


def split3(x):
    first = x.astype(BF)
    rest = x - first.astype(F32)
    second = rest.astype(BF)
    return first, second, (rest - second.astype(F32)).astype(BF)


def cat(parts):
    return jnp.concatenate(parts, axis=1)


def pack_kq(k, q):
    k0, k1, k2 = split3(k)
    q0, q1, q2 = split3(q * SCALE)
    return cat([k0, k1, k0, k1, k0, k2]), cat([q0, q1, q1, q0, q2, q0])


def pack_vd(v, d):
    v0, v1 = split2(v)
    d0, d1 = split2(d)
    return cat([v0, v1, v0, v1]), cat([d0, d1, d1, d0])


def forward_core(ak, bq, av, bd, mask):
    s = jnp.where(mask, nt(ak, bq), NEG)
    dp = nt(av, bd)
    top = jnp.max(s, axis=0, keepdims=True)
    p = jnp.exp(s - top)
    total = jnp.sum(p, axis=0, keepdims=True)
    cross = jnp.sum(p * dp, axis=0, keepdims=True)
    return top, total, cross / total, p, dp


def backward_core(p, dp, delta, ak, bq, av, bd):
    g = p * (dp - delta)
    p0, p1 = split2(p)
    g0, g1 = split2(g)
    d01, q01, v01, k01 = bd[:, :128], bq[:, :128], av[:, :128], ak[:, :128]
    dv = nn(p0, d01) + nn(p1, d01)
    dk = nn(g0, q01) + nn(g1, q01)
    at = tn(v01, p0) + tn(v01, p1)
    qt = tn(k01, g0) + tn(k01, g1)
    return at[:HD] + at[HD:], (qt[:HD] + qt[HD:]) * SCALE, dk, dv


def fold(x):
    return x + pltpu.roll(x, HD, 1)


def half_mask(rows):
    return iota((rows, 128), 1) < HD


def both(a, b):
    return jnp.where(half_mask(a.shape[0]), a, b)


def merge(levels):
    top = functools.reduce(jnp.maximum, [lse for lse, _ in levels])
    weights = [jnp.exp(lse - top) for lse, _ in levels]
    total = functools.reduce(jnp.add, weights)
    delta = functools.reduce(jnp.add, [w * d for w, (_, d) in zip(weights, levels)])
    return top + jnp.log(total), delta / total


def block(a, b):
    at = ROWS * (6 * a + b)
    return pl.ds(at if isinstance(b, int) else pl.multiple_of(at, ROWS), ROWS)


def columns(b):
    return pl.ds(128 * b if isinstance(b, int) else pl.multiple_of(128 * b, 128), 128)


def inward(refs, panel, sems, b):
    return [
        pltpu.make_async_copy(
            ref.at[:, columns(b)], panel.at[block(a, b), :], sems.at[6 * a + b]
        )
        for a, ref in enumerate(refs)
    ]


def fetch(refs, panel, sems):
    for b in range(6):
        for copy in inward(refs, panel, sems, b):
            copy.start()


def arrive(refs, panel, sems, b):
    for copy in inward(refs, panel, sems, b):
        copy.wait()


def near_positions(meta, b):
    lane = iota((1, 128), 1)
    return R2 * (lane % LIVE2) + jnp.where(lane < LIVE2, meta[2 * b], meta[2 * b + 1])


def far_positions(meta, alone):
    lane = iota((1, 128), 1)
    spot = jnp.full((1, 128), -1, jnp.int32)
    for h in range(HEADS):
        near, far = meta[h], meta[HEADS + h]
        start = jnp.where(far % R2 == near, -1, far) if alone else far
        here = lane // LIVE3 == h
        spot = jnp.where(here & (start >= 0), start + R3 * (lane % LIVE3), spot)
    return spot


def pieces(x, count):
    out = []
    for _ in range(count - 1):
        out.append(x.astype(BF).astype(F32))
        x = x - out[-1]
    return [*out, x]


def place(near, far, b):
    def apart(x):
        low = half_mask(x.shape[0])
        return [jnp.where(low, x, 0.0), jnp.where(low, 0.0, x)]

    rows = [x.astype(BF) for x in apart(near)]
    if b:
        rows.append(jnp.zeros((16 * b, 128), BF))
    rows.append(jnp.concatenate(apart(far), axis=0).astype(BF))
    rows.append(jnp.zeros((112 - 16 * b, 128), BF))
    return jnp.concatenate(rows, axis=0)


def live_pieces(near, far, b, count):
    return [place(x, y, b) for x, y in zip(pieces(near, count), pieces(far, count))]


def live_products(k, v, q, d, b):
    k0, k1, k2 = split3(k)
    q0, q1, q2 = live_pieces(q[0] * SCALE, q[1] * SCALE, b, 3)
    v0, v1 = split2(v)
    d0, d1 = live_pieces(*d, b, 2)
    s = nt(cat([k0, k1, k0, k1, k0, k2]), cat([q0, q1, q1, q0, q2, q0]))
    return s, nt(cat([v0, v1, v0, v1]), cat([d0, d1, d1, d0]))


def live_forward(s, dp, spot):
    s = jnp.where(iota((ROWS, 128), 0) <= spot, s, NEG)
    top = jnp.max(s, axis=0, keepdims=True)
    p = jnp.exp(s - top)
    total = jnp.sum(p, axis=0, keepdims=True)
    delta = jnp.sum(p * dp, axis=0, keepdims=True) / total
    return top + jnp.log(total), delta, p / total


def halves(x, e):
    return x[:, HD * e : HD * e + HD]


def turn(x):
    return pltpu.roll(x, HD, 1)


class Flat:
    def __init__(self, ref):
        self.ref = ref

    def __getitem__(self, i):
        return self.ref[i // HEADS, i % HEADS]


def open_kernel(offsets, q, k, v, d, out, live, panel, sems, send, out_sems, shifts, shift_sem):
    shifting = pltpu.make_async_copy(offsets, shifts, shift_sem)
    shifting.start()
    fetch((q, k, v, d), panel, sems)
    shifting.wait()
    meta = Flat(shifts)
    copies, rows = [], []

    def leave(at, count):
        at = pl.ds(at, count)
        copies.append(pltpu.make_async_copy(send.at[at, :], out.at[at, :], out_sems.at[len(copies)]))
        copies[-1].start()

    for b in range(6):
        arrive((q, k, v, d), panel, sems, b)
        at = MESSAGE * b
        found = []
        for a in range(4):
            base = ROWS * (6 * a + b)
            near = both(
                panel[pl.ds(base + meta[2 * b], LIVE2, stride=R2), :],
                panel[pl.ds(base + meta[2 * b + 1], LIVE2, stride=R2), :],
            )
            far = both(
                panel[pl.ds(base + meta[HEADS + 2 * b], LIVE3, stride=R3), :],
                panel[pl.ds(base + meta[HEADS + 2 * b + 1], LIVE3, stride=R3), :],
            )
            send[at + LIVE2 * a : at + LIVE2 * a + LIVE2, :] = near
            send[at + FAR_AT + LIVE3 * a : at + FAR_AT + LIVE3 * a + LIVE3, :] = far
            found.append((near, far))
        leave(at, STAT_AT)
        for n, (near, far) in enumerate((found[0], found[3])):
            keep = PAIR * (2 * b + n)
            live[keep : keep + LIVE2, :] = near
            live[keep + LIVE2 : keep + PAIR, :] = far
        rows.append((found[0], found[3]))
    far_s = far_dp = jnp.zeros((ROWS, 128), F32)
    known = []
    for b in range(6):
        s, dp = live_products(
            panel[block(1, b), :],
            panel[block(2, b), :],
            *rows[b],
            b,
        )
        far_s, far_dp = far_s + s[:, 128:], far_dp + dp[:, 128:]
        known.append(live_forward(s[:, :128], dp[:, :128], near_positions(meta, b))[:2])
    far = live_forward(far_s, far_dp, far_positions(meta, False))[:2]
    for b in range(6):
        at = MESSAGE * b + STAT_AT
        turned = [pltpu.roll(x, (128 - 16 * b) % 128, 1) for x in far]
        send[at : at + 8, :] = jnp.concatenate([*known[b], *turned, jnp.zeros((4, 128), F32)], axis=0)
        leave(at, 8)
    for copy in copies:
        copy.wait()


def live_kernel(meta, k, v, live, weights, stats, panel, sems, kept, out_sems):
    fetch((k, v), panel, sems)
    stats[...] = jnp.zeros_like(stats)
    far_s = far_dp = jnp.zeros((ROWS, 128), F32)
    copies = []

    def record(n, s, dp, spot):
        lse, delta, p = live_forward(s, dp, spot)
        pair = cat(split2(p)), cat(split2(p * (dp - delta)))
        for m, x in enumerate(pair):
            at = pl.ds(ROWS * (7 * m + n), ROWS)
            kept[at, :] = x
            copies.append(pltpu.make_async_copy(kept.at[at, :], weights.at[at, :], out_sems.at[7 * m + n]))
            copies[-1].start()
        stats[n : n + 1, :] = lse
        stats[8 + n : 9 + n, :] = delta
        return pair

    def products(b, p, h):
        kb, vb = cat(split2(panel[block(0, b), :] * SCALE)), cat(split2(panel[block(1, b), :]))
        both_sides = tn(p, cat([vb, kb]))
        for n, x in enumerate((both_sides[:, :256], tn(h, kb), both_sides[:, 256:])):
            yield ROW_AT + 80 * (6 * n + b), x[:128, :128] + x[:128, 128:] + x[128:, :128] + x[128:, 128:]

    for b in range(6):
        arrive((k, v), panel, sems, b)
    for b in range(6):
        rows = []
        for n in range(2):
            keep = PAIR * (2 * b + n)
            rows.append((live[keep : keep + LIVE2, :], live[keep + LIVE2 : keep + PAIR, :]))
        s, dp = live_products(
            panel[block(0, b), :],
            panel[block(1, b), :],
            *rows,
            b,
        )
        far_s, far_dp = far_s + s[:, 128:], far_dp + dp[:, 128:]
        p, h = record(b, s[:, :128], dp[:, :128], near_positions(meta, b))
        for at, x in products(b, p, h):
            kept[at : at + LIVE2, :] = cat(split2(both(x[:LIVE2], x[LIVE2:])))
    p, h = record(6, far_s, far_dp, far_positions(meta, True))
    for b in range(6):
        for at, x in products(b, p, h):
            low, high = x[16 * b : 16 * b + 8], x[16 * b + 8 : 16 * b + 16]
            x = jnp.concatenate([both(low, high), jnp.zeros((8, 128), F32)], axis=0)
            kept[at + LIVE2 : at + 80, :] = cat(split2(x))
    at = pl.ds(ROW_AT, 18 * 80)
    copies.append(pltpu.make_async_copy(kept.at[at, :], weights.at[at, :], out_sems.at[14]))
    copies[-1].start()
    for copy in copies:
        copy.wait()


def gather_rows(ref, at, count):
    return jnp.concatenate(
        [ref[MESSAGE * b + at : MESSAGE * b + at + count, :] for b in range(8)], axis=0
    )


def stat_rows(ref, n):
    rows = [MESSAGE * b + STAT_AT + n for b in range(8)]
    return jnp.concatenate([ref[at : at + 1, :] for at in rows], axis=0)


def write_stat_rows(ref, n, x):
    for b in range(8):
        at = MESSAGE * b + STAT_AT + n
        ref[at : at + 1, :] = x[b : b + 1, :]


def spread_kernel(meta, got, out, kv, sems):
    k, v = gather_rows(got, FAR_AT + 8, 8), gather_rows(got, FAR_AT + 16, 8)
    kv[0] = both(k, turn(v))
    kv[1] = both(turn(k), v)
    copies = [
        pltpu.make_async_copy(kv.at[s % 2], out.at[pl.ds(64 * s, 64), :], sems.at[s])
        for s in range(16)
    ]
    for copy in copies:
        copy.start()
    for copy in copies:
        copy.wait()


def near_shift(meta, e):
    h = jnp.minimum(2 * meta[BLK_AT] + e, HEADS - 1)
    live = meta[HEADS + h] % R2 == meta[h]
    return live, meta[HEADS + h] // R2


def to_rows(x):
    return jnp.concatenate([x[:, HD * b : HD * b + HD] for b in range(8)], axis=0)


def near_blocks(got):
    qs, ks, vs, ds = [gather_rows(got, a * LIVE2, LIVE2) for a in range(4)]
    for e in range(2):
        ak, bq = pack_kq(halves(ks, e), halves(qs, e))
        av, bd = pack_vd(halves(vs, e), halves(ds, e))
        parts = []
        for j in range(2):
            keys, rows = 256 * (j + 1), slice(256 * j, 256 * j + 256)
            mask = iota((keys, 256), 0) <= iota((keys, 256), 1) + 256 * j
            parts.append((ak[:keys], bq[rows], av[:keys], bd[rows], mask))
        yield parts


def near_forward_kernel(meta, got, own, mine, theirs):
    found = []
    for parts in near_blocks(got):
        lses, deltas = [], []
        for part in parts:
            top, total, delta, _, _ = forward_core(*part)
            lses.append(top + jnp.log(total))
            deltas.append(delta)
        found.append((to_rows(cat(lses)), to_rows(cat(deltas))))
    lse, delta = [cat([found[0][n], found[1][n]]) for n in range(2)]
    own[:, :128] = lse
    own[:, 128:] = delta
    sub, lane = iota((128, 128), 0), iota((128, 128), 1)
    spread = ((sub < 8) & (lane < 64) & (lane % 8 == sub)).astype(F32)
    diagonal = iota((8, 128), 0) == iota((8, 128), 1) // 8
    q, d = gather_rows(got, FAR_AT, 8), gather_rows(got, FAR_AT + 24, 8)
    qd = both(q, turn(d)), both(turn(q), d)
    blocks = []
    for e in range(2):
        live, shift = near_shift(meta, e)
        pick = (sub // HD == e) & (sub % HD // 8 == lane) & (sub % 8 == shift)
        pick = pick.astype(F32)
        merged = merge(
            [
                tuple(pltpu.roll(stat_rows(got, 2 + n), 120 * e, 1) for n in range(2)),
                (jnp.where(live, exact(lse, pick), NEG), exact(delta, pick)),
            ]
        )
        flat = [
            jnp.sum(jnp.where(diagonal, exact(x, spread), 0.0), axis=0, keepdims=True)
            for x in merged
        ]
        blocks.append(jnp.concatenate([qd[e], *flat, jnp.zeros((6, 128), F32)], axis=0))
    first = meta[SEG_AT] % 2 == 0
    mine[...] = jnp.where(first, blocks[0], blocks[1])
    theirs[...] = jnp.where(first, blocks[1], blocks[0])


def far_kernel(meta, kv, mine, pair, send, keep, back, parts, sem):
    first = meta[SEG_AT] % 2 == 0
    x, y = mine[...], pair[...]
    low, high = jnp.where(first, x, y), jnp.where(first, y, x)
    qd = jnp.concatenate([low[:LIVE2], high[:LIVE2]], axis=0)
    known = [both(low[64 + n : 65 + n], turn(high[64 + n : 65 + n])) for n in range(2)]
    ak, bq = pack_kq(kv[:, :HD], qd[:, :HD])
    av, bd = pack_vd(kv[:, HD:], qd[:, HD:])
    start = 64 * (meta[SEG_AT] - meta[SEG_AT] % 2)
    mask = iota((1024, 128), 0) <= iota((1024, 128), 1) + start
    top, total, delta3, p, dp = forward_core(ak, bq, av, bd, mask)
    lse3 = top + jnp.log(total)
    lse, delta = merge([tuple(known), (lse3, delta3)])
    at, qt, dk, dv = backward_core(p * jnp.exp(top - lse), dp, delta, ak, bq, av, bd)
    parts[...] = both(fold(dk), fold(dv))
    leaving = pltpu.make_async_copy(parts, send, sem)
    leaving.start()
    aq = jnp.concatenate([at, qt], axis=0).T
    stats = (lse3, delta3, lse, delta)
    front = jnp.concatenate([aq[:LIVE2], *stats, jnp.zeros((4, 128), F32)], axis=0)
    rear = jnp.concatenate([aq[LIVE2:], *[turn(x) for x in stats], jnp.zeros((4, 128), F32)], axis=0)
    keep[...] = jnp.where(first, front, rear)
    back[...] = jnp.where(first, rear, front)
    leaving.wait()


def by_head(meta, keep, back):
    first = meta[SEG_AT] % 2 == 0
    x, y = keep[...], back[...]
    return jnp.where(first, x, y), jnp.where(first, y, x)


def near_backward_kernel(meta, got, own, keep, back, out):
    far = by_head(meta, keep, back)
    sub, lane = iota((128, 128), 0), iota((128, 128), 1)
    diagonal = iota((8, 128), 0) == iota((8, 128), 1) // 8
    known = [stat_rows(got, n) for n in range(2)]
    third = [jnp.zeros((8, 128), F32), jnp.zeros((8, 128), F32)]
    covered = jnp.zeros((8, 128), jnp.bool_)
    l = iota((8, 128), 1)
    for e in range(2):
        live, shift = near_shift(meta, e)
        covered = covered | ((l // HD == e) & (l % 8 == shift) & live)
        place = (sub < 64) & (sub % 8 == lane % HD // 8) & (lane // HD == e)
        place = place.astype(F32)
        for n in range(2):
            x = jnp.where(diagonal, far[e][64 + n : 65 + n], 0.0)
            third[n] = third[n] + exact(x, place)
    lse, delta = merge(
        [
            tuple(known),
            (own[:, :128], own[:, 128:]),
            (jnp.where(covered, third[0], NEG), jnp.where(covered, third[1], 0.0)),
        ]
    )
    for n, x in enumerate((lse, delta)):
        rest = jnp.zeros((8, 128), F32)
        for e in range(2):
            tail = ((sub < 64) & (lane == LIVE3 * e + sub % 8)).astype(F32)
            rest = rest + exact(jnp.where(diagonal, far[e][66 + n : 67 + n], 0.0), tail)
        write_stat_rows(out, n, x)
        write_stat_rows(out, 2 + n, rest)
    ats, qts, dks, dvs = [], [], [], []
    for e, parts in enumerate(near_blocks(got)):
        results = []
        for j, (ak, bq, av, bd, mask) in enumerate(parts):
            at = slice(HD * e, HD * e + HD)
            lse_j = cat([lse[b : b + 1, at] for b in range(4 * j, 4 * j + 4)])
            delta_j = cat([delta[b : b + 1, at] for b in range(4 * j, 4 * j + 4)])
            p = jnp.exp(jnp.where(mask, nt(ak, bq), NEG) - lse_j)
            results.append(backward_core(p, nt(av, bd), delta_j, ak, bq, av, bd))
        ats.append(cat([results[0][0], results[1][0]]))
        qts.append(cat([results[0][1], results[1][1]]))
        for group, n in ((dks, 2), (dvs, 3)):
            x, y = results[0][n], results[1][n]
            group.append(jnp.concatenate([x + y[:256], y[256:]], axis=0))
    finals = (
        jnp.concatenate(ats, axis=0).T,
        jnp.concatenate(qts, axis=0).T,
        both(fold(dks[0]), fold(dks[1])),
        both(fold(dvs[0]), fold(dvs[1])),
    )
    for a, x in enumerate(finals):
        for b in range(8):
            at = MESSAGE * b + a * LIVE2
            out[at : at + LIVE2, :] = x[LIVE2 * b : LIVE2 * b + LIVE2]


def merge_kernel(meta, near, parts, keep, back, out):
    aq = by_head(meta, keep, back)
    kv = []
    for e in range(2):
        total = parts[64 * e : 64 * e + 64, :]
        for s in range(e + 2, 16, 2):
            total = total + parts[64 * s : 64 * s + 64, :]
        kv.append(total)
    aq = [x[:LIVE2] for x in aq]
    far = (
        both(aq[0], turn(aq[1])),
        both(turn(aq[0]), aq[1]),
        both(kv[0], turn(kv[1])),
        both(turn(kv[0]), kv[1]),
    )
    for b in range(8):
        base = MESSAGE * b
        out[base : base + FAR_AT, :] = near[base : base + FAR_AT, :]
        out[base + STAT_AT : base + MESSAGE, :] = near[base + STAT_AT : base + MESSAGE, :]
        for a, x in enumerate(far):
            out[base + FAR_AT + 8 * a : base + FAR_AT + 8 * a + 8, :] = x[8 * b : 8 * b + 8]


def local_kernel(meta, q, k, v, d, at_out, dq_out, dk_out, dv_out, panel, sems):
    fetch((q, k, v, d), panel, sems)
    mask = iota((ROWS, ROWS), 0) <= iota((ROWS, ROWS), 1)
    row = iota((1, ROWS), 1)

    def step(b, carry):
        arrive((q, k, v, d), panel, sems, b)
        qp, kp, vp, dp = [panel[block(a, b), :] for a in range(4)]
        res = []
        for e in range(2):
            ak, bq = pack_kq(halves(kp, e), halves(qp, e))
            av, bd = pack_vd(halves(vp, e), halves(dp, e))
            _, total, delta, p, w = forward_core(ak, bq, av, bd, mask)
            h = 2 * b + e
            live = (row % R2 == meta[h]) | (row % R3 == meta[HEADS + h])
            p = p * jnp.where(live, 0.0, 1.0 / total)
            res.append(backward_core(p, w, delta, ak, bq, av, bd))
        at_out[block(0, b), :] = jnp.concatenate([res[0][0], res[1][0]], axis=0).T
        dq_out[block(0, b), :] = jnp.concatenate([res[0][1], res[1][1]], axis=0).T
        dk_out[block(0, b), :] = both(fold(res[0][2]), fold(res[1][2]))
        dv_out[block(0, b), :] = both(fold(res[0][3]), fold(res[1][3]))
        return carry

    lax.fori_loop(0, 6, step, 0)


def close_kernel(
    meta, at1, dq1, dk1, dv1, live, weights, stats, got,
    at_out, dq_out, dk_out, dv_out, panel, sems,
):
    outs, local = (at_out, dq_out, dk_out, dv_out), (at1, dq1, dk1, dv1)

    def products(n):
        x = weights[ROW_AT + 80 * n : ROW_AT + 80 * n + 80, :].astype(F32)
        return (x[:, :128] + x[:, 128:])[:PAIR]

    first = iota((1, 128), 1) < 16
    far = [jnp.zeros((1, 128), F32), jnp.zeros((1, 128), F32)]
    scales, shifts = [], []
    for b in range(7):
        if b < 6:
            at = MESSAGE * b + STAT_AT
            lse, delta = got[at : at + 1, :], got[at + 1 : at + 2, :]
            for n in range(2):
                x = jnp.where(first, got[at + 2 + n : at + 3 + n, :], 0.0)
                far[n] = far[n] + pltpu.roll(x, 16 * b, 1)
        else:
            lse, delta = far
        scales.append(jnp.exp(stats[b : b + 1, :] - lse))
        shifts.append(delta - stats[8 + b : 9 + b, :])
    zero = jnp.zeros((1, 128), F32)
    table = jnp.concatenate([*scales, zero, *shifts, zero], axis=0).T
    low2, low3 = half_mask(LIVE2), half_mask(LIVE3)
    far_p, far_h = weights[6 * ROWS : 7 * ROWS, :], weights[13 * ROWS : ROW_AT, :]
    copies, spreads = [], []

    def finish(a, b, near, far, kept):
        base = ROWS * (6 * a + b)
        panel[base : base + ROWS, :] = kept
        for e in range(2):
            spot = pl.ds(base + meta[2 * b + e], LIVE2, stride=R2)
            panel[spot, :] = panel[spot, :] + jnp.where(low2 if e == 0 else ~low2, near, 0.0)
            spot = pl.ds(base + meta[HEADS + 2 * b + e], LIVE3, stride=R3)
            panel[spot, :] = panel[spot, :] + jnp.where(low3 if e == 0 else ~low3, far, 0.0)
        copies.append(
            pltpu.make_async_copy(
                panel.at[block(a, b), :], outs[a].at[:, columns(b)], sems.at[6 * a + b]
            )
        )
        copies[-1].start()

    def arrived(a, b):
        near, far = MESSAGE * b + LIVE2 * a, MESSAGE * b + FAR_AT + LIVE3 * a
        return got[near : near + LIVE2, :], got[far : far + LIVE3, :]

    for b in range(6):
        spread = [
            (
                jnp.where(low2, table[:LIVE2, n + b : n + b + 1], table[LIVE2:, n + b : n + b + 1]),
                jnp.where(
                    low3,
                    table[16 * b : 16 * b + 8, n + 6 : n + 7],
                    table[16 * b + 8 : 16 * b + 16, n + 6 : n + 7],
                ),
            )
            for n in (0, 8)
        ]
        spreads.append(spread)
        z, x, y = products(b), products(6 + b), products(12 + b)
        for a in range(2):
            near, far = arrived(a, b)
            if a == 0:
                near, far = near + spread[0][0] * z[:LIVE2], far + spread[0][1] * z[LIVE2:]
            else:
                near = near + spread[0][0] * (x[:LIVE2] - spread[1][0] * y[:LIVE2])
                far = far + spread[0][1] * (x[LIVE2:] - spread[1][1] * y[LIVE2:])
            finish(a, b, near, far, local[a][ROWS * b : ROWS * b + ROWS, :])
    for b in range(6):
        rows = []
        for n in range(2):
            keep = PAIR * (2 * b + n)
            rows.append((live[keep : keep + LIVE2, :], live[keep + LIVE2 : keep + PAIR, :]))
        d = [x * w for x, w in zip(rows[1], spreads[b][0])]
        q = [x * (w * SCALE) for x, w in zip(rows[0], spreads[b][0])]
        t = [-x * w for x, w in zip(q, spreads[b][1])]
        d, q, t = [cat(live_pieces(*x, b, 2)) for x in (d, q, t)]
        own_p, own_h = [weights[ROWS * n : ROWS * n + ROWS, :] for n in (b, 7 + b)]
        dense = [jnp.zeros((ROWS, 256), F32), jnp.zeros((ROWS, 256), F32)]
        for n in range(2):
            at = slice(128 * n, 128 * n + 128)
            p, h = cat([own_p[:, at], far_p[:, at]]), cat([own_h[:, at], far_h[:, at]])
            dense[0] = dense[0] + nn(h, q) + nn(p, t)
            dense[1] = dense[1] + nn(p, d)
        for a, x in zip((2, 3), dense):
            kept = local[a][ROWS * b : ROWS * b + ROWS, :] + (x[:, :128] + x[:, 128:])
            finish(a, b, *arrived(a, b), kept)
    for copy in copies:
        copy.wait()


SMEM = pl.BlockSpec(memory_space=pltpu.SMEM)
HBM = pl.BlockSpec(memory_space=pltpu.HBM)
VMEM = pl.BlockSpec(memory_space=pltpu.VMEM)
PANEL = pltpu.VMEM((24 * ROWS + R3, 128), F32)
COPIES = pltpu.SemaphoreType.DMA((24,))


def call(kernel, name, outs, args, flops, mib, scratch=(), hbm=(), out_spec=VMEM):
    return pl.pallas_call(
        kernel,
        name=name,
        out_shape=[jax.ShapeDtypeStruct(x, F32) if isinstance(x, tuple) else x for x in outs],
        in_specs=[HBM if i in hbm else VMEM if i else SMEM for i in range(len(args))],
        out_specs=out_spec if isinstance(out_spec, list) else [out_spec] * len(outs),
        scratch_shapes=list(scratch),
        compiler_params=pltpu.CompilerParams(vmem_limit_bytes=mib * 1024 * 1024),
        cost_estimate=pl.CostEstimate(flops=flops, bytes_accessed=100_000, transcendentals=0),
    )(*args)


def in_hbm(x):
    return pltpu.with_memory_space_constraint(x, pltpu.HBM)


def swap(x, axis):
    return lax.all_to_all(x, axis, 0, 0, tiled=True)


def swap_cores(x):
    return lax.ppermute(x, "seg", [(s, s ^ 1) for s in range(lax.axis_size("seg"))])


def body(q, k, v, d, offsets):
    place = jnp.stack([lax.axis_index("seg"), lax.axis_index("blk")]).astype(jnp.int32)
    meta = jnp.concatenate([offsets.reshape(-1), place])
    rows = tuple(in_hbm(x) for x in (q, k, v, d))
    given = (1, 2, 3, 4)
    message, pair, far = (8 * MESSAGE, 128), (PAIR, 128), (1024, 128)
    send, live = call(
        open_kernel,
        "open",
        [pltpu.HBM(message, F32), (12 * PAIR, 128)],
        (in_hbm(offsets), *rows),
        10**8,
        16,
        [
            PANEL,
            COPIES,
            pltpu.VMEM(message, F32),
            pltpu.SemaphoreType.DMA((12,)),
            pltpu.SMEM((2, HEADS), jnp.int32),
            pltpu.SemaphoreType.DMA,
        ],
        (0, *given),
        [HBM, VMEM],
    )
    got = swap(send, "blk")
    local = call(
        local_kernel,
        "local",
        [(6 * ROWS, 128)] * 4,
        (meta, *rows),
        10**8,
        24,
        [PANEL, COPIES],
        given,
    )
    got, *local = lax.optimization_barrier((got, *local))
    (keys,) = call(
        spread_kernel,
        "spread",
        [pltpu.HBM(far, F32)],
        (meta, got),
        10**8,
        8,
        [pltpu.VMEM((2, 64, 128), F32), pltpu.SemaphoreType.DMA((16,))],
        out_spec=HBM,
    )
    all_keys = swap(keys, "seg")
    own, mine, theirs = call(
        near_forward_kernel, "near_forward", [(8, 256), pair, pair], (meta, got), 10**8, 24
    )
    rest = call(
        live_kernel,
        "live",
        [pltpu.HBM((ROW_AT + 18 * 80, 256), BF), (16, 128)],
        (meta, rows[1], rows[2], live),
        10**8,
        16,
        [
            pltpu.VMEM((12 * ROWS, 128), F32),
            pltpu.SemaphoreType.DMA((12,)),
            pltpu.VMEM((ROW_AT + 18 * 80, 256), BF),
            pltpu.SemaphoreType.DMA((15,)),
        ],
        (1, 2),
        [HBM, VMEM],
    )
    all_keys, *rest = lax.optimization_barrier((all_keys, *rest))
    partner = swap_cores(theirs)
    parts, keep, back = call(
        far_kernel,
        "far",
        [pltpu.HBM(far, F32), pair, pair],
        (meta, all_keys, mine, partner),
        10**8,
        24,
        [pltpu.VMEM(far, F32), pltpu.SemaphoreType.DMA],
        out_spec=[HBM, VMEM, VMEM],
    )
    sums = swap(parts, "seg")
    back = swap_cores(back)
    (near,) = call(
        near_backward_kernel,
        "near_backward",
        [message],
        (meta, got, own, keep, back),
        10**8,
        24,
    )
    (reply,) = call(merge_kernel, "merge", [message], (meta, near, sums, keep, back), 2 * 10**10, 12)
    home = swap(reply, "blk")
    return tuple(
        call(
            close_kernel,
            "close",
            [(ROWS, HEADS * HD)] * 4,
            (meta, *local, live, *rest, home),
            10**8,
            16,
            [PANEL, COPIES],
            out_spec=HBM,
        )
    )


def solution(mesh):
    rows = P(ALL, None)
    return jax.shard_map(
        body,
        mesh=mesh,
        in_specs=(rows, rows, rows, rows, P()),
        out_specs=(rows, rows, rows, rows),
        check_vma=False,
    )
```

```python
import functools

import jax
import jax.numpy as jnp
from jax import lax
from jax.experimental import pallas as pl
from jax.experimental.pallas import tpu as pltpu
from jax.sharding import PartitionSpec as P

HEADS = 12
HD = 64
ROWS = 256
LIVE2 = 64
LIVE3 = 8
R2 = 4
R3 = 32
NEG = -1e30
SCALE = HD**-0.5
BF = jnp.bfloat16
F32 = jnp.float32
ALL = ("seg", "blk")
SEG_AT, BLK_AT = 24, 25
FAR_AT, STAT_AT, MESSAGE = 256, 288, 296
PAIR = 72
ROW_AT = 14 * ROWS


def nt(a, b):
    return lax.dot_general(a, b, (((1,), (1,)), ((), ())), preferred_element_type=F32)


def nn(a, b):
    return lax.dot_general(a, b, (((1,), (0,)), ((), ())), preferred_element_type=F32)


def tn(a, b):
    return lax.dot_general(a, b, (((0,), (0,)), ((), ())), preferred_element_type=F32)


def exact(a, b, dims=((1,), (0,))):
    return lax.dot_general(
        a, b, (dims, ((), ())), preferred_element_type=F32, precision=lax.Precision.HIGHEST
    )


def iota(shape, axis):
    return lax.broadcasted_iota(jnp.int32, shape, axis)


def split2(x):
    first = x.astype(BF)
    return first, (x - first.astype(F32)).astype(BF)


def split3(x):
    first = x.astype(BF)
    rest = x - first.astype(F32)
    second = rest.astype(BF)
    return first, second, (rest - second.astype(F32)).astype(BF)


def cat(parts):
    return jnp.concatenate(parts, axis=1)


def pack_kq(k, q):
    k0, k1, k2 = split3(k)
    q0, q1, q2 = split3(q * SCALE)
    return cat([k0, k1, k0, k1, k0, k2]), cat([q0, q1, q1, q0, q2, q0])


def pack_vd(v, d):
    v0, v1 = split2(v)
    d0, d1 = split2(d)
    return cat([v0, v1, v0, v1]), cat([d0, d1, d1, d0])


def forward_core(ak, bq, av, bd, mask):
    s = jnp.where(mask, nt(ak, bq), NEG)
    dp = nt(av, bd)
    top = jnp.max(s, axis=0, keepdims=True)
    p = jnp.exp(s - top)
    total = jnp.sum(p, axis=0, keepdims=True)
    cross = jnp.sum(p * dp, axis=0, keepdims=True)
    return top, total, cross / total, p, dp


def backward_core(p, dp, delta, ak, bq, av, bd):
    g = p * (dp - delta)
    p0, p1 = split2(p)
    g0, g1 = split2(g)
    d01, q01, v01, k01 = bd[:, :128], bq[:, :128], av[:, :128], ak[:, :128]
    dv = nn(p0, d01) + nn(p1, d01)
    dk = nn(g0, q01) + nn(g1, q01)
    at = tn(v01, p0) + tn(v01, p1)
    qt = tn(k01, g0) + tn(k01, g1)
    return at[:HD] + at[HD:], (qt[:HD] + qt[HD:]) * SCALE, dk, dv


def fold(x):
    return x + pltpu.roll(x, HD, 1)


def half_mask(rows):
    return iota((rows, 128), 1) < HD


def both(a, b):
    return jnp.where(half_mask(a.shape[0]), a, b)


def merge(levels):
    top = functools.reduce(jnp.maximum, [lse for lse, _ in levels])
    weights = [jnp.exp(lse - top) for lse, _ in levels]
    total = functools.reduce(jnp.add, weights)
    delta = functools.reduce(jnp.add, [w * d for w, (_, d) in zip(weights, levels)])
    return top + jnp.log(total), delta / total


def block(a, b):
    at = ROWS * (6 * a + b)
    return pl.ds(at if isinstance(b, int) else pl.multiple_of(at, ROWS), ROWS)


def columns(b):
    return pl.ds(128 * b if isinstance(b, int) else pl.multiple_of(128 * b, 128), 128)


def inward(refs, panel, sems, b):
    return [
        pltpu.make_async_copy(
            ref.at[:, columns(b)], panel.at[block(a, b), :], sems.at[6 * a + b]
        )
        for a, ref in enumerate(refs)
    ]


def fetch(refs, panel, sems):
    for b in range(6):
        for copy in inward(refs, panel, sems, b):
            copy.start()


def arrive(refs, panel, sems, b):
    for copy in inward(refs, panel, sems, b):
        copy.wait()


def near_positions(meta, b):
    lane = iota((1, 128), 1)
    return R2 * (lane % LIVE2) + jnp.where(lane < LIVE2, meta[2 * b], meta[2 * b + 1])


def far_positions(meta, alone):
    lane = iota((1, 128), 1)
    spot = jnp.full((1, 128), -1, jnp.int32)
    for h in range(HEADS):
        near, far = meta[h], meta[HEADS + h]
        start = jnp.where(far % R2 == near, -1, far) if alone else far
        here = lane // LIVE3 == h
        spot = jnp.where(here & (start >= 0), start + R3 * (lane % LIVE3), spot)
    return spot


def pieces(x, count):
    out = []
    for _ in range(count - 1):
        out.append(x.astype(BF).astype(F32))
        x = x - out[-1]
    return [*out, x]


def place(near, far, b):
    def apart(x):
        low = half_mask(x.shape[0])
        return [jnp.where(low, x, 0.0), jnp.where(low, 0.0, x)]

    rows = [x.astype(BF) for x in apart(near)]
    if b:
        rows.append(jnp.zeros((16 * b, 128), BF))
    rows.append(jnp.concatenate(apart(far), axis=0).astype(BF))
    rows.append(jnp.zeros((112 - 16 * b, 128), BF))
    return jnp.concatenate(rows, axis=0)


def live_pieces(near, far, b, count):
    return [place(x, y, b) for x, y in zip(pieces(near, count), pieces(far, count))]


def live_products(k, v, q, d, b):
    k0, k1, k2 = split3(k)
    q0, q1, q2 = live_pieces(q[0] * SCALE, q[1] * SCALE, b, 3)
    v0, v1 = split2(v)
    d0, d1 = live_pieces(*d, b, 2)
    s = nt(cat([k0, k1, k0, k1, k0, k2]), cat([q0, q1, q1, q0, q2, q0]))
    return s, nt(cat([v0, v1, v0, v1]), cat([d0, d1, d1, d0]))


def live_forward(s, dp, spot):
    s = jnp.where(iota((ROWS, 128), 0) <= spot, s, NEG)
    top = jnp.max(s, axis=0, keepdims=True)
    p = jnp.exp(s - top)
    total = jnp.sum(p, axis=0, keepdims=True)
    delta = jnp.sum(p * dp, axis=0, keepdims=True) / total
    return top + jnp.log(total), delta, p / total


def halves(x, e):
    return x[:, HD * e : HD * e + HD]


def turn(x):
    return pltpu.roll(x, HD, 1)


class Flat:
    def __init__(self, ref):
        self.ref = ref

    def __getitem__(self, i):
        return self.ref[i // HEADS, i % HEADS]


def open_kernel(offsets, q, k, v, d, out, live, panel, sems, send, out_sems, shifts, shift_sem):
    shifting = pltpu.make_async_copy(offsets, shifts, shift_sem)
    shifting.start()
    fetch((q, k, v, d), panel, sems)
    shifting.wait()
    meta = Flat(shifts)
    copies, rows = [], []

    def leave(at, count):
        at = pl.ds(at, count)
        copies.append(pltpu.make_async_copy(send.at[at, :], out.at[at, :], out_sems.at[len(copies)]))
        copies[-1].start()

    for b in range(6):
        arrive((q, k, v, d), panel, sems, b)
        at = MESSAGE * b
        found = []
        for a in range(4):
            base = ROWS * (6 * a + b)
            near = both(
                panel[pl.ds(base + meta[2 * b], LIVE2, stride=R2), :],
                panel[pl.ds(base + meta[2 * b + 1], LIVE2, stride=R2), :],
            )
            far = both(
                panel[pl.ds(base + meta[HEADS + 2 * b], LIVE3, stride=R3), :],
                panel[pl.ds(base + meta[HEADS + 2 * b + 1], LIVE3, stride=R3), :],
            )
            send[at + LIVE2 * a : at + LIVE2 * a + LIVE2, :] = near
            send[at + FAR_AT + LIVE3 * a : at + FAR_AT + LIVE3 * a + LIVE3, :] = far
            found.append((near, far))
        leave(at, STAT_AT)
        for n, (near, far) in enumerate((found[0], found[3])):
            keep = PAIR * (2 * b + n)
            live[keep : keep + LIVE2, :] = near
            live[keep + LIVE2 : keep + PAIR, :] = far
        rows.append((found[0], found[3]))
    far_s = far_dp = jnp.zeros((ROWS, 128), F32)
    known = []
    for b in range(6):
        s, dp = live_products(
            panel[block(1, b), :],
            panel[block(2, b), :],
            *rows[b],
            b,
        )
        far_s, far_dp = far_s + s[:, 128:], far_dp + dp[:, 128:]
        known.append(live_forward(s[:, :128], dp[:, :128], near_positions(meta, b))[:2])
    far = live_forward(far_s, far_dp, far_positions(meta, False))[:2]
    for b in range(6):
        at = MESSAGE * b + STAT_AT
        turned = [pltpu.roll(x, (128 - 16 * b) % 128, 1) for x in far]
        send[at : at + 8, :] = jnp.concatenate([*known[b], *turned, jnp.zeros((4, 128), F32)], axis=0)
        leave(at, 8)
    for copy in copies:
        copy.wait()


def live_kernel(meta, k, v, live, weights, stats, panel, sems, kept, out_sems):
    fetch((k, v), panel, sems)
    stats[...] = jnp.zeros_like(stats)
    far_s = far_dp = jnp.zeros((ROWS, 128), F32)
    copies = []

    def record(n, s, dp, spot):
        lse, delta, p = live_forward(s, dp, spot)
        pair = cat(split2(p)), cat(split2(p * (dp - delta)))
        for m, x in enumerate(pair):
            at = pl.ds(ROWS * (7 * m + n), ROWS)
            kept[at, :] = x
            copies.append(pltpu.make_async_copy(kept.at[at, :], weights.at[at, :], out_sems.at[7 * m + n]))
            copies[-1].start()
        stats[n : n + 1, :] = lse
        stats[8 + n : 9 + n, :] = delta
        return pair

    def products(b, p, h):
        kb, vb = cat(split2(panel[block(0, b), :] * SCALE)), cat(split2(panel[block(1, b), :]))
        both_sides = tn(p, cat([vb, kb]))
        for n, x in enumerate((both_sides[:, :256], tn(h, kb), both_sides[:, 256:])):
            yield ROW_AT + 80 * (6 * n + b), x[:128, :128] + x[:128, 128:] + x[128:, :128] + x[128:, 128:]

    for b in range(6):
        arrive((k, v), panel, sems, b)
    for b in range(6):
        rows = []
        for n in range(2):
            keep = PAIR * (2 * b + n)
            rows.append((live[keep : keep + LIVE2, :], live[keep + LIVE2 : keep + PAIR, :]))
        s, dp = live_products(
            panel[block(0, b), :],
            panel[block(1, b), :],
            *rows,
            b,
        )
        far_s, far_dp = far_s + s[:, 128:], far_dp + dp[:, 128:]
        p, h = record(b, s[:, :128], dp[:, :128], near_positions(meta, b))
        for at, x in products(b, p, h):
            kept[at : at + LIVE2, :] = cat(split2(both(x[:LIVE2], x[LIVE2:])))
    p, h = record(6, far_s, far_dp, far_positions(meta, True))
    for b in range(6):
        for at, x in products(b, p, h):
            low, high = x[16 * b : 16 * b + 8], x[16 * b + 8 : 16 * b + 16]
            x = jnp.concatenate([both(low, high), jnp.zeros((8, 128), F32)], axis=0)
            kept[at + LIVE2 : at + 80, :] = cat(split2(x))
    at = pl.ds(ROW_AT, 18 * 80)
    copies.append(pltpu.make_async_copy(kept.at[at, :], weights.at[at, :], out_sems.at[14]))
    copies[-1].start()
    for copy in copies:
        copy.wait()


def gather_rows(ref, at, count):
    return jnp.concatenate(
        [ref[MESSAGE * b + at : MESSAGE * b + at + count, :] for b in range(8)], axis=0
    )


def stat_rows(ref, n):
    rows = [MESSAGE * b + STAT_AT + n for b in range(8)]
    return jnp.concatenate([ref[at : at + 1, :] for at in rows], axis=0)


def write_stat_rows(ref, n, x):
    for b in range(8):
        at = MESSAGE * b + STAT_AT + n
        ref[at : at + 1, :] = x[b : b + 1, :]


def spread_kernel(meta, got, out, kv, sems):
    k, v = gather_rows(got, FAR_AT + 8, 8), gather_rows(got, FAR_AT + 16, 8)
    kv[:64, :] = kv[128:192, :] = both(k, turn(v))
    kv[64:128, :] = kv[192:, :] = both(turn(k), v)
    copies = [
        pltpu.make_async_copy(kv, out.at[pl.ds(256 * s, 256), :], sems.at[s]) for s in range(4)
    ]
    for copy in copies:
        copy.start()
    for copy in copies:
        copy.wait()


def near_shift(meta, e):
    h = jnp.minimum(2 * meta[BLK_AT] + e, HEADS - 1)
    live = meta[HEADS + h] % R2 == meta[h]
    return live, meta[HEADS + h] // R2


def to_rows(x):
    return jnp.concatenate([x[:, HD * b : HD * b + HD] for b in range(8)], axis=0)


def near_blocks(got):
    qs, ks, vs, ds = [gather_rows(got, a * LIVE2, LIVE2) for a in range(4)]
    for e in range(2):
        ak, bq = pack_kq(halves(ks, e), halves(qs, e))
        av, bd = pack_vd(halves(vs, e), halves(ds, e))
        parts = []
        for j in range(2):
            keys, rows = 256 * (j + 1), slice(256 * j, 256 * j + 256)
            mask = iota((keys, 256), 0) <= iota((keys, 256), 1) + 256 * j
            parts.append((ak[:keys], bq[rows], av[:keys], bd[rows], mask))
        yield parts


def near_forward_kernel(meta, got, own, mine, theirs):
    found = []
    for parts in near_blocks(got):
        lses, deltas = [], []
        for part in parts:
            top, total, delta, _, _ = forward_core(*part)
            lses.append(top + jnp.log(total))
            deltas.append(delta)
        found.append((to_rows(cat(lses)), to_rows(cat(deltas))))
    lse, delta = [cat([found[0][n], found[1][n]]) for n in range(2)]
    own[:, :128] = lse
    own[:, 128:] = delta
    sub, lane = iota((128, 128), 0), iota((128, 128), 1)
    spread = ((sub < 8) & (lane < 64) & (lane % 8 == sub)).astype(F32)
    diagonal = iota((8, 128), 0) == iota((8, 128), 1) // 8
    q, d = gather_rows(got, FAR_AT, 8), gather_rows(got, FAR_AT + 24, 8)
    qd = both(q, turn(d)), both(turn(q), d)
    blocks = []
    for e in range(2):
        live, shift = near_shift(meta, e)
        pick = (sub // HD == e) & (sub % HD // 8 == lane) & (sub % 8 == shift)
        pick = pick.astype(F32)
        merged = merge(
            [
                tuple(pltpu.roll(stat_rows(got, 2 + n), 120 * e, 1) for n in range(2)),
                (jnp.where(live, exact(lse, pick), NEG), exact(delta, pick)),
            ]
        )
        flat = [
            jnp.sum(jnp.where(diagonal, exact(x, spread), 0.0), axis=0, keepdims=True)
            for x in merged
        ]
        blocks.append(jnp.concatenate([qd[e], *flat, jnp.zeros((6, 128), F32)], axis=0))
    first = meta[SEG_AT] % 2 == 0
    mine[...] = jnp.where(first, blocks[0], blocks[1])
    theirs[...] = jnp.where(first, blocks[1], blocks[0])


def far_kernel(meta, kv, mine, pair, send, keep, back, parts, sem):
    first = meta[SEG_AT] % 2 == 0
    x, y = mine[...], pair[...]
    low, high = jnp.where(first, x, y), jnp.where(first, y, x)
    qd = jnp.concatenate([low[:LIVE2], high[:LIVE2]], axis=0)
    known = [both(low[64 + n : 65 + n], turn(high[64 + n : 65 + n])) for n in range(2)]
    ak, bq = pack_kq(kv[:, :HD], qd[:, :HD])
    av, bd = pack_vd(kv[:, HD:], qd[:, HD:])
    start = 64 * (meta[SEG_AT] - meta[SEG_AT] % 2)
    mask = iota((1024, 128), 0) <= iota((1024, 128), 1) + start
    top, total, delta3, p, dp = forward_core(ak, bq, av, bd, mask)
    lse3 = top + jnp.log(total)
    lse, delta = merge([tuple(known), (lse3, delta3)])
    at, qt, dk, dv = backward_core(p * jnp.exp(top - lse), dp, delta, ak, bq, av, bd)
    parts[...] = both(fold(dk), fold(dv))
    leaving = pltpu.make_async_copy(parts, send, sem)
    leaving.start()
    aq = jnp.concatenate([at, qt], axis=0).T
    stats = (lse3, delta3, lse, delta)
    front = jnp.concatenate([aq[:LIVE2], *stats, jnp.zeros((4, 128), F32)], axis=0)
    rear = jnp.concatenate([aq[LIVE2:], *[turn(x) for x in stats], jnp.zeros((4, 128), F32)], axis=0)
    keep[...] = jnp.where(first, front, rear)
    back[...] = jnp.where(first, rear, front)
    leaving.wait()


def by_head(meta, keep, back):
    first = meta[SEG_AT] % 2 == 0
    x, y = keep[...], back[...]
    return jnp.where(first, x, y), jnp.where(first, y, x)


def near_backward_kernel(meta, got, own, keep, back, out):
    far = by_head(meta, keep, back)
    sub, lane = iota((128, 128), 0), iota((128, 128), 1)
    diagonal = iota((8, 128), 0) == iota((8, 128), 1) // 8
    known = [stat_rows(got, n) for n in range(2)]
    third = [jnp.zeros((8, 128), F32), jnp.zeros((8, 128), F32)]
    covered = jnp.zeros((8, 128), jnp.bool_)
    l = iota((8, 128), 1)
    for e in range(2):
        live, shift = near_shift(meta, e)
        covered = covered | ((l // HD == e) & (l % 8 == shift) & live)
        place = (sub < 64) & (sub % 8 == lane % HD // 8) & (lane // HD == e)
        place = place.astype(F32)
        for n in range(2):
            x = jnp.where(diagonal, far[e][64 + n : 65 + n], 0.0)
            third[n] = third[n] + exact(x, place)
    lse, delta = merge(
        [
            tuple(known),
            (own[:, :128], own[:, 128:]),
            (jnp.where(covered, third[0], NEG), jnp.where(covered, third[1], 0.0)),
        ]
    )
    for n, x in enumerate((lse, delta)):
        rest = jnp.zeros((8, 128), F32)
        for e in range(2):
            tail = ((sub < 64) & (lane == LIVE3 * e + sub % 8)).astype(F32)
            rest = rest + exact(jnp.where(diagonal, far[e][66 + n : 67 + n], 0.0), tail)
        write_stat_rows(out, n, x)
        write_stat_rows(out, 2 + n, rest)
    ats, qts, dks, dvs = [], [], [], []
    for e, parts in enumerate(near_blocks(got)):
        results = []
        for j, (ak, bq, av, bd, mask) in enumerate(parts):
            at = slice(HD * e, HD * e + HD)
            lse_j = cat([lse[b : b + 1, at] for b in range(4 * j, 4 * j + 4)])
            delta_j = cat([delta[b : b + 1, at] for b in range(4 * j, 4 * j + 4)])
            p = jnp.exp(jnp.where(mask, nt(ak, bq), NEG) - lse_j)
            results.append(backward_core(p, nt(av, bd), delta_j, ak, bq, av, bd))
        ats.append(cat([results[0][0], results[1][0]]))
        qts.append(cat([results[0][1], results[1][1]]))
        for group, n in ((dks, 2), (dvs, 3)):
            x, y = results[0][n], results[1][n]
            group.append(jnp.concatenate([x + y[:256], y[256:]], axis=0))
    finals = (
        jnp.concatenate(ats, axis=0).T,
        jnp.concatenate(qts, axis=0).T,
        both(fold(dks[0]), fold(dks[1])),
        both(fold(dvs[0]), fold(dvs[1])),
    )
    for a, x in enumerate(finals):
        for b in range(8):
            at = MESSAGE * b + a * LIVE2
            out[at : at + LIVE2, :] = x[LIVE2 * b : LIVE2 * b + LIVE2]


def merge_kernel(meta, near, parts, keep, back, out):
    aq = by_head(meta, keep, back)
    kv = []
    for e in range(2):
        total = parts[64 * e : 64 * e + 64, :]
        for s in range(e + 2, 16, 2):
            total = total + parts[64 * s : 64 * s + 64, :]
        kv.append(total)
    aq = [x[:LIVE2] for x in aq]
    far = (
        both(aq[0], turn(aq[1])),
        both(turn(aq[0]), aq[1]),
        both(kv[0], turn(kv[1])),
        both(turn(kv[0]), kv[1]),
    )
    for b in range(8):
        base = MESSAGE * b
        out[base : base + FAR_AT, :] = near[base : base + FAR_AT, :]
        out[base + STAT_AT : base + MESSAGE, :] = near[base + STAT_AT : base + MESSAGE, :]
        for a, x in enumerate(far):
            out[base + FAR_AT + 8 * a : base + FAR_AT + 8 * a + 8, :] = x[8 * b : 8 * b + 8]


def local_kernel(meta, q, k, v, d, at_out, dq_out, dk_out, dv_out, panel, sems):
    fetch((q, k, v, d), panel, sems)
    mask = iota((ROWS, ROWS), 0) <= iota((ROWS, ROWS), 1)
    row = iota((1, ROWS), 1)

    def step(b, carry):
        arrive((q, k, v, d), panel, sems, b)
        qp, kp, vp, dp = [panel[block(a, b), :] for a in range(4)]
        res = []
        for e in range(2):
            ak, bq = pack_kq(halves(kp, e), halves(qp, e))
            av, bd = pack_vd(halves(vp, e), halves(dp, e))
            _, total, delta, p, w = forward_core(ak, bq, av, bd, mask)
            h = 2 * b + e
            live = (row % R2 == meta[h]) | (row % R3 == meta[HEADS + h])
            p = p * jnp.where(live, 0.0, 1.0 / total)
            res.append(backward_core(p, w, delta, ak, bq, av, bd))
        at_out[block(0, b), :] = jnp.concatenate([res[0][0], res[1][0]], axis=0).T
        dq_out[block(0, b), :] = jnp.concatenate([res[0][1], res[1][1]], axis=0).T
        dk_out[block(0, b), :] = both(fold(res[0][2]), fold(res[1][2]))
        dv_out[block(0, b), :] = both(fold(res[0][3]), fold(res[1][3]))
        return carry

    lax.fori_loop(0, 6, step, 0)


def close_kernel(
    meta, at1, dq1, dk1, dv1, live, weights, stats, got,
    at_out, dq_out, dk_out, dv_out, panel, sems,
):
    outs, local = (at_out, dq_out, dk_out, dv_out), (at1, dq1, dk1, dv1)

    def products(n):
        x = weights[ROW_AT + 80 * n : ROW_AT + 80 * n + 80, :].astype(F32)
        return (x[:, :128] + x[:, 128:])[:PAIR]

    first = iota((1, 128), 1) < 16
    far = [jnp.zeros((1, 128), F32), jnp.zeros((1, 128), F32)]
    scales, shifts = [], []
    for b in range(7):
        if b < 6:
            at = MESSAGE * b + STAT_AT
            lse, delta = got[at : at + 1, :], got[at + 1 : at + 2, :]
            for n in range(2):
                x = jnp.where(first, got[at + 2 + n : at + 3 + n, :], 0.0)
                far[n] = far[n] + pltpu.roll(x, 16 * b, 1)
        else:
            lse, delta = far
        scales.append(jnp.exp(stats[b : b + 1, :] - lse))
        shifts.append(delta - stats[8 + b : 9 + b, :])
    zero = jnp.zeros((1, 128), F32)
    table = jnp.concatenate([*scales, zero, *shifts, zero], axis=0).T
    low2, low3 = half_mask(LIVE2), half_mask(LIVE3)
    far_p, far_h = weights[6 * ROWS : 7 * ROWS, :], weights[13 * ROWS : ROW_AT, :]
    copies, spreads = [], []

    def finish(a, b, near, far, kept):
        base = ROWS * (6 * a + b)
        panel[base : base + ROWS, :] = kept
        for e in range(2):
            spot = pl.ds(base + meta[2 * b + e], LIVE2, stride=R2)
            panel[spot, :] = panel[spot, :] + jnp.where(low2 if e == 0 else ~low2, near, 0.0)
            spot = pl.ds(base + meta[HEADS + 2 * b + e], LIVE3, stride=R3)
            panel[spot, :] = panel[spot, :] + jnp.where(low3 if e == 0 else ~low3, far, 0.0)
        copies.append(
            pltpu.make_async_copy(
                panel.at[block(a, b), :], outs[a].at[:, columns(b)], sems.at[6 * a + b]
            )
        )
        copies[-1].start()

    def arrived(a, b):
        near, far = MESSAGE * b + LIVE2 * a, MESSAGE * b + FAR_AT + LIVE3 * a
        return got[near : near + LIVE2, :], got[far : far + LIVE3, :]

    for b in range(6):
        spread = [
            (
                jnp.where(low2, table[:LIVE2, n + b : n + b + 1], table[LIVE2:, n + b : n + b + 1]),
                jnp.where(
                    low3,
                    table[16 * b : 16 * b + 8, n + 6 : n + 7],
                    table[16 * b + 8 : 16 * b + 16, n + 6 : n + 7],
                ),
            )
            for n in (0, 8)
        ]
        spreads.append(spread)
        z, x, y = products(b), products(6 + b), products(12 + b)
        for a in range(2):
            near, far = arrived(a, b)
            if a == 0:
                near, far = near + spread[0][0] * z[:LIVE2], far + spread[0][1] * z[LIVE2:]
            else:
                near = near + spread[0][0] * (x[:LIVE2] - spread[1][0] * y[:LIVE2])
                far = far + spread[0][1] * (x[LIVE2:] - spread[1][1] * y[LIVE2:])
            finish(a, b, near, far, local[a][ROWS * b : ROWS * b + ROWS, :])
    for b in range(6):
        rows = []
        for n in range(2):
            keep = PAIR * (2 * b + n)
            rows.append((live[keep : keep + LIVE2, :], live[keep + LIVE2 : keep + PAIR, :]))
        d = [x * w for x, w in zip(rows[1], spreads[b][0])]
        q = [x * (w * SCALE) for x, w in zip(rows[0], spreads[b][0])]
        t = [-x * w for x, w in zip(q, spreads[b][1])]
        d, q, t = [cat(live_pieces(*x, b, 2)) for x in (d, q, t)]
        own_p, own_h = [weights[ROWS * n : ROWS * n + ROWS, :] for n in (b, 7 + b)]
        dense = [jnp.zeros((ROWS, 256), F32), jnp.zeros((ROWS, 256), F32)]
        for n in range(2):
            at = slice(128 * n, 128 * n + 128)
            p, h = cat([own_p[:, at], far_p[:, at]]), cat([own_h[:, at], far_h[:, at]])
            dense[0] = dense[0] + nn(h, q) + nn(p, t)
            dense[1] = dense[1] + nn(p, d)
        for a, x in zip((2, 3), dense):
            kept = local[a][ROWS * b : ROWS * b + ROWS, :] + (x[:, :128] + x[:, 128:])
            finish(a, b, *arrived(a, b), kept)
    for copy in copies:
        copy.wait()


SMEM = pl.BlockSpec(memory_space=pltpu.SMEM)
HBM = pl.BlockSpec(memory_space=pltpu.HBM)
VMEM = pl.BlockSpec(memory_space=pltpu.VMEM)
PANEL = pltpu.VMEM((24 * ROWS + R3, 128), F32)
COPIES = pltpu.SemaphoreType.DMA((24,))


def call(kernel, name, outs, args, flops, mib, scratch=(), hbm=(), out_spec=VMEM):
    return pl.pallas_call(
        kernel,
        name=name,
        out_shape=[jax.ShapeDtypeStruct(x, F32) if isinstance(x, tuple) else x for x in outs],
        in_specs=[HBM if i in hbm else VMEM if i else SMEM for i in range(len(args))],
        out_specs=out_spec if isinstance(out_spec, list) else [out_spec] * len(outs),
        scratch_shapes=list(scratch),
        compiler_params=pltpu.CompilerParams(vmem_limit_bytes=mib * 1024 * 1024),
        cost_estimate=pl.CostEstimate(flops=flops, bytes_accessed=100_000, transcendentals=0),
    )(*args)


def in_hbm(x):
    return pltpu.with_memory_space_constraint(x, pltpu.HBM)


def swap(x, axis):
    return lax.all_to_all(x, axis, 0, 0, tiled=True)


def swap_cores(x):
    return lax.ppermute(x, "seg", [(s, s ^ 1) for s in range(lax.axis_size("seg"))])


def body(q, k, v, d, offsets):
    place = jnp.stack([lax.axis_index("seg"), lax.axis_index("blk")]).astype(jnp.int32)
    meta = jnp.concatenate([offsets.reshape(-1), place])
    rows = tuple(in_hbm(x) for x in (q, k, v, d))
    given = (1, 2, 3, 4)
    message, pair, far = (8 * MESSAGE, 128), (PAIR, 128), (1024, 128)
    send, live = call(
        open_kernel,
        "open",
        [pltpu.HBM(message, F32), (12 * PAIR, 128)],
        (in_hbm(offsets), *rows),
        10**8,
        16,
        [
            PANEL,
            COPIES,
            pltpu.VMEM(message, F32),
            pltpu.SemaphoreType.DMA((12,)),
            pltpu.SMEM((2, HEADS), jnp.int32),
            pltpu.SemaphoreType.DMA,
        ],
        (0, *given),
        [HBM, VMEM],
    )
    got = swap(send, "blk")
    local = call(
        local_kernel,
        "local",
        [(6 * ROWS, 128)] * 4,
        (meta, *rows),
        10**8,
        24,
        [PANEL, COPIES],
        given,
    )
    got, *local = lax.optimization_barrier((got, *local))
    (keys,) = call(
        spread_kernel,
        "spread",
        [pltpu.HBM(far, F32)],
        (meta, got),
        10**8,
        8,
        [pltpu.VMEM((256, 128), F32), pltpu.SemaphoreType.DMA((4,))],
        out_spec=HBM,
    )
    all_keys = swap(keys, "seg")
    own, mine, theirs = call(
        near_forward_kernel, "near_forward", [(8, 256), pair, pair], (meta, got), 10**8, 24
    )
    rest = call(
        live_kernel,
        "live",
        [pltpu.HBM((ROW_AT + 18 * 80, 256), BF), (16, 128)],
        (meta, rows[1], rows[2], live),
        10**8,
        16,
        [
            pltpu.VMEM((12 * ROWS, 128), F32),
            pltpu.SemaphoreType.DMA((12,)),
            pltpu.VMEM((ROW_AT + 18 * 80, 256), BF),
            pltpu.SemaphoreType.DMA((15,)),
        ],
        (1, 2),
        [HBM, VMEM],
    )
    all_keys, *rest = lax.optimization_barrier((all_keys, *rest))
    partner = swap_cores(theirs)
    parts, keep, back = call(
        far_kernel,
        "far",
        [pltpu.HBM(far, F32), pair, pair],
        (meta, all_keys, mine, partner),
        10**8,
        24,
        [pltpu.VMEM(far, F32), pltpu.SemaphoreType.DMA],
        out_spec=[HBM, VMEM, VMEM],
    )
    sums = swap(parts, "seg")
    back = swap_cores(back)
    (near,) = call(
        near_backward_kernel,
        "near_backward",
        [message],
        (meta, got, own, keep, back),
        10**8,
        24,
    )
    (reply,) = call(merge_kernel, "merge", [message], (meta, near, sums, keep, back), 2 * 10**10, 12)
    home = swap(reply, "blk")
    return tuple(
        call(
            close_kernel,
            "close",
            [(ROWS, HEADS * HD)] * 4,
            (meta, *local, live, *rest, home),
            10**8,
            16,
            [PANEL, COPIES],
            out_spec=HBM,
        )
    )


def solution(mesh):
    rows = P(ALL, None)
    return jax.shard_map(
        body,
        mesh=mesh,
        in_specs=(rows, rows, rows, rows, P()),
        out_specs=(rows, rows, rows, rows),
        check_vma=False,
    )
```
